32 devices in a mesh: dp: 16 (over z, y, x), ctx: 2 (over core).
Axes of the slice: x: 2, y: 2, z: 4, core: 2. Of those that a mesh axis runs over, the one named last changes fastest.
Arguments:
- tokens_in: bfloat16 [16, 1024, 768], P('dp', 'ctx'), may hold values from -6 to 6
- cond_vec: bfloat16 [16, 128], P('dp'), may hold values from -6 to 6
- positions: int32 [16, 1024], P('dp', 'ctx'), may hold values from 0 to 3069, as said below
- absorbed: int32 [16, 1024], P('dp', 'ctx'), may hold values 0 or 1
- cotangent: bfloat16 [16, 1024, 768], P('dp', 'ctx'), may hold values from -6 to 6
- norm1_gain: bfloat16 [768], replicated, may hold values from 0.5 to 1.5
- qkv_weight: bfloat16 [768, 2304], replicated, may hold values from -0.21875 to 0.21875
- out_weight: bfloat16 [768, 768], replicated, may hold values from -0.875 to 0.875
- norm2_gain: bfloat16 [768], replicated, may hold values from 0.5 to 1.5
- fc1_weight: bfloat16 [768, 3072], replicated, may hold values from -0.21875 to 0.21875
- fc1_bias: bfloat16 [3072], replicated, may hold values from -1.75 to 1.75
- fc2_weight: bfloat16 [3072, 768], replicated, may hold values from -0.109375 to 0.109375
- fc2_bias: bfloat16 [768], replicated, may hold values from -1.75 to 1.75
- ada_weight: bfloat16 [128, 4608], replicated, may hold values from -0.25 to 0.25
- ada_bias: bfloat16 [4608], replicated, may hold values from -1.75 to 1.75
Outputs:
- mixed: bfloat16 [16, 1024, 768], P('dp', 'ctx')
- input_grad: bfloat16 [16, 1024, 768], P('dp', 'ctx')
- cond_grad: float32 [16, 128], P('dp')
- norm1_gain_grad: float32 [768], P('dp')
- qkv_grad: float32 [768, 2304], P('dp')
- out_grad: float32 [768, 768], P('dp')
- norm2_gain_grad: float32 [768], P('dp')
- fc1_grad: float32 [768, 3072], P('dp')
- fc1_bias_grad: float32 [3072], P('dp')
- fc2_grad: float32 [3072, 768], P('dp')
- fc2_bias_grad: float32 [768], P('dp')
- ada_grad: float32 [128, 4608], P(None, 'dp')
- ada_bias_grad: float32 [4608], P('dp')
The draws below stay inside these ranges and needn't reach their ends.
Inputs may be any that keep to these rules, and one draw needn't show every extreme that they name: In each sequence the positions start at 0 and rise by 1 to 3 from one token to the next.
All inputs are finite; a program needn't handle non-finite values. No bound on the sum of `absorbed` on one device may be relied on, other than what follows from the above.
Results may differ from the reference program's by a relative error of at most 0.019.
Values may be sent and summed in bfloat16 or wider, within the bound.
No kernel may reach another device: no remote copies, remote signals or barrier semaphores. Data moves between devices by JAX's collectives and lax.ppermute only.
A program may use at most 192 MiB of HBM per device.

```python
import math
import jax
import jax.numpy as jnp
from jax import lax

D = 768
HEADS = 12
HEAD_DIM = 64
FF = 3072
COND = 128
SEQ_LEN = 1024
BATCH = 16


def draw_positions(key, part):
    key = jax.random.fold_in(key, 11)
    step_key, row_key = jax.random.split(key)
    steps_up = jax.random.randint(step_key, (BATCH, SEQ_LEN), 1, 4)
    widest = jax.random.randint(row_key, (), 0, BATCH)
    row_ids = jnp.arange(BATCH, dtype=jnp.int32)[:, None]
    steps_up = jnp.where(row_ids == widest, 3, steps_up)
    return (jnp.cumsum(steps_up, axis=1) - steps_up[:, :1]).astype(jnp.int32)


def place_ends(entries, own_key, low, top_value):
    dims = entries.shape
    spot = [jax.random.randint(jax.random.fold_in(own_key, axis), (), 0, dims[axis]) for axis in range(len(dims))]
    entries = entries.at[tuple(spot)].set(low)
    longest = dims.index(max(dims))
    spot[longest] = (spot[longest] + 1) % dims[longest]
    return entries.at[tuple(spot)].set(top_value)


def steps_of(own_key, dims, shards, smallest, top_value):
    def one(axis_at, blocks):
        steps = jax.random.uniform(jax.random.fold_in(jax.random.fold_in(own_key, 6), axis_at), (blocks,), jnp.float32, smallest / len(shards), top_value / len(shards))
        return jnp.repeat(jnp.exp(steps), dims[axis_at] // blocks).reshape((-1,) + (1,) * (len(dims) - axis_at - 1))

    loudness = one(*shards[0])
    for cut in shards[1:]:
        loudness = loudness * one(*cut)
    return loudness


def bell_draw(key, extent, spread, limit, cuts=(), kind=jnp.bfloat16):
    gain = steps_of(key, extent, cuts, -0.22, 0.18) if cuts else 1.0
    entries = jax.random.normal(key, extent, jnp.float32) * spread * gain
    return jnp.minimum(jnp.maximum(entries, -limit), limit).astype(kind)


def setup_inputs(seed: int = 0) -> dict:
    keys = jax.random.split(jax.random.key(seed), 16)
    tokens_in = bell_draw(keys[0], (BATCH, SEQ_LEN, D), 1.0, 6.0, ((0, 16), (1, 2)))
    cond_vec = bell_draw(keys[1], (BATCH, COND), 1.0, 6.0, ((0, 16),))
    positions = draw_positions(jax.random.fold_in(keys[15], 71), 0)
    absorbed = place_ends((jax.random.randint(keys[3], (BATCH, SEQ_LEN), 0, 2) < 1).astype(jnp.int32), jax.random.fold_in(keys[3], 1), 0, 1)
    cotangent = bell_draw(keys[4], (BATCH, SEQ_LEN, D), 1.0, 6.0, ((0, 16), (1, 2)))
    norm1_gain = jnp.clip(1.0 + 0.1 * jax.random.normal(keys[5], (D,), jnp.float32), 0.5, 1.5).astype(jnp.bfloat16)
    qkv_weight = bell_draw(keys[6], (D, 3 * D), D ** -0.5, 0.21875)
    out_weight = bell_draw(keys[7], (D, D), (max(1, D * 64 // SEQ_LEN)) ** -0.5, 0.875)
    norm2_gain = jnp.clip(1.0 + 0.1 * jax.random.normal(keys[8], (D,), jnp.float32), 0.5, 1.5).astype(jnp.bfloat16)
    fc1_weight = bell_draw(keys[9], (D, FF), D ** -0.5, 0.21875)
    fc1_bias = bell_draw(keys[10], (FF,), 0.3, 1.75)
    fc2_weight = bell_draw(keys[11], (FF, D), FF ** -0.5, 0.109375)
    fc2_bias = bell_draw(keys[12], (D,), 0.3, 1.75)
    ada_weight = bell_draw(keys[13], (COND, 6 * D), (4 * COND) ** -0.5, 0.25)
    ada_bias = bell_draw(keys[14], (6 * D,), 0.3, 1.75)
    return dict(tokens_in=tokens_in, cond_vec=cond_vec, positions=positions, absorbed=absorbed, cotangent=cotangent, norm1_gain=norm1_gain, qkv_weight=qkv_weight, out_weight=out_weight, norm2_gain=norm2_gain, fc1_weight=fc1_weight, fc1_bias=fc1_bias, fc2_weight=fc2_weight, fc2_bias=fc2_bias, ada_weight=ada_weight, ada_bias=ada_bias)


EPS = 1e-05
SCORE_SCALE = 0.125

@jax.custom_vjp
def low(v):
    return lax.optimization_barrier(v.astype(jnp.bfloat16)).astype(jnp.float32)

@jax.custom_vjp
def low_back(v):
    return v

def low_keep(v):
    return (low(v), None)

def low_pass(kept, grad):
    return (grad,)

def back_keep(v):
    return (v, None)

def back_low(kept, grad):
    return (low(grad),)
low.defvjp(low_keep, low_pass)
low_back.defvjp(back_keep, back_low)

def matmul_hi(left_arr, right_arr):
    return jnp.dot(left_arr, right_arr, precision=lax.Precision.HIGHEST, preferred_element_type=jnp.float32)

def layer_norm(stream):
    row_mean = lax.optimization_barrier(jnp.mean(stream, axis=-1, keepdims=True))
    centred = stream - row_mean
    variance = lax.optimization_barrier(jnp.mean(centred * centred, axis=-1, keepdims=True))
    return centred * lax.rsqrt(variance + EPS)

def pre_norm(stream, norm_gain, shift_vec, scale_vec):
    return layer_norm(stream) * norm_gain * (1.0 + scale_vec[:, None, :]) + shift_vec[:, None, :]

def block_rows(row_count):
    size_now = row_count
    while size_now > 512 and size_now % 2 == 0:
        size_now = size_now // 2
    return size_now

def rotary_tables(positions):
    inv_freq = 10000.0 ** (-jnp.arange(0, HEAD_DIM, 2).astype(jnp.float32) / HEAD_DIM)
    angles = positions.astype(jnp.float32)[..., None] * inv_freq
    cos_table = jnp.concatenate([jnp.cos(angles), jnp.cos(angles)], axis=-1)[..., None, :]
    sin_table = jnp.concatenate([jnp.sin(angles), jnp.sin(angles)], axis=-1)[..., None, :]
    return (cos_table, sin_table)

def rotate_pos(stream, cos_table, sin_table):
    half_dim = stream.shape[-1] // 2
    turned = jnp.concatenate([-stream[..., half_dim:], stream[..., :half_dim]], axis=-1)
    return stream * cos_table + turned * sin_table

def attend(queries, key_all, value_all):
    groups, length = (queries.shape[0], queries.shape[1])
    block_len = block_rows(length)
    blocks = length // block_len
    split_q = queries.reshape(groups, blocks, block_len, HEADS, HEAD_DIM).transpose(1, 0, 2, 3, 4)

    def one_block(query_block, key_set, value_set):
        scores = low_back(jnp.einsum('gqhd,gkhd->gqhk', query_block, key_set, precision=lax.Precision.HIGHEST) * SCORE_SCALE)
        row_top = lax.optimization_barrier(jnp.max(scores, axis=-1, keepdims=True))
        raised = jnp.exp(scores - row_top)
        probability = low(raised / lax.optimization_barrier(jnp.sum(raised, axis=-1, keepdims=True)))
        return jnp.einsum('gqhk,gkhd->gqhd', probability, value_set, precision=lax.Precision.HIGHEST)
    checked = jax.checkpoint(one_block)
    outputs = lax.map(lambda query_block: checked(query_block, key_all, value_all), split_q)
    return outputs.transpose(1, 0, 2, 3, 4).reshape(groups, length, HEADS * HEAD_DIM)

def layer(params, stream, cond_rows, positions):
    gain_one, w_qkv, w_out, gain_two, w_up, b_up, w_down, b_down, w_ada, b_ada = params
    modulation = matmul_hi(cond_rows, w_ada) + b_ada
    shift_one, scale_one, gate_one, shift_two, scale_two, gate_two = jnp.split(modulation, 6, axis=-1)
    groups, length = (stream.shape[0], stream.shape[1])
    normed_one = low(pre_norm(stream, gain_one, shift_one, scale_one))
    projected = low_back(matmul_hi(normed_one, w_qkv)).reshape(groups, length, 3, HEADS, HEAD_DIM)
    cos_table, sin_table = rotary_tables(positions)
    queries = low(rotate_pos(projected[:, :, 0], cos_table, sin_table))
    key_all = low(rotate_pos(projected[:, :, 1], cos_table, sin_table))
    value_all = low(projected[:, :, 2])
    attended = low(low_back(attend(queries, key_all, value_all)))
    branch_att = low_back(matmul_hi(attended, w_out))
    middle = stream + gate_one[:, None, :] * branch_att
    normed_two = low(pre_norm(middle, gain_two, shift_two, scale_two))
    hidden_pre = low_back(matmul_hi(normed_two, w_up) + b_up)
    hidden = low(jax.nn.gelu(hidden_pre, approximate=True))
    branch_mlp = low_back(matmul_hi(hidden, w_down) + b_down)
    return middle + gate_two[:, None, :] * branch_mlp

def reference(tokens_in, cond_vec, positions, absorbed, cotangent, norm1_gain, qkv_weight, out_weight, norm2_gain, fc1_weight, fc1_bias, fc2_weight, fc2_bias, ada_weight, ada_bias):
    params = tuple((member.astype(jnp.float32) for member in (norm1_gain, qkv_weight, out_weight, norm2_gain, fc1_weight, fc1_bias, fc2_weight, fc2_bias, ada_weight, ada_bias)))
    batch_rows = tokens_in.shape[0]
    group = math.gcd(batch_rows, max(1, 4096 // SEQ_LEN))
    steps_n = batch_rows // group

    def regroup(array_in):
        return array_in.reshape((steps_n, group) + array_in.shape[1:])
    item_all = (regroup(tokens_in.astype(jnp.float32)), regroup(cond_vec.astype(jnp.float32)), regroup(positions), regroup(absorbed), regroup(cotangent.astype(jnp.float32)))

    def one_step(totals, item_set):
        stream, cond_rows, pos_rows, mask_rows, cot_rows = item_set

        def forward_fn(param_set, stream_in, cond_in):
            return layer(param_set, stream_in, cond_in, pos_rows)
        mixed_rows, pull_back = jax.vjp(forward_fn, params, stream, cond_rows)
        grad_params, grad_stream, grad_cond = pull_back(cot_rows * mask_rows.astype(jnp.float32)[..., None])
        totals = jax.tree.map(lambda left_arr, right_arr: left_arr + right_arr, totals, grad_params)
        return (totals, (mixed_rows.astype(jnp.bfloat16), grad_stream.astype(jnp.bfloat16), grad_cond))
    zero_set = jax.tree.map(jnp.zeros_like, params)
    totals, (mixed_all, grad_all, cond_all) = lax.scan(one_step, zero_set, item_all)
    return (mixed_all.reshape(tokens_in.shape), grad_all.reshape(tokens_in.shape), cond_all.reshape(cond_vec.shape), totals[0], totals[1], totals[2], totals[3], totals[4], totals[5], totals[6], totals[7], totals[8], totals[9])
```

```python
import functools

import jax
import jax.numpy as jnp
from jax import lax
from jax.experimental import pallas as pl
from jax.experimental.pallas import tpu as pltpu
from jax.sharding import PartitionSpec as P

HEADS = 12
HEAD_DIM = 64
EPS = 1e-05
SCORE_SCALE = 0.125
NEG_START = -1e30

def mask_half(value, head):
    lane = lax.broadcasted_iota(jnp.int32, value.shape, 1)
    keep = (lane < HEAD_DIM) if head == 0 else (lane >= HEAD_DIM)
    return jnp.where(keep, value, jnp.zeros_like(value))


def attn_fwd_body(q_ref, k_ref, v_ref, out_ref, prob_ref, inv_ref, km_ref, vt_ref):
    @pl.when(pl.program_id(1) == 0)
    def _():
        keys = k_ref[...]
        for head in (0, 1):
            km_ref[head] = mask_half(keys, head)
        vt_ref[...] = v_ref[...].T

    queries = q_ref[...]
    for head in (0, 1):
        rows = slice(head * HEAD_DIM, (head + 1) * HEAD_DIM)
        scores = lax.dot_general(
            km_ref[head], queries, (((1,), (1,)), ((), ())), preferred_element_type=jnp.float32
        )
        top = jnp.max(scores, axis=0, keepdims=True)
        raised = jnp.exp(scores - top)
        total = jnp.sum(raised, axis=0, keepdims=True)
        prob = raised.astype(jnp.bfloat16)
        prob_ref[head] = prob
        inverse = 1.0 / total
        inv_ref[0, head : head + 1, :] = inverse
        part = jnp.dot(vt_ref[rows, :], prob, preferred_element_type=jnp.float32)
        out_ref[rows, :] = (part * inverse).astype(jnp.bfloat16)


def attn_fwd(queries, keys, values, blk):
    length, width = keys.shape
    pairs = width // 128
    nq = queries.shape[0]
    return pl.pallas_call(
        attn_fwd_body,
        grid=(pairs, nq // blk),
        in_specs=[
            pl.BlockSpec((blk, 128), lambda p, i: (i, p)),
            pl.BlockSpec((length, 128), lambda p, i: (0, p)),
            pl.BlockSpec((length, 128), lambda p, i: (0, p)),
        ],
        out_specs=[
            pl.BlockSpec((128, blk), lambda p, i: (p, i)),
            pl.BlockSpec((2, length, blk), lambda p, i: (p, 0, i)),
            pl.BlockSpec((1, 8, blk), lambda p, i: (p, 0, i)),
        ],
        out_shape=[
            jax.ShapeDtypeStruct((width, nq), jnp.bfloat16),
            jax.ShapeDtypeStruct((2 * pairs, length, nq), jnp.bfloat16),
            jax.ShapeDtypeStruct((pairs, 8, nq), jnp.float32),
        ],
        scratch_shapes=[
            pltpu.VMEM((2, length, 128), jnp.bfloat16),
            pltpu.VMEM((128, length), jnp.bfloat16),
        ],
        compiler_params=pltpu.CompilerParams(vmem_limit_bytes=48 << 20),
        cost_estimate=pl.CostEstimate(
            flops=8 * nq * length * width, bytes_accessed=nq * length * 4 * pairs, transcendentals=0
        ),
    )(queries, keys, values)


def attn_bwd_body(
    prob_ref, inv_ref, gt_ref, out_ref, q_ref, k_ref, v_ref,
    dq_ref, dk_ref, dv_ref, vm_ref, kt_ref, dk_acc, dv_acc,
):
    step = pl.program_id(1)

    @pl.when(step == 0)
    def _():
        values = v_ref[...]
        for head in (0, 1):
            vm_ref[head] = mask_half(values, head)
        kt_ref[...] = k_ref[...].T

    queries = q_ref[...]
    grad_t = gt_ref[...].astype(jnp.float32)
    blk = grad_t.shape[1]
    row_id = lax.broadcasted_iota(jnp.int32, (128, blk), 0)
    inverse = jnp.where(row_id < HEAD_DIM, inv_ref[0, 0:1, :], inv_ref[0, 1:2, :])
    grad_t = grad_t * inverse
    product = grad_t * out_ref[...].astype(jnp.float32)
    grad_b = grad_t.astype(jnp.bfloat16)
    dk_new = None
    for head in (0, 1):
        rows = slice(head * HEAD_DIM, (head + 1) * HEAD_DIM)
        delta = jnp.sum(product[rows], axis=0, keepdims=True)
        keep = (row_id < HEAD_DIM) if head == 0 else (row_id >= HEAD_DIM)
        grad_m = jnp.where(keep, grad_b, jnp.zeros_like(grad_b))
        grad_p = jnp.dot(vm_ref[head], grad_b, preferred_element_type=jnp.float32)
        prob = prob_ref[head]
        grad_s = (prob.astype(jnp.float32) * (grad_p - delta)).astype(jnp.bfloat16)
        dv_h = lax.dot_general(
            prob, grad_m, (((1,), (1,)), ((), ())), preferred_element_type=jnp.float32
        )
        dk_h = jnp.dot(grad_s, mask_half(queries, head), preferred_element_type=jnp.float32)
        if dk_new is None:
            dk_new, dv_new = dk_h, dv_h
        else:
            dk_new, dv_new = dk_new + dk_h, dv_new + dv_h
        dq_t = jnp.dot(kt_ref[rows, :], grad_s, preferred_element_type=jnp.float32)
        dq_ref[rows, :] = dq_t * SCORE_SCALE

    @pl.when(step == 0)
    def _():
        dk_acc[...] = dk_new
        dv_acc[...] = dv_new

    @pl.when(step > 0)
    def _():
        dk_acc[...] += dk_new
        dv_acc[...] += dv_new

    @pl.when(step == pl.num_programs(1) - 1)
    def _():
        dk_ref[...] = dk_acc[...]
        dv_ref[...] = dv_acc[...].astype(jnp.bfloat16)


def attn_bwd(prob, inverse, grad_t, out_t, queries, keys, values, blk):
    length, width = keys.shape
    pairs = width // 128
    nq = queries.shape[0]
    return pl.pallas_call(
        attn_bwd_body,
        grid=(pairs, nq // blk),
        in_specs=[
            pl.BlockSpec((2, length, blk), lambda p, i: (p, 0, i)),
            pl.BlockSpec((1, 8, blk), lambda p, i: (p, 0, i)),
            pl.BlockSpec((128, blk), lambda p, i: (p, i)),
            pl.BlockSpec((128, blk), lambda p, i: (p, i)),
            pl.BlockSpec((blk, 128), lambda p, i: (i, p)),
            pl.BlockSpec((length, 128), lambda p, i: (0, p)),
            pl.BlockSpec((length, 128), lambda p, i: (0, p)),
        ],
        out_specs=[
            pl.BlockSpec((128, blk), lambda p, i: (p, i)),
            pl.BlockSpec((length, 128), lambda p, i: (0, p)),
            pl.BlockSpec((length, 128), lambda p, i: (0, p)),
        ],
        out_shape=[
            jax.ShapeDtypeStruct((width, nq), jnp.float32),
            jax.ShapeDtypeStruct((length, width), jnp.float32),
            jax.ShapeDtypeStruct((length, width), jnp.bfloat16),
        ],
        scratch_shapes=[
            pltpu.VMEM((2, length, 128), jnp.bfloat16),
            pltpu.VMEM((128, length), jnp.bfloat16),
            pltpu.VMEM((length, 128), jnp.float32),
            pltpu.VMEM((length, 128), jnp.float32),
        ],
        compiler_params=pltpu.CompilerParams(vmem_limit_bytes=48 << 20),
        cost_estimate=pl.CostEstimate(
            flops=16 * nq * length * width, bytes_accessed=nq * length * 4 * pairs, transcendentals=0
        ),
    )(prob, inverse, grad_t, out_t, queries, keys, values)


def layer_stats(stream):
    row_mean = jnp.mean(stream, axis=-1, keepdims=True)
    centred = stream - row_mean
    variance = jnp.mean(centred * centred, axis=-1, keepdims=True)
    inv = lax.rsqrt(variance + EPS)
    return centred * inv, inv


def tables(positions):
    inv_freq = 10000.0 ** (-jnp.arange(0, HEAD_DIM, 2).astype(jnp.float32) / HEAD_DIM)
    angles = positions.astype(jnp.float32)[:, None] * inv_freq
    cos_t, sin_t = jnp.cos(angles), jnp.sin(angles)
    return jnp.concatenate([cos_t, cos_t], -1), jnp.concatenate([-sin_t, sin_t], -1)


def swap_halves(x):
    rows, width = x.shape
    half = HEAD_DIM // 2
    lane = lax.broadcasted_iota(jnp.int32, x.shape, 1) % HEAD_DIM
    return jnp.where(lane < half, jnp.roll(x, -half, 1), jnp.roll(x, half, 1))


def dot(a, b):
    return jnp.dot(a, b, preferred_element_type=jnp.float32)


def dot_tn(a, b):
    return lax.dot_general(a, b, (((0,), (0,)), ((), ())), preferred_element_type=jnp.float32)


def dot_nt(a, b):
    return lax.dot_general(a, b, (((1,), (1,)), ((), ())), preferred_element_type=jnp.float32)


class Grid:
    def __init__(self, ndp):
        self.nz = ndp // 4
        self.me = lax.axis_index("dp")
        self.x = self.me % 2
        self.y = (self.me // 2) % 2
        self.z = self.me // 4
        self.px = [(i, i ^ 1) for i in range(ndp)]
        self.py = [(i, i ^ 2) for i in range(ndp)]
        self.pz = [[(i, (i + 4 * k) % ndp) for i in range(ndp)] for k in range(self.nz)]

    def pick(self, arr, index, axis):
        return lax.dynamic_index_in_dim(arr, index, axis, keepdims=False)

    def reduce(self, grad):
        rows, cols = grad.shape
        r = rows // (4 * self.nz)
        g = grad.reshape(self.nz, 2, 2, r, cols)
        h = cols // 2
        ga, gb = g[..., :h], g[..., h:]
        ra = lax.ppermute(self.pick(ga, 1 - self.x, 2), "dp", self.px)
        rb = lax.ppermute(self.pick(gb, 1 - self.y, 1), "dp", self.py)
        ha = self.pick(ga, self.x, 2) + ra
        hb = self.pick(gb, self.y, 1) + rb
        ra = lax.ppermute(self.pick(ha, 1 - self.y, 1), "dp", self.py)
        rb = lax.ppermute(self.pick(hb, 1 - self.x, 1), "dp", self.px)
        ja = self.pick(ha, self.y, 1) + ra
        jb = self.pick(hb, self.x, 1) + rb
        j = jnp.concatenate([ja, jb], axis=-1)
        total = self.pick(j, self.z, 0).astype(jnp.float32)
        for k in range(1, self.nz):
            got = lax.ppermute(self.pick(j, (self.z + k) % self.nz, 0), "dp", self.pz[k])
            total = total + got.astype(jnp.float32)
        return total

    def spread(self, mine):
        n = mine.shape[-1]
        m = mine.reshape(self.nz, 2, 2, n)
        got = lax.ppermute(self.pick(m, 1 - self.x, 2), "dp", self.px)
        m = jnp.stack([self.pick(m, self.x, 2), got], 0)
        got = lax.ppermute(self.pick(m, 1 - self.y, 2), "dp", self.py)
        m = jnp.stack([self.pick(m, self.y, 2), got], 0)
        parts = [self.pick(m, self.z, 2)]
        for k in range(1, self.nz):
            parts.append(
                lax.ppermute(self.pick(m, (self.z + k) % self.nz, 2), "dp", self.pz[k])
            )
        return jnp.stack(parts, 0).reshape(4 * self.nz, n)


def local_pair(
    tokens_in, cond_vec, positions, absorbed, cotangent, norm1_gain, qkv_weight, out_weight,
    norm2_gain, fc1_weight, fc1_bias, fc2_weight, fc2_bias, ada_weight, ada_bias, *, ndp,
):
    f32, bf16 = jnp.float32, jnp.bfloat16
    _, span, width = tokens_in.shape
    ff = fc1_weight.shape[1]
    hw, hf = width // 2, ff // 2
    core = lax.axis_index("ctx")
    grid = Grid(ndp)
    swap = lambda v: lax.ppermute(v, "ctx", [(0, 1), (1, 0)])

    tok = tokens_in[0]
    weighted_b = cotangent[0] * absorbed[0].astype(bf16)[:, None]
    tok_all = jnp.concatenate([tok, swap(tok)], 0)
    wtd_all = jnp.concatenate([weighted_b, swap(weighted_b)], 0)
    pos_all = jnp.concatenate([positions[0], swap(positions[0])], 0)

    modulation = dot(cond_vec, ada_weight) + ada_bias.astype(f32)
    shift_one, scale_one, gate_one, shift_two, scale_two, gate_two = jnp.split(modulation, 6, -1)
    gain_one = norm1_gain.astype(f32)[None]
    gain_two = norm2_gain.astype(f32)[None]
    stream = tok_all.astype(f32)
    a_one, inv_one = layer_stats(stream)
    normed_one = (a_one * gain_one * (1.0 + scale_one) + shift_one).astype(bf16)

    def cols(w, start, n):
        return lax.dynamic_slice_in_dim(w, start, n, 1)

    def rows(w, start, n):
        return lax.dynamic_slice_in_dim(w, start, n, 0)

    w_q = cols(qkv_weight, core * hw, hw)
    w_k = cols(qkv_weight, width + core * hw, hw)
    w_v = cols(qkv_weight, 2 * width + core * hw, hw)
    cos_t, sin_t = tables(pos_all)
    cos_w = jnp.tile(cos_t, (1, hw // HEAD_DIM))
    sin_w = jnp.tile(sin_t, (1, hw // HEAD_DIM))
    q_pre, k_pre = dot(normed_one, w_q), dot(normed_one, w_k)
    queries = (SCORE_SCALE * (q_pre * cos_w + swap_halves(q_pre) * sin_w)).astype(bf16)
    keys = (k_pre * cos_w + swap_halves(k_pre) * sin_w).astype(bf16)
    values = dot(normed_one, w_v).astype(bf16)

    att_t, prob, inverse = attn_fwd(queries, keys, values, 512)
    att_other = swap(att_t[:, span:])
    w_o_mine = rows(out_weight, core * hw, hw)
    w_o_other = rows(out_weight, (1 - core) * hw, hw)
    branch_att = dot_tn(att_t[:, :span], w_o_mine) + dot_tn(att_other, w_o_other)
    middle = stream[:span] + gate_one * branch_att
    a_two, inv_two = layer_stats(middle)
    normed_two = (a_two * gain_two * (1.0 + scale_two) + shift_two).astype(bf16)
    n2_all = jnp.concatenate([normed_two, swap(normed_two)], 0)

    w1 = cols(fc1_weight, core * hf, hf)
    b1 = lax.dynamic_slice_in_dim(fc1_bias, core * hf, hf, 0).astype(f32)
    w2 = rows(fc2_weight, core * hf, hf)
    hidden_pre = dot(n2_all, w1) + b1
    c0 = 0.7978845608028654
    th = jnp.tanh(c0 * (hidden_pre + 0.044715 * hidden_pre * hidden_pre * hidden_pre))
    hidden = (0.5 * hidden_pre * (1.0 + th)).astype(bf16)
    slope = 0.5 * (1.0 + th) + 0.5 * hidden_pre * (1.0 - th * th) * c0 * (
        1.0 + 3 * 0.044715 * hidden_pre * hidden_pre
    )
    wtd = wtd_all.astype(f32)
    g_mlp = (wtd * gate_two).astype(bf16)
    grad_pre = (dot_nt(g_mlp, w2) * slope).astype(bf16)
    grad_fc1 = dot_tn(n2_all, grad_pre).astype(bf16)
    red_fc1 = grid.reduce(grad_fc1)
    grad_fc2 = dot_tn(hidden, g_mlp).astype(bf16)
    keep2 = cols(grad_fc2, core * hw, hw)
    got2 = swap(cols(grad_fc2, (1 - core) * hw, hw))
    low2 = jnp.where(core == 0, keep2, got2)
    high2 = jnp.where(core == 0, got2, keep2)
    red_fc2 = grid.reduce(jnp.concatenate([low2, high2], 0))
    sum_fc2b = jnp.sum(g_mlp.astype(f32), axis=0)
    sum_fc1b = jnp.sum(grad_pre.astype(f32), axis=0)
    part_mlp = dot(hidden, w2)
    g_gate_two = jnp.sum(wtd * part_mlp, axis=0) + fc2_bias.astype(f32) * jnp.sum(wtd[:span], axis=0)
    branch_mlp = part_mlp[:span] + swap(part_mlp[span:].astype(bf16)).astype(f32) + fc2_bias.astype(f32)
    mixed = (middle + gate_two * branch_mlp).astype(bf16)
    part_n2 = dot_nt(grad_pre, w1)
    g_n2 = part_n2[:span] + swap(part_n2[span:].astype(bf16)).astype(f32)

    g_shift_two = jnp.sum(g_n2, axis=0)
    sum_ga_two = jnp.sum(g_n2 * a_two, axis=0)
    ga = g_n2 * gain_two * (1.0 + scale_two)
    g_mid = wtd[:span] + inv_two * (
        ga - jnp.mean(ga, -1, keepdims=True) - a_two * jnp.mean(ga * a_two, -1, keepdims=True)
    )
    g_gate_one = jnp.sum(g_mid * branch_att, axis=0)
    g_att = (g_mid * gate_one).astype(bf16)
    g_att_all = jnp.concatenate([g_att, swap(g_att)], 0)
    g_attn_t = dot_nt(w_o_mine, g_att_all).astype(bf16)
    grad_out = dot(att_t, g_att_all).astype(bf16)
    keep_o = cols(grad_out, core * hw, hw)
    got_o = swap(cols(grad_out, (1 - core) * hw, hw))
    low_o = jnp.where(core == 0, keep_o, got_o)
    high_o = jnp.where(core == 0, got_o, keep_o)
    red_out = grid.reduce(jnp.concatenate([low_o, high_o], 0))

    dq_t, dk, dv = attn_bwd(prob, inverse, g_attn_t, att_t, queries, keys, values, 512)
    dq = dq_t.T
    g_q = (dq * cos_w - swap_halves(dq) * sin_w).astype(bf16)
    g_k = (dk * cos_w - swap_halves(dk) * sin_w).astype(bf16)
    g_qkv = jnp.concatenate([g_q, g_k, dv], 1)
    grad_qkv = dot_tn(normed_one, g_qkv).astype(bf16)
    red_qkv = grid.reduce(grad_qkv)
    w_qkv = jnp.concatenate([w_q, w_k, w_v], 1)
    part_n1 = dot_nt(g_qkv, w_qkv)
    g_n1 = part_n1[:span] + swap(part_n1[span:].astype(bf16)).astype(f32)
    a_own = a_one[:span]
    g_shift_one = jnp.sum(g_n1, axis=0)
    sum_ga_one = jnp.sum(g_n1 * a_own, axis=0)
    ga = g_n1 * gain_one * (1.0 + scale_one)
    input_grad = (
        g_mid
        + inv_one[:span]
        * (ga - jnp.mean(ga, -1, keepdims=True) - a_own * jnp.mean(ga * a_own, -1, keepdims=True))
    ).astype(bf16)

    vec = jnp.stack(
        [
            g_shift_one, sum_ga_one * gain_one[0], g_gate_one,
            g_shift_two, sum_ga_two * gain_two[0], g_gate_two,
            sum_ga_one * (1.0 + scale_one[0]), sum_ga_two * (1.0 + scale_two[0]),
        ]
    )
    vec = vec + swap(vec)
    g_mod = vec[:6].reshape(1, 6 * width)
    cond_grad = lax.dot_general(
        g_mod, ada_weight.astype(f32), (((1,), (1,)), ((), ())),
        precision=lax.Precision.HIGHEST, preferred_element_type=f32,
    )
    other_b1 = swap(sum_fc1b)
    fc1b = jnp.where(
        core == 0, jnp.concatenate([sum_fc1b, other_b1]), jnp.concatenate([other_b1, sum_fc1b])
    )
    na, nb, nc = 6 * width // ndp, width // ndp, ff // ndp
    small = jnp.concatenate(
        [
            g_mod.reshape(ndp, na), vec[6].reshape(ndp, nb), vec[7].reshape(ndp, nb),
            sum_fc2b.reshape(ndp, nb), fc1b.reshape(ndp, nc),
        ],
        axis=1,
    )
    got = grid.spread(small)
    cond_all = grid.spread(jnp.broadcast_to(cond_vec.astype(f32), (ndp, cond_vec.shape[1])))
    ada_grad = lax.dot_general(
        cond_all, got[:, :na], (((0,), (0,)), ((), ())),
        precision=lax.Precision.HIGHEST, preferred_element_type=f32,
    )
    sums = jnp.sum(got, axis=0)
    ada_bias_grad = sums[:na]
    norm1_grad = sums[na : na + nb]
    norm2_grad = sums[na + nb : na + 2 * nb]
    fc2_bias_grad = sums[na + 2 * nb : na + 3 * nb]
    fc1_bias_grad = sums[na + 3 * nb :]

    def both(mine):
        mine_b = mine.astype(bf16)
        other = swap(mine_b)
        low = jnp.where(core == 0, mine_b, other).astype(f32)
        high = jnp.where(core == 0, other, mine_b).astype(f32)
        return low, high

    fc1_grad = jnp.concatenate(both(red_fc1), 1)
    fc2_grad = jnp.concatenate(both(red_fc2), 1)
    out_grad = jnp.concatenate(both(red_out), 1)
    lo, hi = both(red_qkv)
    qkv_grad = jnp.concatenate(
        [lo[:, :hw], hi[:, :hw], lo[:, hw : 2 * hw], hi[:, hw : 2 * hw], lo[:, 2 * hw :], hi[:, 2 * hw :]], 1
    )
    return (
        mixed[None], input_grad[None], cond_grad, norm1_grad, qkv_grad, out_grad, norm2_grad,
        fc1_grad, fc1_bias_grad, fc2_grad, fc2_bias_grad, ada_grad, ada_bias_grad,
    )


def layer_norm(stream):
    row_mean = jnp.mean(stream, axis=-1, keepdims=True)
    centred = stream - row_mean
    variance = jnp.mean(centred * centred, axis=-1, keepdims=True)
    return centred * lax.rsqrt(variance + EPS)


def pre_norm(stream, norm_gain, shift_vec, scale_vec):
    return layer_norm(stream) * norm_gain * (1.0 + scale_vec[:, None, :]) + shift_vec[:, None, :]


def gelu_tanh(stream):
    return jax.nn.gelu(stream, approximate=True)


def block_rows(row_count):
    size_now = row_count
    while size_now > 512 and size_now % 2 == 0:
        size_now = size_now // 2
    return size_now


def rotary_tables(positions):
    inv_freq = 10000.0 ** (-jnp.arange(0, HEAD_DIM, 2).astype(jnp.float32) / HEAD_DIM)
    angles = positions.astype(jnp.float32)[..., None] * inv_freq
    cos_table = jnp.concatenate([jnp.cos(angles), jnp.cos(angles)], axis=-1)[..., None, :]
    sin_table = jnp.concatenate([jnp.sin(angles), jnp.sin(angles)], axis=-1)[..., None, :]
    return (cos_table, sin_table)


def rotate_pos(stream, cos_table, sin_table):
    half_dim = stream.shape[-1] // 2
    turned = jnp.concatenate([-stream[..., half_dim:], stream[..., :half_dim]], axis=-1)
    return stream * cos_table + turned * sin_table


def over_blocks(step_fn, fold_state, pieces):
    row_count = pieces[0].shape[1]
    size_now = block_rows(row_count)

    def one_turn(turn_idx, inner_state):
        part_list = tuple(
            (
                lax.dynamic_slice_in_dim(member, turn_idx * size_now, size_now, 1)
                for member in pieces
            )
        )
        return step_fn(inner_state, part_list, turn_idx * size_now)

    return lax.fori_loop(0, row_count // size_now, one_turn, fold_state)


def score_grads(query_blk, key_blk, value_blk, grad_blk, top_blk, total_blk, delta_blk):
    scores = (
        jnp.einsum("sqhd,skhd->sqhk", query_blk, key_blk, preferred_element_type=jnp.float32)
        * SCORE_SCALE
    )
    probability = jnp.exp(scores - top_blk[..., None]) / total_blk[..., None]
    grad_prob = jnp.einsum(
        "sqhd,skhd->sqhk", grad_blk, value_blk, preferred_element_type=jnp.float32
    )
    grad_scores = (probability * (grad_prob - delta_blk[..., None])).astype(jnp.bfloat16)
    return (probability, grad_scores)


def local_any(
    tokens_in,
    cond_vec,
    positions,
    absorbed,
    cotangent,
    norm1_gain,
    qkv_weight,
    out_weight,
    norm2_gain,
    fc1_weight,
    fc1_bias,
    fc2_weight,
    fc2_bias,
    ada_weight,
    ada_bias,
):
    seqs_here, span_len, model_width = tokens_in.shape
    head_shape = (seqs_here, span_len, HEADS, HEAD_DIM)
    stream = tokens_in.astype(jnp.float32)
    modulation = jnp.dot(
        cond_vec, ada_weight, preferred_element_type=jnp.float32
    ) + ada_bias.astype(jnp.float32)
    shift_one, scale_one, gate_one, shift_two, scale_two, gate_two = jnp.split(
        modulation, 6, axis=-1
    )
    gain_one = norm1_gain.astype(jnp.float32)
    gain_two = norm2_gain.astype(jnp.float32)
    normed_f, pull_one = jax.vjp(pre_norm, stream, gain_one, shift_one, scale_one)
    normed_one = normed_f.astype(jnp.bfloat16)
    projected = jnp.dot(normed_one, qkv_weight, preferred_element_type=jnp.float32)
    cos_table, sin_table = rotary_tables(positions)
    turned_pair, pull_rot = jax.vjp(
        lambda query_pre, key_pre: (
            rotate_pos(query_pre, cos_table, sin_table),
            rotate_pos(key_pre, cos_table, sin_table),
        ),
        projected[..., :model_width].reshape(head_shape),
        projected[..., model_width : 2 * model_width].reshape(head_shape),
    )
    queries = turned_pair[0].astype(jnp.bfloat16)
    key_loc = turned_pair[1].astype(jnp.bfloat16).reshape(seqs_here, span_len, model_width)
    value_loc = projected[..., 2 * model_width :].astype(jnp.bfloat16)

    def forward_step(fold_state, part_list, offset):
        run_max, run_sum, run_acc = fold_state
        key_blk = part_list[0].reshape(seqs_here, -1, HEADS, HEAD_DIM)
        value_blk = part_list[1].reshape(seqs_here, -1, HEADS, HEAD_DIM)
        scores = (
            jnp.einsum("sqhd,skhd->sqhk", queries, key_blk, preferred_element_type=jnp.float32)
            * SCORE_SCALE
        )
        new_max = jnp.maximum(run_max, jnp.max(scores, axis=-1))
        raised = jnp.exp(scores - new_max[..., None])
        shrink = jnp.exp(run_max - new_max)
        run_sum = run_sum * shrink + jnp.sum(raised, axis=-1)
        run_acc = run_acc * shrink[..., None] + jnp.einsum(
            "sqhk,skhd->sqhd",
            raised.astype(jnp.bfloat16),
            value_blk,
            preferred_element_type=jnp.float32,
        )
        return (new_max, run_sum, run_acc)

    empty_state = (
        jnp.full((seqs_here, span_len, HEADS), NEG_START, jnp.float32),
        jnp.zeros((seqs_here, span_len, HEADS), jnp.float32),
        jnp.zeros(head_shape, jnp.float32),
    )
    final_max, final_sum, final_acc = over_blocks(
        forward_step,
        empty_state,
        (
            lax.all_gather(key_loc, "ctx", axis=1, tiled=True),
            lax.all_gather(value_loc, "ctx", axis=1, tiled=True),
        ),
    )
    attn_out = final_acc / final_sum[..., None]
    attended = attn_out.reshape(seqs_here, span_len, model_width).astype(jnp.bfloat16)
    branch_att = jnp.dot(attended, out_weight, preferred_element_type=jnp.float32)
    middle = stream + gate_one[:, None, :] * branch_att
    normed_f2, pull_two = jax.vjp(pre_norm, middle, gain_two, shift_two, scale_two)
    normed_two = normed_f2.astype(jnp.bfloat16)
    hidden_pre = jnp.dot(
        normed_two, fc1_weight, preferred_element_type=jnp.float32
    ) + fc1_bias.astype(jnp.float32)
    hidden_f, pull_gelu = jax.vjp(gelu_tanh, hidden_pre)
    hidden = hidden_f.astype(jnp.bfloat16)
    branch_mlp = jnp.dot(hidden, fc2_weight, preferred_element_type=jnp.float32) + fc2_bias.astype(
        jnp.float32
    )
    mixed = (middle + gate_two[:, None, :] * branch_mlp).astype(jnp.bfloat16)
    weighted = cotangent.astype(jnp.float32) * absorbed.astype(jnp.float32)[..., None]
    grad_gate_two = jnp.sum(weighted * branch_mlp, axis=1)
    grad_mlp = (weighted * gate_two[:, None, :]).astype(jnp.bfloat16)
    grad_fc2b = jnp.sum(grad_mlp.astype(jnp.float32), axis=(0, 1))
    grad_fc2 = jnp.einsum("scf,scd->fd", hidden, grad_mlp, preferred_element_type=jnp.float32)
    grad_hidden = jnp.einsum(
        "scd,fd->scf", grad_mlp, fc2_weight, preferred_element_type=jnp.float32
    )
    grad_pre = pull_gelu(grad_hidden)[0].astype(jnp.bfloat16)
    grad_fc1b = jnp.sum(grad_pre.astype(jnp.float32), axis=(0, 1))
    grad_fc1 = jnp.einsum("scd,scf->df", normed_two, grad_pre, preferred_element_type=jnp.float32)
    grad_normed_two = jnp.einsum(
        "scf,df->scd", grad_pre, fc1_weight, preferred_element_type=jnp.float32
    )
    grad_mid_part, grad_gain_two, grad_shift_two, grad_scale_two = pull_two(grad_normed_two)
    grad_middle = weighted + grad_mid_part
    grad_gate_one = jnp.sum(grad_middle * branch_att, axis=1)
    grad_att = (grad_middle * gate_one[:, None, :]).astype(jnp.bfloat16)
    grad_out = jnp.einsum("scd,sce->de", attended, grad_att, preferred_element_type=jnp.float32)
    grad_attended = (
        jnp.einsum("sce,de->scd", grad_att, out_weight, preferred_element_type=jnp.float32)
        .astype(jnp.bfloat16)
        .reshape(head_shape)
    )
    row_delta = jnp.sum(grad_attended.astype(jnp.float32) * attn_out, axis=-1)

    def query_only_step(fold_state, part_list, offset):
        piece_len = part_list[0].shape[1]
        key_blk = part_list[0].reshape(seqs_here, piece_len, HEADS, HEAD_DIM)
        value_blk = part_list[1].reshape(seqs_here, piece_len, HEADS, HEAD_DIM)
        probability, grad_scores = score_grads(
            queries, key_blk, value_blk, grad_attended, final_max, final_sum, row_delta
        )
        return (
            fold_state
            + jnp.einsum(
                "sqhk,skhd->sqhd", grad_scores, key_blk, preferred_element_type=jnp.float32
            )
            * SCORE_SCALE
        )

    start_state = jnp.zeros(head_shape, jnp.float32)
    back_state = over_blocks(
        query_only_step,
        start_state,
        (
            lax.all_gather(key_loc, "ctx", axis=1, tiled=True),
            lax.all_gather(value_loc, "ctx", axis=1, tiled=True),
        ),
    )
    key_heads = key_loc.reshape(head_shape)
    value_heads = value_loc.reshape(head_shape)

    def local_key_step(fold_state, part_list, offset):
        grad_key_loc, grad_value_loc = fold_state
        query_blk = part_list[0].astype(jnp.bfloat16)
        grad_blk = part_list[1].astype(jnp.bfloat16)
        probability, grad_scores = score_grads(
            query_blk, key_heads, value_heads, grad_blk, part_list[2], part_list[3], part_list[4]
        )
        grad_value_loc = grad_value_loc + jnp.einsum(
            "sqhk,sqhd->skhd",
            probability.astype(jnp.bfloat16),
            grad_blk,
            preferred_element_type=jnp.float32,
        )
        grad_key_loc = (
            grad_key_loc
            + jnp.einsum(
                "sqhk,sqhd->skhd", grad_scores, query_blk, preferred_element_type=jnp.float32
            )
            * SCORE_SCALE
        )
        return (grad_key_loc, grad_value_loc)

    key_start = (jnp.zeros(head_shape, jnp.float32), jnp.zeros(head_shape, jnp.float32))
    grad_key_h, grad_value_h = over_blocks(
        local_key_step,
        key_start,
        (
            lax.all_gather(queries.astype(jnp.float32), "ctx", axis=1, tiled=True),
            lax.all_gather(grad_attended.astype(jnp.float32), "ctx", axis=1, tiled=True),
            lax.all_gather(final_max, "ctx", axis=1, tiled=True),
            lax.all_gather(final_sum, "ctx", axis=1, tiled=True),
            lax.all_gather(row_delta, "ctx", axis=1, tiled=True),
        ),
    )
    grad_key_loc = grad_key_h.reshape(seqs_here, span_len, model_width)
    grad_value_loc = grad_value_h.reshape(seqs_here, span_len, model_width)
    grad_query_pre, grad_key_pre = pull_rot((back_state, grad_key_loc.reshape(head_shape)))
    grad_proj = jnp.concatenate(
        [
            grad_query_pre.reshape(seqs_here, span_len, model_width),
            grad_key_pre.reshape(seqs_here, span_len, model_width),
            grad_value_loc,
        ],
        axis=-1,
    ).astype(jnp.bfloat16)
    grad_qkv = jnp.einsum("scd,sce->de", normed_one, grad_proj, preferred_element_type=jnp.float32)
    grad_normed_one = jnp.einsum(
        "sce,de->scd", grad_proj, qkv_weight, preferred_element_type=jnp.float32
    )
    grad_in_part, grad_gain_one, grad_shift_one, grad_scale_one = pull_one(grad_normed_one)
    input_grad = (grad_middle + grad_in_part).astype(jnp.bfloat16)
    partial_mod = jnp.concatenate(
        [
            grad_shift_one,
            grad_scale_one,
            grad_gate_one,
            grad_shift_two,
            grad_scale_two,
            grad_gate_two,
        ],
        axis=-1,
    )
    grad_mod = lax.psum(partial_mod, "ctx")
    cond_grad = jnp.einsum(
        "se,ce->sc",
        grad_mod,
        ada_weight.astype(jnp.float32),
        precision=lax.Precision.HIGHEST,
        preferred_element_type=jnp.float32,
    )
    first_cycle = (lax.axis_index("ctx") == 0).astype(jnp.float32)
    grad_ada = (
        jnp.einsum(
            "sc,se->ce",
            cond_vec.astype(jnp.float32),
            grad_mod,
            precision=lax.Precision.HIGHEST,
            preferred_element_type=jnp.float32,
        )
        * first_cycle
    )
    grad_adab = jnp.sum(grad_mod, axis=0) * first_cycle
    (
        part_g1,
        part_qkv,
        part_out,
        part_g2,
        part_fc1,
        part_fc1b,
        part_fc2,
        part_fc2b,
        part_ada,
        part_adab,
    ) = (
        lax.psum_scatter(grad_gain_one, "dp", scatter_dimension=0, tiled=True),
        lax.psum_scatter(grad_qkv, "dp", scatter_dimension=0, tiled=True),
        lax.psum_scatter(grad_out, "dp", scatter_dimension=0, tiled=True),
        lax.psum_scatter(grad_gain_two, "dp", scatter_dimension=0, tiled=True),
        lax.psum_scatter(grad_fc1, "dp", scatter_dimension=0, tiled=True),
        lax.psum_scatter(grad_fc1b, "dp", scatter_dimension=0, tiled=True),
        lax.psum_scatter(grad_fc2, "dp", scatter_dimension=0, tiled=True),
        lax.psum_scatter(grad_fc2b, "dp", scatter_dimension=0, tiled=True),
        lax.psum_scatter(grad_ada, "dp", scatter_dimension=1, tiled=True),
        lax.psum_scatter(grad_adab, "dp", scatter_dimension=0, tiled=True),
    )
    summed = lax.psum(
        (
            part_g1,
            part_qkv,
            part_out,
            part_g2,
            part_fc1,
            part_fc1b,
            part_fc2,
            part_fc2b,
            part_ada,
            part_adab,
        ),
        "ctx",
    )
    return (mixed, input_grad, cond_grad) + tuple(summed)


def local(*args, ndp, nctx):
    seqs, span, _ = args[0].shape
    if nctx == 2 and seqs == 1 and ndp % 4 == 0 and span % 256 == 0:
        return local_pair(*args, ndp=ndp)
    return local_any(*args)


def solution(mesh):
    in_specs = (
        P("dp", "ctx", None),
        P("dp", None),
        P("dp", "ctx"),
        P("dp", "ctx"),
        P("dp", "ctx", None),
        P(),
        P(),
        P(),
        P(),
        P(),
        P(),
        P(),
        P(),
        P(),
        P(),
    )
    out_specs = (
        P("dp", "ctx", None),
        P("dp", "ctx", None),
        P("dp", None),
        P("dp"),
        P("dp", None),
        P("dp", None),
        P("dp"),
        P("dp", None),
        P("dp"),
        P("dp", None),
        P("dp"),
        P(None, "dp"),
        P("dp"),
    )
    step = functools.partial(local, ndp=mesh.shape["dp"], nctx=mesh.shape["ctx"])
    return jax.shard_map(step, mesh=mesh, in_specs=in_specs, out_specs=out_specs, check_vma=False)
```

```python
import functools

import jax
import jax.numpy as jnp
import numpy as np
from jax import lax
from jax.experimental import pallas as pl
from jax.experimental.pallas import tpu as pltpu
from jax.sharding import PartitionSpec as P

HEADS = 12
HEAD_DIM = 64
EPS = 1e-05
SCORE_SCALE = 0.125
NEG_START = -1e30
F32, BF16 = jnp.float32, jnp.bfloat16
COST = 2e8


def dot(a, b):
    return jnp.dot(a, b, preferred_element_type=F32)


def dot_tn(a, b):
    return lax.dot_general(a, b, (((0,), (0,)), ((), ())), preferred_element_type=F32)


def dot_nt(a, b):
    return lax.dot_general(a, b, (((1,), (1,)), ((), ())), preferred_element_type=F32)


def sds(shape, dtype):
    return jax.ShapeDtypeStruct(shape, dtype)


def hbm(x):
    return pltpu.with_memory_space_constraint(x, pltpu.HBM)


class Order:
    def __init__(self, place):
        self.place, self.token = place, None

    def call(
        self, body, args, grid, in_specs, out_specs, out_shape, scratch=(), mb=32, us=1.0, aliases=None, after=(),
        name=None,
    ):
        after = list(after) + ([] if self.token is None else [self.token])
        extra, n_in, n_out = len(after), 1 + len(args), len(out_shape)

        def inner(*refs):
            outs = refs[n_in + extra :]
            body(*refs[:n_in], *outs[:n_out], *outs[n_out + 1 :])

        *outs, self.token = pl.pallas_call(
            inner,
            grid_spec=pltpu.PrefetchScalarGridSpec(
                num_scalar_prefetch=1,
                grid=grid,
                in_specs=list(in_specs) + [ANY] * extra,
                out_specs=list(out_specs) + [ANY],
                scratch_shapes=list(scratch),
            ),
            out_shape=list(out_shape) + [sds((8, 128), F32)],
            input_output_aliases=aliases or {},
            compiler_params=pltpu.CompilerParams(vmem_limit_bytes=mb << 20),
            cost_estimate=pl.CostEstimate(flops=int(us * COST), bytes_accessed=1 << 16, transcendentals=0),
            name=name,
        )(self.place, *args, *after)
        return outs


ANY = pl.BlockSpec(memory_space=pl.ANY)


def whole(shape):
    return pl.BlockSpec(shape, lambda *a: (0,) * len(shape))


def layer_stats(stream):
    row_mean = jnp.mean(stream, axis=-1, keepdims=True)
    centred = stream - row_mean
    variance = jnp.mean(centred * centred, axis=-1, keepdims=True)
    inv = lax.rsqrt(variance + EPS)
    return centred * inv, inv


def swap_lanes(x):
    lane = lax.broadcasted_iota(jnp.int32, x.shape, 1) % HEAD_DIM
    half = HEAD_DIM // 2
    return jnp.where(lane < half, pltpu.roll(x, 128 - half, 1), pltpu.roll(x, half, 1))


def mask_half(value, head):
    lane = lax.broadcasted_iota(jnp.int32, value.shape, 1)
    keep = (lane < HEAD_DIM) if head == 0 else (lane >= HEAD_DIM)
    return jnp.where(keep, value, jnp.zeros_like(value))


def attend_body(
    s_ref, ta_ref, tb_ref, cond_ref, ada_ref, adab_ref, gain_ref, wq_ref, wk_ref, wv_ref, pa_ref, pb_ref, freq_ref,
    cot_ref, abs_ref,
    n1_out, q_out, k_out, v_out, cost_ref, sint_ref,
    out_ref, prob_ref, inv_ref, mod_ref, wtd_ref, km_ref, vt_ref, n1_ref, q_ref, k_ref, v_ref,
):
    pair, step = pl.program_id(0), pl.program_id(1)
    span, width = ta_ref.shape
    blk = out_ref.shape[1]

    @pl.when((pair == 0) & (step == 0))
    def _():
        kept = jnp.broadcast_to(abs_ref[...].astype(F32), (128, span)).T[:, 0:1]
        wtd_ref[...] = (cot_ref[...].astype(F32) * kept).astype(BF16)
        cond = jnp.broadcast_to(cond_ref[...].astype(F32), (16, cond_ref.shape[1])).astype(BF16)
        mod_ref[...] = dot(cond, ada_ref[...])[:8] + adab_ref[...].astype(F32)[None, :]
        shift, scale = mod_ref[0:1, 0:width], mod_ref[0:1, width : 2 * width]
        gain = gain_ref[...].astype(F32)[None, :] * (1.0 + scale)
        for half, (t_ref, p_ref) in enumerate(((ta_ref, pa_ref), (tb_ref, pb_ref))):
            rows = slice(half * span, (half + 1) * span)
            angles = freq_ref[...] * p_ref[...].astype(F32)
            cos_h, sin_h = jnp.cos(angles), jnp.sin(angles)
            cos_t, sin_t = rotation(cos_h, sin_h)
            cost_ref[:, rows] = cos_h
            sint_ref[:, rows] = sin_h
            cos_n, sin_n = cos_t.T, sin_t.T
            a_one, _ = layer_stats(t_ref[...].astype(F32))
            normed = (a_one * gain + shift).astype(BF16)
            n1_ref[rows, :] = normed
            q_pre = dot(normed, wq_ref[...])
            k_pre = dot(normed, wk_ref[...])
            v_ref[rows, :] = dot(normed, wv_ref[...]).astype(BF16)
            for p in range(q_pre.shape[1] // 128):
                at = slice(p * 128, (p + 1) * 128)
                part = q_pre[:, at]
                q_ref[rows, at] = (SCORE_SCALE * (part * cos_n + swap_lanes(part) * sin_n)).astype(BF16)
                part = k_pre[:, at]
                k_ref[rows, at] = (part * cos_n + swap_lanes(part) * sin_n).astype(BF16)

    lanes = pl.ds(pl.multiple_of(pair * 128, 128), 128)
    piece = jnp.minimum(pair * pl.num_programs(1) + step, n1_ref.shape[0] // n1_out.shape[0] - 1)
    n1_out[...] = n1_ref[pl.ds(pl.multiple_of(piece * n1_out.shape[0], 128), n1_out.shape[0]), :]

    @pl.when(step == 0)
    def _():
        keys = k_ref[:, lanes]
        q_out[...] = q_ref[:, lanes]
        k_out[...] = keys
        v_out[...] = v_ref[:, lanes]
        for head in (0, 1):
            km_ref[head] = mask_half(keys, head)
        vt_ref[...] = v_ref[:, lanes].T

    queries = q_ref[pl.ds(pl.multiple_of(step * blk, blk), blk), lanes]
    for head in (0, 1):
        rows = slice(head * HEAD_DIM, (head + 1) * HEAD_DIM)
        scores = dot_nt(km_ref[head], queries)
        top = jnp.max(scores, axis=0, keepdims=True)
        raised = jnp.exp(scores - top)
        total = jnp.sum(raised, axis=0, keepdims=True)
        prob = raised.astype(BF16)
        prob_ref[head] = prob
        inverse = 1.0 / total
        inv_ref[0, head : head + 1, :] = inverse
        out_ref[rows, :] = (dot(vt_ref[rows, :], prob) * inverse).astype(BF16)


def attend_call(order, tok, tok_o, cond, ada, adab, gain, qkv_weight, pos, pos_o, cot, absorbed):
    span, width = tok.shape
    length, hw = 2 * span, width // 2
    pairs, blk = hw // 128, 512
    freq = np.power(10000.0, -np.arange(0, HEAD_DIM, 2) / HEAD_DIM).astype(np.float32)[:, None]
    wspec = lambda j: pl.BlockSpec((width, hw), lambda p, i, s: (0, 2 * j + s[0]))
    col = pl.BlockSpec((length, 128), lambda p, i, s: (0, p))
    return order.call(
        attend_body,
        [hbm(tok), tok_o, hbm(cond), hbm(ada), hbm(adab), hbm(gain), *[hbm(qkv_weight)] * 3, hbm(pos), pos_o, hbm(jnp.asarray(freq)), hbm(cot), hbm(absorbed)],
        (pairs, length // blk),
        [whole(tok.shape), whole(tok.shape), whole(cond.shape), whole(ada.shape), whole(adab.shape), whole(gain.shape), wspec(0), wspec(1), wspec(2),
         whole(pos.shape), whole(pos.shape), whole(freq.shape), whole(cot.shape), whole(absorbed.shape)],
        [pl.BlockSpec((length // 4, width), lambda p, i, s: (jnp.minimum(p * (length // blk) + i, 3), 0)),
         col, col, col, whole((HEAD_DIM // 2, length)), whole((HEAD_DIM // 2, length)),
         pl.BlockSpec((128, blk), lambda p, i, s: (p, i)),
         pl.BlockSpec((2, length, blk), lambda p, i, s: (p, 0, i)),
         pl.BlockSpec((1, 8, blk), lambda p, i, s: (p, 0, i)), whole((8, ada.shape[1])), whole(tok.shape)],
        [sds((length, width), BF16)] + [sds((length, hw), BF16)] * 3
        + [sds((HEAD_DIM // 2, length), F32)] * 2
        + [sds((hw, length), BF16), pltpu.HBM((2 * pairs, length, length), BF16), sds((pairs, 8, length), F32),
           sds((8, ada.shape[1]), F32), sds(tok.shape, BF16)],
        scratch=[pltpu.VMEM((2, length, 128), BF16), pltpu.VMEM((128, length), BF16),
                 pltpu.VMEM((length, width), BF16)] + [pltpu.VMEM((length, hw), BF16)] * 3,
        mb=32, us=20, name="attend",
    )


def swap_rows(x):
    half = HEAD_DIM // 2
    return jnp.concatenate([x[half * j : half * (j + 1)] for j in (1, 0, 3, 2)], axis=0)


def rotation(cos_h, sin_h):
    return jnp.concatenate([cos_h] * 4, axis=0), jnp.concatenate([-sin_h, sin_h, -sin_h, sin_h], axis=0)


def attn_bwd_body(
    r, s_ref, prob_ref, inv_ref, gt_ref, out_ref, q_ref, k_ref, v_ref, cost_ref, sint_ref, n1_ref,
    g_ref, keep_ref, send_ref, vm_ref, kt_ref, dk_acc, dv_acc, acc_ref,
):
    step = pl.program_id(1)
    blk = q_ref.shape[0]

    @pl.when(step == 0)
    def _():
        values = v_ref[...]
        for head in (0, 1):
            vm_ref[head] = mask_half(values, head)
        kt_ref[...] = k_ref[...].T

    queries = q_ref[...]
    grad_t = gt_ref[...].astype(jnp.float32)
    row_id = lax.broadcasted_iota(jnp.int32, (128, blk), 0)
    inverse = jnp.where(row_id < HEAD_DIM, inv_ref[0, 0:1, :], inv_ref[0, 1:2, :])
    grad_t = grad_t * inverse
    product = grad_t * out_ref[...].astype(jnp.float32)
    grad_b = grad_t.astype(jnp.bfloat16)
    dk_new = None
    dq_parts = []
    for head in (0, 1):
        rows = slice(head * HEAD_DIM, (head + 1) * HEAD_DIM)
        delta = jnp.sum(product[rows], axis=0, keepdims=True)
        keep = (row_id < HEAD_DIM) if head == 0 else (row_id >= HEAD_DIM)
        grad_m = jnp.where(keep, grad_b, jnp.zeros_like(grad_b))
        grad_p = jnp.dot(vm_ref[head], grad_b, preferred_element_type=jnp.float32)
        prob = prob_ref[head]
        grad_s = (prob.astype(jnp.float32) * (grad_p - delta)).astype(jnp.bfloat16)
        dv_h = dot_nt(prob, grad_m)
        dk_h = dot(grad_s, mask_half(queries, head))
        if dk_new is None:
            dk_new, dv_new = dk_h, dv_h
        else:
            dk_new, dv_new = dk_new + dk_h, dv_new + dv_h
        dq_parts.append(dot(kt_ref[rows, :], grad_s) * SCORE_SCALE)
    dq_t = jnp.concatenate(dq_parts, axis=0)
    here = pl.ds(pl.multiple_of(step * blk, blk), blk)
    cos_t, sin_t = rotation(cost_ref[:, here], sint_ref[:, here])
    dq_t = dq_t * cos_t - swap_rows(dq_t) * sin_t
    g_ref[here, 0:128] = dq_t.T.astype(jnp.bfloat16)

    @pl.when(step == 0)
    def _():
        dk_acc[...] = dk_new
        dv_acc[...] = dv_new

    @pl.when(step > 0)
    def _():
        dk_acc[...] += dk_new
        dv_acc[...] += dv_new

    @pl.when(step == pl.num_programs(1) - 1)
    def _():
        dk = dk_acc[...]
        cos_t, sin_t = rotation(cost_ref[...], sint_ref[...])
        g_ref[:, 128:256] = (dk * cos_t.T - swap_lanes(dk) * sin_t.T).astype(jnp.bfloat16)
        g_ref[:, 256:384] = dv_acc[...].astype(jnp.bfloat16)
        acc_ref[...] = dot_tn(n1_ref[...], g_ref[...]).astype(jnp.bfloat16)
        store_parts(s_ref, acc_ref, r, keep_ref, send_ref)


def attn_bwd(
    order, start, count, prob, inverse, grad_t, out_t, queries, keys, values, cos_t, sin_t, normed_one,
    old, block, blocks,
):
    length = keys.shape[0]
    width = normed_one.shape[1]
    blk = 512
    r = width // 16
    col = pl.BlockSpec((length, 128), lambda p, i, s: (0, p + start))
    rowt = pl.BlockSpec((128, blk), lambda p, i, s: (p + start, i))
    out = pl.BlockSpec((2, 4, r, 384), lambda p, i, s: (0, 0, 0, p + block))
    args = [prob, inverse, grad_t, out_t, queries, keys, values, cos_t, sin_t, normed_one]
    aliases = {}
    after = []
    if old is not None:
        aliases = {1 + len(args) + j: 1 + j for j in range(2)}
        after = list(old)
    return order.call(
        functools.partial(attn_bwd_body, r), args, (count, length // blk),
        [
            pl.BlockSpec((2, length, blk), lambda p, i, s: (p + start, 0, i)),
            pl.BlockSpec((1, 8, blk), lambda p, i, s: (p + start, 0, i)),
            rowt, rowt,
            pl.BlockSpec((blk, 128), lambda p, i, s: (i, p + start)),
            col, col, whole(cos_t.shape), whole(cos_t.shape), whole(normed_one.shape),
        ],
        [pl.BlockSpec((length, 384), lambda p, i, s: (0, p))] + [out] * 2,
        [sds((length, 384 * count), BF16)] + [sds((2, 4, r, 384 * blocks), BF16)] * 2,
        scratch=[
            pltpu.VMEM((2, length, 128), BF16),
            pltpu.VMEM((128, length), BF16),
            pltpu.VMEM((length, 128), F32),
            pltpu.VMEM((length, 128), F32),
            pltpu.VMEM((width, 384), BF16),
        ],
        mb=18, us=8.0 * count, aliases=aliases, after=after, name="attn_bwd",
    )


def mix_body(s_ref, own_ref, got_ref, mid_ref, wtd_ref, mod_ref, bias_ref, out_ref, sum_ref):
    width = mid_ref.shape[1]
    branch = own_ref[...] + got_ref[...].astype(F32) + bias_ref[...].astype(F32)[None, :]
    out_ref[...] = (mid_ref[...] + mod_ref[0:1, 5 * width : 6 * width] * branch).astype(BF16)

    @pl.when(pl.program_id(0) == 0)
    def _():
        sum_ref[...] = jnp.zeros_like(sum_ref)

    sum_ref[0:1, :] += jnp.sum(wtd_ref[...].astype(F32) * branch, axis=0, keepdims=True)


def mix_call(order, own, got, mid, wtd, mod, bias):
    span, width = mid.shape
    blk = 256
    row = pl.BlockSpec((blk, width), lambda i, s: (i, 0))
    return order.call(
        mix_body, [own, got, mid, wtd, mod, bias], (span // blk,),
        [row] * 4 + [whole(mod.shape), whole(bias.shape)],
        [row, whole((8, width))], [sds((span, width), BF16), sds((8, width), F32)],
        mb=8, us=2.5, name="mix",
    )


def post_body(s_ref, att_ref, oth_ref, wm_ref, wo_ref, tok_ref, mod_ref, gain_ref, mid_ref, br_ref, n2_ref):
    width = tok_ref.shape[1]
    branch = dot_tn(att_ref[...], wm_ref[...]) + dot_tn(oth_ref[...], wo_ref[...])
    br_ref[...] = branch
    middle = tok_ref[...].astype(F32) + mod_ref[0:1, 2 * width : 3 * width] * branch
    mid_ref[...] = middle
    a_two, _ = layer_stats(middle)
    scale = mod_ref[0:1, 4 * width : 5 * width]
    n2_ref[...] = (
        a_two * (gain_ref[...].astype(F32)[None, :] * (1.0 + scale)) + mod_ref[0:1, 3 * width : 4 * width]
    ).astype(BF16)


def post_call(order, att_t, att_o, out_weight, tok, mod, gain):
    span, width = tok.shape
    hw = width // 2
    blk = 256
    n = span // blk
    row = pl.BlockSpec((blk, width), lambda i, s: (i, 0))
    return order.call(
        post_body, [att_t, att_o, out_weight, out_weight, tok, mod, gain], (n,),
        [
            pl.BlockSpec((hw, blk), lambda i, s: (0, i)),
            pl.BlockSpec((hw, blk), lambda i, s: (0, i + n)),
            pl.BlockSpec((hw, width), lambda i, s: (s[0], 0)),
            pl.BlockSpec((hw, width), lambda i, s: (1 - s[0], 0)),
            row, whole(mod.shape), whole(gain.shape),
        ],
        [row, row, row],
        [sds((span, width), F32), sds((span, width), F32), sds((span, width), BF16)],
        mb=8, us=3, name="post",
    )


def mlp_body(
    s_ref, n2a_ref, n2b_ref, wa_ref, wb_ref, mod_ref, w1_ref, b1_ref, w2_ref,
    hid_ref, pre_ref, gm_ref, b1g_ref, b2g_ref,
):
    step = pl.program_id(0)
    first = step < pl.num_programs(0) // 2
    width = n2a_ref.shape[1]
    x = jnp.where(first, n2a_ref[...], n2b_ref[...])
    wtd = jnp.where(first, wa_ref[...], wb_ref[...]).astype(F32)
    g_mlp = (wtd * mod_ref[0:1, 5 * width : 6 * width]).astype(BF16)
    gm_ref[...] = g_mlp
    bias = b1_ref[...].astype(F32)[None, :]
    hf = w1_ref.shape[1]
    v = dot(x, w1_ref[...]) + jnp.where(s_ref[0] == 0, bias[:, :hf], bias[:, hf:])
    gh = dot_nt(g_mlp, w2_ref[...])
    c0 = 0.7978845608028654
    c1 = c0 * 0.044715
    v2 = v * v
    th = jnp.tanh(v * (c0 + c1 * v2))
    up = 0.5 + 0.5 * th
    hid_ref[...] = (v * up).astype(BF16)
    slope = up + v * (0.5 - 0.5 * (th * th)) * (c0 + 3.0 * c1 * v2)
    pre = (gh * slope).astype(BF16)
    pre_ref[...] = pre
    b1_part = jnp.sum(pre.astype(F32), axis=0, keepdims=True)
    b2_part = jnp.sum(g_mlp.astype(F32), axis=0, keepdims=True)

    @pl.when(step == 0)
    def _():
        b1g_ref[...] = b1_part
        b2g_ref[...] = b2_part

    @pl.when(step > 0)
    def _():
        b1g_ref[...] += b1_part
        b2g_ref[...] += b2_part


def halves(blk, width, n):
    return [
        pl.BlockSpec((blk, width), lambda i, s: (jnp.minimum(i, n - 1), 0)),
        pl.BlockSpec((blk, width), lambda i, s: (jnp.maximum(i - n, 0), 0)),
    ]


def mlp_call(order, n2a, n2b, wa, wb, mod, w1, b1, w2):
    span, width = n2a.shape
    hf = w1.shape[1] // 2
    blk = 256
    n = span // blk
    row = lambda w: pl.BlockSpec((blk, w), lambda i, s: (i, 0))
    return order.call(
        mlp_body, [n2a, n2b, wa, wb, mod, w1, b1, w2], (2 * n,),
        halves(blk, width, n) + halves(blk, width, n)
        + [
            whole(mod.shape),
            pl.BlockSpec((width, hf), lambda i, s: (0, s[0])),
            whole(b1.shape),
            pl.BlockSpec((hf, width), lambda i, s: (s[0], 0)),
        ],
        [row(hf), row(hf), row(width), whole((1, hf)), whole((1, width))],
        [sds((2 * span, hf), BF16), sds((2 * span, hf), BF16), sds((2 * span, width), BF16),
         sds((1, hf), F32), sds((1, width), F32)],
        mb=10, us=9.6, name="mlp",
    )


def store_parts(s_ref, acc_ref, r, keep_ref, send_ref):
    for i in range(8):
        rest = sum(((i >> (2 - j)) & 1) * s_ref[6 + j] for j in range(3))
        for ref, bit in ((keep_ref, s_ref[1]), (send_ref, 1 - s_ref[1])):
            at = pl.ds(pl.multiple_of((rest + bit * s_ref[5]) * r, 16), r)
            ref[i // 4, i % 4] = acc_ref[at, :]


def wgrad_body(r, s_ref, la_ref, lb_ref, g_ref, keep_ref, send_ref, acc_ref):
    span = la_ref.shape[0]
    acc_ref[...] = (dot_tn(la_ref[...], g_ref[:span]) + dot_tn(lb_ref[...], g_ref[span:])).astype(BF16)
    store_parts(s_ref, acc_ref, r, keep_ref, send_ref)


def wgrad_call(order, left_a, left_b, right, blk):
    rows, cols = left_a.shape[1], right.shape[1]
    length = right.shape[0]
    r = rows // 16
    out = pl.BlockSpec((2, 4, r, blk), lambda i, s: (0, 0, 0, i))
    return order.call(
        functools.partial(wgrad_body, r), [left_a, left_b, right], (cols // blk,),
        [whole(left_a.shape), whole(left_b.shape), pl.BlockSpec((length, blk), lambda i, s: (0, i))],
        [out] * 2, [sds((2, 4, r, cols), BF16)] * 2,
        scratch=[pltpu.VMEM((rows, blk), BF16)], mb=8, us=4.2, name="wgrad_fc1",
    )


def wgrad2_body(r, s_ref, lm_ref, lo_ref, g_ref, keep_ref, send_ref, acc_ref):
    step, n = pl.program_id(0), pl.num_programs(0)
    mine = lax.div(step, n // 2) == s_ref[0]
    span = g_ref.shape[0] // 2
    rows = lm_ref.shape[1]
    here = pl.ds(pl.multiple_of(step * rows, 128), rows)

    @pl.when(mine)
    def _():
        acc_ref[here, :] = dot_tn(lm_ref[...], g_ref[...]).astype(BF16)

    @pl.when(jnp.logical_not(mine))
    def _():
        acc_ref[here, :] = (dot_tn(lo_ref[:span], g_ref[span:]) + dot_tn(lo_ref[span:], g_ref[:span])).astype(BF16)

    @pl.when(step == n - 1)
    def _():
        store_parts(s_ref, acc_ref, r, keep_ref, send_ref)


def wgrad2_call(order, hidden, hidden_o, g_mlp):
    length, hf = hidden.shape
    hw = g_mlp.shape[1] // 2
    r = hf // 8
    left = pl.BlockSpec((length, 4 * r), lambda i, s: (0, lax.rem(i, 2)))
    return order.call(
        functools.partial(wgrad2_body, r), [hidden, hidden_o, g_mlp], (4,),
        [left, left, pl.BlockSpec((length, hw), lambda i, s: (0, s[0]))],
        [whole((2, 4, r, hw))] * 2, [sds((2, 4, r, hw), BF16)] * 2,
        scratch=[pltpu.VMEM((2 * hf, hw), BF16)], mb=16, us=4.5, name="wgrad_fc2",
    )


def fold_body(s_ref, ka, ra, ks, rs, away_ref, stay_ref):
    away_ref[...] = ka[0] + ra[0]
    stay_ref[...] = ks[0] + rs[0]


def fold_call(order, step, keep, got):
    _, count, r, n = keep.shape
    blk = 768 if n % 768 == 0 else 384
    away = pl.BlockSpec((1, count, r, blk), lambda i, s: (1 - s[step], 0, 0, i))
    stay = pl.BlockSpec((1, count, r, blk), lambda i, s: (s[step], 0, 0, i))
    out = pl.BlockSpec((count, r, blk), lambda i, s: (0, 0, i))
    return order.call(
        fold_body, [keep, got, keep, got], (n // blk,), [away, away, stay, stay], [out] * 2,
        [sds((count, r, n), BF16)] * 2, mb=8, us=1.2, name="fold",
    )


def total(refs):
    out = refs[0][...].astype(F32)
    for ref in refs[1:]:
        out = out + ref[...].astype(F32)
    return out.astype(BF16)


def sum_ff_body(s_ref, *refs):
    one, two, out_ref = refs[:2], refs[2:4], refs[4]
    r, n = one[0].shape
    out_ref[:r] = total(one)
    second = total(two)
    width = second.shape[1]
    for q in range(n // width):
        out_ref[r:, q * width : (q + 1) * width] = second[q * r : (q + 1) * r]


def sum_ff_call(order, one, two):
    r, n = one[0].shape
    return order.call(
        sum_ff_body, [*one, *two], (1,), [whole(a.shape) for a in (*one, *two)],
        [whole((2 * r, n))], [sds((2 * r, n), BF16)], mb=8, us=1.0, name="sum_ff",
    )[0]


def place_ff_body(s_ref, mine_ref, other_ref, fc1_ref, fc2_ref):
    core = s_ref[0]
    r, n = fc1_ref.shape[0], mine_ref.shape[1]
    width = fc2_ref.shape[1] // 2
    for ref, at in ((mine_ref, core), (other_ref, 1 - core)):
        fc1_ref[:, pl.ds(pl.multiple_of(at * n, 128), n)] = ref[:r].astype(F32)
        cols = pl.ds(pl.multiple_of(at * width, 128), width)
        for q in range(n // width):
            fc2_ref[q * r : (q + 1) * r, cols] = ref[r:, q * width : (q + 1) * width].astype(F32)


def place_ff_call(order, mine, other, hw):
    r, n = mine.shape[0] // 2, mine.shape[1]
    shapes = [(r, 2 * n), (r * (n // hw), 2 * hw)]
    return order.call(
        place_ff_body, [mine, other], (1,), [whole(mine.shape)] * 2, [whole(x) for x in shapes],
        [sds(x, F32) for x in shapes], mb=8, us=1.0, name="place_ff",
    )


def sum_att_body(s_ref, *refs):
    one, two, out_ref = refs[:2], refs[2:4], refs[4]
    n = one[0].shape[1]
    out_ref[:, :n] = total(one)
    out_ref[:, n:] = total(two)


def sum_att_call(order, one, two):
    r, n = one[0].shape
    shape = (r, n + two[0].shape[1])
    return order.call(
        sum_att_body, [*one, *two], (1,), [whole(a.shape) for a in (*one, *two)],
        [whole(shape)], [sds(shape, BF16)], mb=8, us=1.0, name="sum_att",
    )[0]


def place_att_body(s_ref, mine_ref, other_ref, out_ref, qkv_ref):
    core = s_ref[0]
    width = out_ref.shape[1]
    hw = width // 2
    for ref, at in ((mine_ref, core), (other_ref, 1 - core)):
        out_ref[:, pl.ds(pl.multiple_of(at * hw, 128), hw)] = ref[:, :hw].astype(F32)
        for p in range(hw // 128):
            for j in range(3):
                to = pl.ds(pl.multiple_of(j * width + at * hw + p * 128, 128), 128)
                src = hw + p * 384 + j * 128
                qkv_ref[:, to] = ref[:, src : src + 128].astype(F32)


def place_att_call(order, mine, other, width):
    r = mine.shape[0]
    shapes = [(r, width), (r, 3 * width)]
    return order.call(
        place_att_body, [mine, other], (1,), [whole(mine.shape)] * 2, [whole(x) for x in shapes],
        [sds(x, F32) for x in shapes], mb=8, us=1.0, name="place_att",
    )


ROWS = 16


def pack_body(s_ref, s1_ref, s2_ref, s3_ref, b1_ref, b2_ref, g1_ref, g2_ref, mod_ref, cond_ref, out_ref):
    width = s1_ref.shape[1]
    h = width // 2
    core = s_ref[0]
    gain_one, gain_two = g1_ref[...].astype(F32)[None, :], g2_ref[...].astype(F32)[None, :]
    scale_one = 1.0 + mod_ref[0:1, width : 2 * width]
    scale_two = 1.0 + mod_ref[0:1, 4 * width : 5 * width]
    second_one, second_two = s1_ref[1:2, :], s2_ref[1:2, :]
    rows = [
        s1_ref[0:1, :], second_one * gain_one, s2_ref[2:3, :],
        s2_ref[0:1, :], second_two * gain_two, s3_ref[0:1, :],
    ]
    gains = [second_one * scale_one, second_two * scale_two]
    b2 = 0.5 * b2_ref[...]
    out_ref[...] = jnp.zeros_like(out_ref)
    nz = out_ref.shape[0] // ROWS
    per = 12 // nz
    for z in range(nz):
        at = z * ROWS
        for j in range(per):
            i = per * z + j
            out_ref[at + j : at + j + 1, :] = rows[i // 2][:, (i % 2) * h : (i % 2 + 1) * h]
        mine = jnp.where(core == z // (nz // 2), 1.0, 0.0)
        for j in range(2):
            i = 2 * (z % (nz // 2)) + j
            out_ref[at + 3 + j : at + 4 + j, :] = mine * b1_ref[:, i * h : (i + 1) * h]
        for j in range(4):
            out_ref[at + 5 + j : at + 6 + j, :] = gains[j // 2][:, (j % 2) * h : (j % 2 + 1) * h]
        for j in range(2):
            out_ref[at + 9 + j : at + 10 + j, :] = b2[:, j * h : (j + 1) * h]
        out_ref[at + 11 : at + 12, 0:128] = 0.5 * cond_ref[...].astype(F32)


def pack_call(order, nz, *args):
    h = args[0].shape[1] // 2
    return order.call(
        pack_body, list(args), (1,), [whole(a.shape) for a in args], [whole((nz * ROWS, h))],
        [sds((nz * ROWS, h), F32)], mb=8, us=1.0, name="pack",
    )[0]


def deal_body(nz, s_ref, a_ref, b_ref, ada_ref, cg_ref, *outs):
    both = a_ref[...] + b_ref[...]
    acc = outs[nz]
    acc[...] = both.reshape(acc.shape)
    for k in range(nz):
        outs[k][...] = acc[lax.bitwise_xor(s_ref[9], k)]
    per = 12 // nz
    flat = jnp.concatenate([both[z * ROWS + j : z * ROWS + j + 1] for z in range(nz) for j in range(per)], axis=1)
    high = flat.astype(BF16)
    rest = flat - high.astype(F32)
    mid = rest.astype(BF16)
    low = (rest - mid.astype(F32)).astype(BF16)
    terms = jnp.concatenate([high.astype(F32), mid.astype(F32), low.astype(F32)] + [jnp.zeros_like(flat)] * 13, axis=0)
    cg_ref[...] = jnp.sum(dot_nt(terms.astype(BF16), ada_ref[...]), axis=0, keepdims=True)


def deal_call(order, nz, mine, got, ada):
    n = mine.shape[1]
    return order.call(
        functools.partial(deal_body, nz), [mine, got, ada], (1,),
        [whole(mine.shape), whole(mine.shape), whole(ada.shape)],
        [whole((1, ada.shape[0]))] + [whole((ROWS, n))] * nz,
        [sds((1, ada.shape[0]), F32)] + [sds((ROWS, n), F32)] * nz,
        scratch=[pltpu.VMEM((nz, ROWS, n), F32)], mb=8, us=1.0, name="deal",
    )


def last_body(s_ref, *refs):
    packs, (ada_ref, sum_ref) = refs[:-2], refs[-2:]
    parts = [ref[k * ROWS : (k + 1) * ROWS] for ref in packs for k in range(ref.shape[0] // ROWS)]
    whole_sum = parts[0]
    for part in parts[1:]:
        whole_sum = whole_sum + part
    sum_ref[...] = whole_sum
    cond = jnp.concatenate([part[11:12, 0:128] for part in parts], axis=0)
    grads = jnp.concatenate([jnp.concatenate([part[j : j + 1] for j in range(3)], axis=1) for part in parts], axis=0)
    ada_ref[...] = lax.dot_general(
        cond, grads, (((0,), (0,)), ((), ())), precision=lax.Precision.HIGHEST, preferred_element_type=F32
    )


def last_call(order, packs):
    n = packs[0].shape[1]
    return order.call(
        last_body, packs, (1,), [whole(a.shape) for a in packs], [whole((128, 3 * n)), whole((ROWS, n))],
        [sds((128, 3 * n), F32), sds((ROWS, n), F32)], mb=8, us=1.0, name="small_last",
    )


def part_body(nt, s_ref, g_ref, w_ref, own_ref, oth_ref):
    step = pl.program_id(0)
    half = pl.num_programs(0) // 2
    part = dot_nt(g_ref[...], w_ref[...]) if nt else dot(g_ref[...], w_ref[...])

    @pl.when(step < half)
    def _():
        oth_ref[...] = part.astype(BF16)

    @pl.when(step >= half)
    def _():
        own_ref[...] = part


def part_call(order, nt, g, w):
    length, hf = g.shape
    width = w.shape[0] if nt else w.shape[1]
    blk = 256
    n = length // 2 // blk
    wspec = (
        pl.BlockSpec((width, hf), lambda i, s: (0, s[0]))
        if nt
        else pl.BlockSpec((hf, width), lambda i, s: (s[0], 0))
    )
    return order.call(
        functools.partial(part_body, nt), [g, w], (2 * n,),
        [pl.BlockSpec((blk, hf), lambda i, s: ((i + n) % (2 * n), 0)), wspec],
        [
            pl.BlockSpec((blk, width), lambda i, s: (jnp.maximum(i - n, 0), 0)),
            pl.BlockSpec((blk, width), lambda i, s: (jnp.minimum(i, n - 1), 0)),
        ],
        [sds((length // 2, width), F32), sds((length // 2, width), BF16)],
        mb=8, us=4.2, name="part",
    )


def norm2_body(s_ref, own_ref, got_ref, mid_ref, br_ref, wtd_ref, mod_ref, gain_ref, gmid_ref, gatt_ref, sum_ref):
    width = mid_ref.shape[1]
    g = own_ref[...] + got_ref[...].astype(F32)
    a_two, inv = layer_stats(mid_ref[...])
    ga = g * (gain_ref[...].astype(F32)[None, :] * (1.0 + mod_ref[0:1, 4 * width : 5 * width]))
    gaa = ga * a_two
    g_mid = wtd_ref[...].astype(F32) + inv * (
        ga - jnp.mean(ga, -1, keepdims=True) - a_two * jnp.mean(gaa, -1, keepdims=True)
    )
    gmid_ref[...] = g_mid
    gatt_ref[...] = (g_mid * mod_ref[0:1, 2 * width : 3 * width]).astype(BF16)
    sums = jnp.concatenate(
        [
            jnp.sum(g, axis=0, keepdims=True),
            jnp.sum(g * a_two, axis=0, keepdims=True),
            jnp.sum(g_mid * br_ref[...], axis=0, keepdims=True),
        ],
        axis=0,
    )

    @pl.when(pl.program_id(0) == 0)
    def _():
        sum_ref[...] = jnp.zeros_like(sum_ref)

    sum_ref[0:3, :] += sums


def norm2_call(order, own, got, mid, br, wtd, mod, gain):
    span, width = mid.shape
    blk = 256
    row = pl.BlockSpec((blk, width), lambda i, s: (i, 0))
    return order.call(
        norm2_body, [own, got, mid, br, wtd, mod, gain], (span // blk,),
        [row] * 5 + [whole(mod.shape), whole(gain.shape)],
        [row, row, whole((8, width))],
        [sds((span, width), F32), sds((span, width), BF16), sds((8, width), F32)],
        mb=8, us=3, name="norm2",
    )


def oproj_body(r, s_ref, w_ref, ga_ref, gb_ref, am_ref, ao_ref, gt_ref, keep_ref, send_ref, acc_ref):
    span = ga_ref.shape[0]
    half = am_ref.shape[0]
    core = s_ref[0]
    w = w_ref[...]
    gt_ref[:, :span] = dot_nt(w, ga_ref[...]).astype(BF16)
    gt_ref[:, span:] = dot_nt(w, gb_ref[...]).astype(BF16)
    cols = pl.ds(pl.multiple_of(core * half, 128), half)
    gac, gbc = ga_ref[:, cols], gb_ref[:, cols]
    mine = dot(am_ref[:, :span], gac) + dot(am_ref[:, span:], gbc)
    other = dot(ao_ref[:, span:], gac) + dot(ao_ref[:, :span], gbc)
    acc_ref[pl.ds(pl.multiple_of(core * half, 16), half), :] = mine.astype(BF16)
    acc_ref[pl.ds(pl.multiple_of((1 - core) * half, 16), half), :] = other.astype(BF16)
    store_parts(s_ref, acc_ref, r, keep_ref, send_ref)


def oproj_call(order, blocks, out_weight, ga, gb, att_t, att_o):
    span, width = ga.shape
    hw = width // 2
    r = width // 16
    out = pl.BlockSpec((2, 4, r, hw), lambda i, s: (0, 0, 0, 0))
    return order.call(
        functools.partial(oproj_body, r), [out_weight, ga, gb, att_t, att_o], (1,),
        [pl.BlockSpec((hw, width), lambda i, s: (s[0], 0)), whole(ga.shape), whole(ga.shape),
         whole(att_t.shape), whole(att_t.shape)],
        [whole((hw, 2 * span))] + [out] * 2,
        [sds((hw, 2 * span), BF16)] + [sds((2, 4, r, blocks * hw), BF16)] * 2,
        scratch=[pltpu.VMEM((width, hw), BF16)], mb=8, us=3, name="oproj",
    )


def norm1_body(s_ref, own_ref, got_ref, tok_ref, gmid_ref, mod_ref, gain_ref, out_ref, sum_ref):
    width = tok_ref.shape[1]
    g = own_ref[...] + got_ref[...].astype(F32)
    a_one, inv = layer_stats(tok_ref[...].astype(F32))
    ga = g * (gain_ref[...].astype(F32)[None, :] * (1.0 + mod_ref[0:1, width : 2 * width]))
    gaa = ga * a_one
    out_ref[...] = (
        gmid_ref[...]
        + inv * (ga - jnp.mean(ga, -1, keepdims=True) - a_one * jnp.mean(gaa, -1, keepdims=True))
    ).astype(BF16)

    @pl.when(pl.program_id(0) == 0)
    def _():
        sum_ref[...] = jnp.zeros_like(sum_ref)

    sum_ref[0:1, :] += jnp.sum(g, axis=0, keepdims=True)
    sum_ref[1:2, :] += jnp.sum(g * a_one, axis=0, keepdims=True)


def norm1_call(order, own, got, tok, gmid, mod, gain):
    span, width = tok.shape
    blk = 256
    row = pl.BlockSpec((blk, width), lambda i, s: (i, 0))
    return order.call(
        norm1_body, [own, got, tok, gmid, mod, gain], (span // blk,),
        [row] * 4 + [whole(mod.shape), whole(gain.shape)],
        [row, whole((8, width))],
        [sds((span, width), BF16), sds((8, width), F32)],
        mb=8, us=3, name="norm1",
    )


def dgrad_body(np_, s_ref, *refs):
    gs, (wq_ref, wk_ref, wv_ref), (own_ref, oth_ref) = refs[:np_], refs[np_ : np_ + 3], refs[np_ + 3 :]
    step = pl.program_id(0)
    half = pl.num_programs(0) // 2
    total = None
    for j, w_ref in enumerate((wq_ref, wk_ref, wv_ref)):
        left = jnp.concatenate(
            [g[:, at + j * 128 : at + (j + 1) * 128] for g in gs for at in range(0, g.shape[1], 384)], axis=1
        )
        part = dot_nt(left, w_ref[...])
        total = part if total is None else total + part

    @pl.when(step < half)
    def _():
        oth_ref[...] = total.astype(BF16)

    @pl.when(step >= half)
    def _():
        own_ref[...] = total


def dgrad_call(order, gs, qkv_weight):
    length = gs[0].shape[0]
    width = qkv_weight.shape[0]
    hw = width // 2
    blk = 256
    n = length // 2 // blk
    wspec = lambda j: pl.BlockSpec((width, hw), lambda i, s: (0, 2 * j + s[0]))
    return order.call(
        functools.partial(dgrad_body, len(gs)), [*gs, qkv_weight, qkv_weight, qkv_weight], (2 * n,),
        [pl.BlockSpec((blk, g.shape[1]), lambda i, s: ((i + n) % (2 * n), 0)) for g in gs]
        + [wspec(0), wspec(1), wspec(2)],
        [
            pl.BlockSpec((blk, width), lambda i, s: (jnp.maximum(i - n, 0), 0)),
            pl.BlockSpec((blk, width), lambda i, s: (jnp.minimum(i, n - 1), 0)),
        ],
        [sds((length // 2, width), F32), sds((length // 2, width), BF16)],
        mb=8, us=4, name="dgrad",
    )


class Grid:
    ORDERS = ((1, 2, 4, 8), (2, 1, 8, 4))

    def __init__(self, ndp):
        self.nz = ndp // 4
        self.index = lax.axis_index("dp")
        core = lax.axis_index("ctx")
        self.flip = lambda mask: [(i, i ^ mask) for i in range(ndp)]
        masks = [jnp.where(core == 0, a, b) for a, b in zip(*self.ORDERS)]
        bits = [jnp.where((self.index & m) > 0, 1, 0) for m in masks]
        self.place = jnp.stack([core, *bits, *masks, self.index // 4]).astype(jnp.int32)
        self.pairs = [
            [(2 * i + c, 2 * (i ^ self.ORDERS[c][step]) + c) for i in range(ndp) for c in range(2)] for step in range(4)
        ]


class Job:
    def __init__(self, pairs):
        self.pairs, self.step = pairs, 0

    def start(self, keep, send):
        self.keep = keep
        self.got = lax.ppermute(send, ("dp", "ctx"), self.pairs[self.step])
        self.step += 1

    def fold(self, order):
        shape = self.keep.shape
        if self.step > 1:
            shape = (2, shape[0] // 2) + shape[1:]
        away, stay = fold_call(order, self.step + 1, self.keep.reshape(shape), self.got.reshape(shape))
        self.start(stay, away)

    def parts(self):
        return [self.keep[0], self.got[0]]


def local_pair(
    tokens_in, cond_vec, positions, absorbed, cotangent, norm1_gain, qkv_weight, out_weight,
    norm2_gain, fc1_weight, fc1_bias, fc2_weight, fc2_bias, ada_weight, ada_bias, *, ndp,
):
    _, span, width = tokens_in.shape
    ff_width = fc1_weight.shape[1]
    hw = width // 2
    grid = Grid(ndp)
    nz = grid.nz
    order = Order(grid.place)
    swap = lambda v: lax.ppermute(v, "ctx", [(0, 1), (1, 0)])

    tok = tokens_in[0]
    tok_o = swap(tok)
    pos_o = swap(positions)

    normed_one, queries, keys, values, cos_t, sin_t, att_t, prob, inverse, mod, wtd = attend_call(
        order, tok, tok_o, cond_vec, ada_weight, ada_bias, norm1_gain, qkv_weight, positions, pos_o,
        cotangent[0], absorbed,
    )
    wtd_o = swap(wtd)
    att_o = swap(att_t)
    middle, branch, n2 = post_call(order, att_t, att_o, out_weight, hbm(tok), mod, norm2_gain)
    n2_o = swap(n2)
    hidden, g_pre, g_mlp, b1_sum, b2_sum = mlp_call(
        order, n2, n2_o, wtd, wtd_o, mod, fc1_weight, fc1_bias, fc2_weight
    )
    hidden_o = swap(hidden)
    fc1, fc2, rest, last = (Job(grid.pairs) for _ in range(4))
    fc1.start(*wgrad_call(order, n2, n2_o, g_pre, 384))
    pn_own, pn_oth = part_call(order, True, g_pre, fc1_weight)
    pn_got = swap(pn_oth)
    fc2.start(*wgrad2_call(order, hidden, hidden_o, g_mlp))
    g_mid, g_att, sums2 = norm2_call(
        order, pn_own, pn_got, middle, branch, wtd, mod, norm2_gain
    )
    g_att_o = swap(g_att)
    g_attn_t, *bufs = oproj_call(
        order, 3, out_weight, g_att, g_att_o, att_t, att_o
    )

    fc1.fold(order)

    def back(start, count, old, block, blocks):
        return attn_bwd(
            order, start, count, hbm(prob), inverse, g_attn_t, att_t, queries, keys, values, cos_t, sin_t,
            normed_one, old, block, blocks,
        )

    pairs = hw // 128
    g_a, *bufs = back(0, pairs - 1, bufs, 1, pairs)
    rest.start(*bufs)
    fc2.fold(order)
    fc1.fold(order)
    g_b, *bufs = back(pairs - 1, 1, None, 0, 1)
    last.start(*bufs)
    fc2.fold(order)
    fc1.fold(order)
    rest.fold(order)
    d_own, d_oth = dgrad_call(order, [g_a, g_b], qkv_weight)
    d_got = swap(d_oth)
    last.fold(order)
    fc2.fold(order)
    rest.fold(order)
    pm_own, pm_oth = part_call(order, False, hidden, fc2_weight)
    pm_got = swap(pm_oth)
    last.fold(order)
    rest.fold(order)
    input_grad, sums1 = norm1_call(order, d_own, d_got, tok, g_mid, mod, norm1_gain)
    mixed, sums3 = mix_call(order, pm_own, pm_got, middle, wtd, mod, fc2_bias)
    packet = pack_call(
        order, nz, sums1, sums2, sums3, b1_sum, b2_sum, norm1_gain, norm2_gain, mod, cond_vec
    )
    packet_o = swap(packet)
    last.fold(order)
    ff = sum_ff_call(order, fc1.parts(), fc2.parts())
    ff_o = swap(ff)
    cond_grad, *deals = deal_call(order, nz, packet, packet_o, ada_weight)
    deals = [deals[0]] + [lax.ppermute(deals[k], "dp", grid.flip(4 * k)) for k in range(1, nz)]
    att = sum_att_call(order, rest.parts(), last.parts())
    att_o2 = swap(att)
    fc1_grad, fc2_grad = place_ff_call(order, ff, ff_o, hw)
    deals = jnp.concatenate(deals, 0)
    packs = [deals] + [lax.ppermute(deals, "dp", grid.flip(mask)) for mask in (1, 2, 3)]
    out_grad, qkv_grad = place_att_call(order, att, att_o2, width)
    ada_part, sums = last_call(order, packs)

    na, nb, nc = 6 * width // ndp, width // ndp, ff_width // ndp
    inner = lax.rem(grid.index, 4)
    take = lambda v, start, n: lax.dynamic_slice_in_dim(v, start, n, v.ndim - 1)
    ada_grad = take(ada_part, inner * na, na)
    ada_bias_grad = take(sums[0:3].reshape(-1), inner * na, na)
    fc1_bias_grad = take(sums[3:5].reshape(-1), inner * nc, nc)
    norm1_grad = take(sums[5:7].reshape(-1), grid.index * nb, nb)
    norm2_grad = take(sums[7:9].reshape(-1), grid.index * nb, nb)
    fc2_bias_grad = take(sums[9:11].reshape(-1), grid.index * nb, nb)
    return (
        mixed[None], input_grad[None], cond_grad, norm1_grad, qkv_grad, out_grad, norm2_grad,
        fc1_grad, fc1_bias_grad, fc2_grad, fc2_bias_grad, ada_grad, ada_bias_grad,
    )


def layer_norm(stream):
    row_mean = jnp.mean(stream, axis=-1, keepdims=True)
    centred = stream - row_mean
    variance = jnp.mean(centred * centred, axis=-1, keepdims=True)
    return centred * lax.rsqrt(variance + EPS)


def pre_norm(stream, norm_gain, shift_vec, scale_vec):
    return layer_norm(stream) * norm_gain * (1.0 + scale_vec[:, None, :]) + shift_vec[:, None, :]


def gelu_tanh(stream):
    return jax.nn.gelu(stream, approximate=True)


def block_rows(row_count):
    size_now = row_count
    while size_now > 512 and size_now % 2 == 0:
        size_now = size_now // 2
    return size_now


def rotary_tables(positions):
    inv_freq = 10000.0 ** (-jnp.arange(0, HEAD_DIM, 2).astype(jnp.float32) / HEAD_DIM)
    angles = positions.astype(jnp.float32)[..., None] * inv_freq
    cos_table = jnp.concatenate([jnp.cos(angles), jnp.cos(angles)], axis=-1)[..., None, :]
    sin_table = jnp.concatenate([jnp.sin(angles), jnp.sin(angles)], axis=-1)[..., None, :]
    return (cos_table, sin_table)


def rotate_pos(stream, cos_table, sin_table):
    half_dim = stream.shape[-1] // 2
    turned = jnp.concatenate([-stream[..., half_dim:], stream[..., :half_dim]], axis=-1)
    return stream * cos_table + turned * sin_table


def over_blocks(step_fn, fold_state, pieces):
    row_count = pieces[0].shape[1]
    size_now = block_rows(row_count)

    def one_turn(turn_idx, inner_state):
        part_list = tuple(
            (
                lax.dynamic_slice_in_dim(member, turn_idx * size_now, size_now, 1)
                for member in pieces
            )
        )
        return step_fn(inner_state, part_list, turn_idx * size_now)

    return lax.fori_loop(0, row_count // size_now, one_turn, fold_state)


def score_grads(query_blk, key_blk, value_blk, grad_blk, top_blk, total_blk, delta_blk):
    scores = (
        jnp.einsum("sqhd,skhd->sqhk", query_blk, key_blk, preferred_element_type=jnp.float32)
        * SCORE_SCALE
    )
    probability = jnp.exp(scores - top_blk[..., None]) / total_blk[..., None]
    grad_prob = jnp.einsum(
        "sqhd,skhd->sqhk", grad_blk, value_blk, preferred_element_type=jnp.float32
    )
    grad_scores = (probability * (grad_prob - delta_blk[..., None])).astype(jnp.bfloat16)
    return (probability, grad_scores)


def local_any(
    tokens_in,
    cond_vec,
    positions,
    absorbed,
    cotangent,
    norm1_gain,
    qkv_weight,
    out_weight,
    norm2_gain,
    fc1_weight,
    fc1_bias,
    fc2_weight,
    fc2_bias,
    ada_weight,
    ada_bias,
):
    seqs_here, span_len, model_width = tokens_in.shape
    head_shape = (seqs_here, span_len, HEADS, HEAD_DIM)
    stream = tokens_in.astype(jnp.float32)
    modulation = jnp.dot(
        cond_vec, ada_weight, preferred_element_type=jnp.float32
    ) + ada_bias.astype(jnp.float32)
    shift_one, scale_one, gate_one, shift_two, scale_two, gate_two = jnp.split(
        modulation, 6, axis=-1
    )
    gain_one = norm1_gain.astype(jnp.float32)
    gain_two = norm2_gain.astype(jnp.float32)
    normed_f, pull_one = jax.vjp(pre_norm, stream, gain_one, shift_one, scale_one)
    normed_one = normed_f.astype(jnp.bfloat16)
    projected = jnp.dot(normed_one, qkv_weight, preferred_element_type=jnp.float32)
    cos_table, sin_table = rotary_tables(positions)
    turned_pair, pull_rot = jax.vjp(
        lambda query_pre, key_pre: (
            rotate_pos(query_pre, cos_table, sin_table),
            rotate_pos(key_pre, cos_table, sin_table),
        ),
        projected[..., :model_width].reshape(head_shape),
        projected[..., model_width : 2 * model_width].reshape(head_shape),
    )
    queries = turned_pair[0].astype(jnp.bfloat16)
    key_loc = turned_pair[1].astype(jnp.bfloat16).reshape(seqs_here, span_len, model_width)
    value_loc = projected[..., 2 * model_width :].astype(jnp.bfloat16)

    def forward_step(fold_state, part_list, offset):
        run_max, run_sum, run_acc = fold_state
        key_blk = part_list[0].reshape(seqs_here, -1, HEADS, HEAD_DIM)
        value_blk = part_list[1].reshape(seqs_here, -1, HEADS, HEAD_DIM)
        scores = (
            jnp.einsum("sqhd,skhd->sqhk", queries, key_blk, preferred_element_type=jnp.float32)
            * SCORE_SCALE
        )
        new_max = jnp.maximum(run_max, jnp.max(scores, axis=-1))
        raised = jnp.exp(scores - new_max[..., None])
        shrink = jnp.exp(run_max - new_max)
        run_sum = run_sum * shrink + jnp.sum(raised, axis=-1)
        run_acc = run_acc * shrink[..., None] + jnp.einsum(
            "sqhk,skhd->sqhd",
            raised.astype(jnp.bfloat16),
            value_blk,
            preferred_element_type=jnp.float32,
        )
        return (new_max, run_sum, run_acc)

    empty_state = (
        jnp.full((seqs_here, span_len, HEADS), NEG_START, jnp.float32),
        jnp.zeros((seqs_here, span_len, HEADS), jnp.float32),
        jnp.zeros(head_shape, jnp.float32),
    )
    final_max, final_sum, final_acc = over_blocks(
        forward_step,
        empty_state,
        (
            lax.all_gather(key_loc, "ctx", axis=1, tiled=True),
            lax.all_gather(value_loc, "ctx", axis=1, tiled=True),
        ),
    )
    attn_out = final_acc / final_sum[..., None]
    attended = attn_out.reshape(seqs_here, span_len, model_width).astype(jnp.bfloat16)
    branch_att = jnp.dot(attended, out_weight, preferred_element_type=jnp.float32)
    middle = stream + gate_one[:, None, :] * branch_att
    normed_f2, pull_two = jax.vjp(pre_norm, middle, gain_two, shift_two, scale_two)
    normed_two = normed_f2.astype(jnp.bfloat16)
    hidden_pre = jnp.dot(
        normed_two, fc1_weight, preferred_element_type=jnp.float32
    ) + fc1_bias.astype(jnp.float32)
    hidden_f, pull_gelu = jax.vjp(gelu_tanh, hidden_pre)
    hidden = hidden_f.astype(jnp.bfloat16)
    branch_mlp = jnp.dot(hidden, fc2_weight, preferred_element_type=jnp.float32) + fc2_bias.astype(
        jnp.float32
    )
    mixed = (middle + gate_two[:, None, :] * branch_mlp).astype(jnp.bfloat16)
    weighted = cotangent.astype(jnp.float32) * absorbed.astype(jnp.float32)[..., None]
    grad_gate_two = jnp.sum(weighted * branch_mlp, axis=1)
    grad_mlp = (weighted * gate_two[:, None, :]).astype(jnp.bfloat16)
    grad_fc2b = jnp.sum(grad_mlp.astype(jnp.float32), axis=(0, 1))
    grad_fc2 = jnp.einsum("scf,scd->fd", hidden, grad_mlp, preferred_element_type=jnp.float32)
    grad_hidden = jnp.einsum(
        "scd,fd->scf", grad_mlp, fc2_weight, preferred_element_type=jnp.float32
    )
    grad_pre = pull_gelu(grad_hidden)[0].astype(jnp.bfloat16)
    grad_fc1b = jnp.sum(grad_pre.astype(jnp.float32), axis=(0, 1))
    grad_fc1 = jnp.einsum("scd,scf->df", normed_two, grad_pre, preferred_element_type=jnp.float32)
    grad_normed_two = jnp.einsum(
        "scf,df->scd", grad_pre, fc1_weight, preferred_element_type=jnp.float32
    )
    grad_mid_part, grad_gain_two, grad_shift_two, grad_scale_two = pull_two(grad_normed_two)
    grad_middle = weighted + grad_mid_part
    grad_gate_one = jnp.sum(grad_middle * branch_att, axis=1)
    grad_att = (grad_middle * gate_one[:, None, :]).astype(jnp.bfloat16)
    grad_out = jnp.einsum("scd,sce->de", attended, grad_att, preferred_element_type=jnp.float32)
    grad_attended = (
        jnp.einsum("sce,de->scd", grad_att, out_weight, preferred_element_type=jnp.float32)
        .astype(jnp.bfloat16)
        .reshape(head_shape)
    )
    row_delta = jnp.sum(grad_attended.astype(jnp.float32) * attn_out, axis=-1)

    def query_only_step(fold_state, part_list, offset):
        piece_len = part_list[0].shape[1]
        key_blk = part_list[0].reshape(seqs_here, piece_len, HEADS, HEAD_DIM)
        value_blk = part_list[1].reshape(seqs_here, piece_len, HEADS, HEAD_DIM)
        probability, grad_scores = score_grads(
            queries, key_blk, value_blk, grad_attended, final_max, final_sum, row_delta
        )
        return (
            fold_state
            + jnp.einsum(
                "sqhk,skhd->sqhd", grad_scores, key_blk, preferred_element_type=jnp.float32
            )
            * SCORE_SCALE
        )

    start_state = jnp.zeros(head_shape, jnp.float32)
    back_state = over_blocks(
        query_only_step,
        start_state,
        (
            lax.all_gather(key_loc, "ctx", axis=1, tiled=True),
            lax.all_gather(value_loc, "ctx", axis=1, tiled=True),
        ),
    )
    key_heads = key_loc.reshape(head_shape)
    value_heads = value_loc.reshape(head_shape)

    def local_key_step(fold_state, part_list, offset):
        grad_key_loc, grad_value_loc = fold_state
        query_blk = part_list[0].astype(jnp.bfloat16)
        grad_blk = part_list[1].astype(jnp.bfloat16)
        probability, grad_scores = score_grads(
            query_blk, key_heads, value_heads, grad_blk, part_list[2], part_list[3], part_list[4]
        )
        grad_value_loc = grad_value_loc + jnp.einsum(
            "sqhk,sqhd->skhd",
            probability.astype(jnp.bfloat16),
            grad_blk,
            preferred_element_type=jnp.float32,
        )
        grad_key_loc = (
            grad_key_loc
            + jnp.einsum(
                "sqhk,sqhd->skhd", grad_scores, query_blk, preferred_element_type=jnp.float32
            )
            * SCORE_SCALE
        )
        return (grad_key_loc, grad_value_loc)

    key_start = (jnp.zeros(head_shape, jnp.float32), jnp.zeros(head_shape, jnp.float32))
    grad_key_h, grad_value_h = over_blocks(
        local_key_step,
        key_start,
        (
            lax.all_gather(queries.astype(jnp.float32), "ctx", axis=1, tiled=True),
            lax.all_gather(grad_attended.astype(jnp.float32), "ctx", axis=1, tiled=True),
            lax.all_gather(final_max, "ctx", axis=1, tiled=True),
            lax.all_gather(final_sum, "ctx", axis=1, tiled=True),
            lax.all_gather(row_delta, "ctx", axis=1, tiled=True),
        ),
    )
    grad_key_loc = grad_key_h.reshape(seqs_here, span_len, model_width)
    grad_value_loc = grad_value_h.reshape(seqs_here, span_len, model_width)
    grad_query_pre, grad_key_pre = pull_rot((back_state, grad_key_loc.reshape(head_shape)))
    grad_proj = jnp.concatenate(
        [
            grad_query_pre.reshape(seqs_here, span_len, model_width),
            grad_key_pre.reshape(seqs_here, span_len, model_width),
            grad_value_loc,
        ],
        axis=-1,
    ).astype(jnp.bfloat16)
    grad_qkv = jnp.einsum("scd,sce->de", normed_one, grad_proj, preferred_element_type=jnp.float32)
    grad_normed_one = jnp.einsum(
        "sce,de->scd", grad_proj, qkv_weight, preferred_element_type=jnp.float32
    )
    grad_in_part, grad_gain_one, grad_shift_one, grad_scale_one = pull_one(grad_normed_one)
    input_grad = (grad_middle + grad_in_part).astype(jnp.bfloat16)
    partial_mod = jnp.concatenate(
        [
            grad_shift_one,
            grad_scale_one,
            grad_gate_one,
            grad_shift_two,
            grad_scale_two,
            grad_gate_two,
        ],
        axis=-1,
    )
    grad_mod = lax.psum(partial_mod, "ctx")
    cond_grad = jnp.einsum(
        "se,ce->sc",
        grad_mod,
        ada_weight.astype(jnp.float32),
        precision=lax.Precision.HIGHEST,
        preferred_element_type=jnp.float32,
    )
    first_cycle = (lax.axis_index("ctx") == 0).astype(jnp.float32)
    grad_ada = (
        jnp.einsum(
            "sc,se->ce",
            cond_vec.astype(jnp.float32),
            grad_mod,
            precision=lax.Precision.HIGHEST,
            preferred_element_type=jnp.float32,
        )
        * first_cycle
    )
    grad_adab = jnp.sum(grad_mod, axis=0) * first_cycle
    (
        part_g1,
        part_qkv,
        part_out,
        part_g2,
        part_fc1,
        part_fc1b,
        part_fc2,
        part_fc2b,
        part_ada,
        part_adab,
    ) = (
        lax.psum_scatter(grad_gain_one, "dp", scatter_dimension=0, tiled=True),
        lax.psum_scatter(grad_qkv, "dp", scatter_dimension=0, tiled=True),
        lax.psum_scatter(grad_out, "dp", scatter_dimension=0, tiled=True),
        lax.psum_scatter(grad_gain_two, "dp", scatter_dimension=0, tiled=True),
        lax.psum_scatter(grad_fc1, "dp", scatter_dimension=0, tiled=True),
        lax.psum_scatter(grad_fc1b, "dp", scatter_dimension=0, tiled=True),
        lax.psum_scatter(grad_fc2, "dp", scatter_dimension=0, tiled=True),
        lax.psum_scatter(grad_fc2b, "dp", scatter_dimension=0, tiled=True),
        lax.psum_scatter(grad_ada, "dp", scatter_dimension=1, tiled=True),
        lax.psum_scatter(grad_adab, "dp", scatter_dimension=0, tiled=True),
    )
    summed = lax.psum(
        (
            part_g1,
            part_qkv,
            part_out,
            part_g2,
            part_fc1,
            part_fc1b,
            part_fc2,
            part_fc2b,
            part_ada,
            part_adab,
        ),
        "ctx",
    )
    return (mixed, input_grad, cond_grad) + tuple(summed)


def local(*args, ndp, nctx):
    seqs, span, _ = args[0].shape
    if nctx == 2 and seqs == 1 and ndp == 16 and span == 512:
        return local_pair(*args, ndp=ndp)
    return local_any(*args)


def solution(mesh):
    in_specs = (
        P("dp", "ctx", None),
        P("dp", None),
        P("dp", "ctx"),
        P("dp", "ctx"),
        P("dp", "ctx", None),
        P(),
        P(),
        P(),
        P(),
        P(),
        P(),
        P(),
        P(),
        P(),
        P(),
    )
    out_specs = (
        P("dp", "ctx", None),
        P("dp", "ctx", None),
        P("dp", None),
        P("dp"),
        P("dp", None),
        P("dp", None),
        P("dp"),
        P("dp", None),
        P("dp"),
        P("dp", None),
        P("dp"),
        P(None, "dp"),
        P("dp"),
    )
    step = functools.partial(local, ndp=mesh.shape["dp"], nctx=mesh.shape["ctx"])
    return jax.shard_map(step, mesh=mesh, in_specs=in_specs, out_specs=out_specs, check_vma=False)
```

```python
import functools

import jax
import jax.numpy as jnp
import numpy as np
from jax import lax
from jax.experimental import pallas as pl
from jax.experimental.pallas import tpu as pltpu
from jax.sharding import PartitionSpec as P

HEADS = 12
HEAD_DIM = 64
EPS = 1e-05
SCORE_SCALE = 0.125
NEG_START = -1e30
F32, BF16 = jnp.float32, jnp.bfloat16
COST = 2e8
MLP_COLS = 1536
BWD_BLK = 1024


def dot(a, b):
    return jnp.dot(a, b, preferred_element_type=F32)


def dot_tn(a, b):
    return lax.dot_general(a, b, (((0,), (0,)), ((), ())), preferred_element_type=F32)


def dot_nt(a, b):
    return lax.dot_general(a, b, (((1,), (1,)), ((), ())), preferred_element_type=F32)


def sds(shape, dtype):
    return jax.ShapeDtypeStruct(shape, dtype)


def hbm(x):
    return pltpu.with_memory_space_constraint(x, pltpu.HBM)


class Order:
    def __init__(self, place):
        self.place, self.token = place, None

    def call(
        self, body, args, grid, in_specs, out_specs, out_shape, scratch=(), mb=32, us=1.0, aliases=None, after=(),
        name=None,
    ):
        after = list(after) + ([] if self.token is None else [self.token])
        extra, n_in, n_out = len(after), 1 + len(args), len(out_shape)

        def inner(*refs):
            outs = refs[n_in + extra :]
            body(*refs[:n_in], *outs[:n_out], *outs[n_out + 1 :])

        *outs, self.token = pl.pallas_call(
            inner,
            grid_spec=pltpu.PrefetchScalarGridSpec(
                num_scalar_prefetch=1,
                grid=grid,
                in_specs=list(in_specs) + [ANY] * extra,
                out_specs=list(out_specs) + [ANY],
                scratch_shapes=list(scratch),
            ),
            out_shape=list(out_shape) + [sds((8, 128), F32)],
            input_output_aliases=aliases or {},
            compiler_params=pltpu.CompilerParams(vmem_limit_bytes=mb << 20),
            cost_estimate=pl.CostEstimate(flops=int(us * COST), bytes_accessed=1 << 16, transcendentals=0),
            name=name,
        )(self.place, *args, *after)
        return outs


ANY = pl.BlockSpec(memory_space=pl.ANY)


def whole(shape):
    return pl.BlockSpec(shape, lambda *a: (0,) * len(shape))


def layer_stats(stream):
    row_mean = jnp.mean(stream, axis=-1, keepdims=True)
    centred = stream - row_mean
    variance = jnp.mean(centred * centred, axis=-1, keepdims=True)
    inv = lax.rsqrt(variance + EPS)
    return centred * inv, inv


def swap_lanes(x):
    lane = lax.broadcasted_iota(jnp.int32, x.shape, 1) % HEAD_DIM
    half = HEAD_DIM // 2
    return jnp.where(lane < half, pltpu.roll(x, 128 - half, 1), pltpu.roll(x, half, 1))


def mask_half(value, head):
    lane = lax.broadcasted_iota(jnp.int32, value.shape, 1)
    keep = (lane < HEAD_DIM) if head == 0 else (lane >= HEAD_DIM)
    return jnp.where(keep, value, jnp.zeros_like(value))


def attend_body(
    s_ref, ta_ref, tb_ref, cond_ref, ada_ref, adab_ref, gain_ref, wq_ref, wk_ref, wv_ref, pa_ref, pb_ref, freq_ref,
    cot_ref, abs_ref,
    n1_out, q_out, k_out, v_out, cost_ref, sint_ref,
    out_ref, prob_ref, inv_ref, mod_ref, wtd_ref, scores_ref, top_ref, vt_ref, n1_ref, q_ref, k_ref, v_ref,
):
    pair, step = pl.program_id(0), pl.program_id(1)
    span, width = ta_ref.shape
    blk = out_ref.shape[1]

    @pl.when((pair == 0) & (step == 0))
    def _():
        kept = jnp.broadcast_to(abs_ref[...].astype(F32), (128, span)).T[:, 0:1]
        wtd_ref[...] = (cot_ref[...].astype(F32) * kept).astype(BF16)
        cond = jnp.broadcast_to(cond_ref[...].astype(F32), (16, cond_ref.shape[1])).astype(BF16)
        mod_ref[...] = dot(cond, ada_ref[...])[:8] + adab_ref[...].astype(F32)[None, :]
        shift, scale = mod_ref[0:1, 0:width], mod_ref[0:1, width : 2 * width]
        gain = gain_ref[...].astype(F32)[None, :] * (1.0 + scale)
        for half, (t_ref, p_ref) in enumerate(((ta_ref, pa_ref), (tb_ref, pb_ref))):
            rows = slice(half * span, (half + 1) * span)
            angles = freq_ref[...] * p_ref[...].astype(F32)
            cos_h, sin_h = jnp.cos(angles), jnp.sin(angles)
            cos_t, sin_t = rotation(cos_h, sin_h)
            cost_ref[:, rows] = cos_h
            sint_ref[:, rows] = sin_h
            cos_n, sin_n = cos_t.T, sin_t.T
            a_one, _ = layer_stats(t_ref[...].astype(F32))
            normed = (a_one * gain + shift).astype(BF16)
            n1_ref[rows, :] = a_one.astype(BF16)
            q_pre = dot(normed, wq_ref[...])
            k_pre = dot(normed, wk_ref[...])
            v_ref[rows, :] = dot(normed, wv_ref[...]).astype(BF16)
            for p in range(q_pre.shape[1] // 128):
                at = slice(p * 128, (p + 1) * 128)
                part = q_pre[:, at]
                q_ref[rows, at] = (SCORE_SCALE * (part * cos_n + swap_lanes(part) * sin_n)).astype(BF16)
                part = k_pre[:, at]
                k_ref[rows, at] = (part * cos_n + swap_lanes(part) * sin_n).astype(BF16)

    pairs, blocks = pl.num_programs(0), pl.num_programs(1)
    lanes = lambda p: pl.ds(pl.multiple_of(p * 128, 128), 128)
    piece = jnp.minimum(pair * blocks + step, n1_ref.shape[0] // n1_out.shape[0] - 1)
    n1_out[...] = n1_ref[pl.ds(pl.multiple_of(piece * n1_out.shape[0], 128), n1_out.shape[0]), :]
    length = k_ref.shape[0]
    cut = 512

    def queries(p, i, head):
        return mask_half(q_ref[pl.ds(pl.multiple_of(i * blk, blk), blk), lanes(p)], head)

    def top_rows(scores):
        return jnp.max(scores.reshape(scores.shape[0] // 8, 8, blk), axis=0)

    @pl.when((pair == 0) & (step == 0))
    def _():
        vt_ref[...] = v_ref[...].T
        q_0 = queries(0, 0, 0)
        top = None
        for at in range(0, length, cut):
            scores = dot_nt(k_ref[at : at + cut, 0:128], q_0)
            scores_ref[0, at : at + cut] = scores
            top = top_rows(scores) if top is None else jnp.maximum(top, top_rows(scores))
        top_ref[0] = top

    @pl.when(step == 0)
    def _():
        q_out[...] = q_ref[:, lanes(pair)]
        k_out[...] = k_ref[:, lanes(pair)]
        v_out[...] = v_ref[:, lanes(pair)]

    for head in (0, 1):
        if head == 0:
            next_pair, next_step = pair, step
        else:
            wrap = step == blocks - 1
            next_step = jnp.where(wrap, 0, step + 1)
            next_pair = jnp.minimum(jnp.where(wrap, pair + 1, pair), pairs - 1)
        q_next = queries(next_pair, next_step, 1 - head)
        top = jnp.max(top_ref[head], axis=0, keepdims=True)
        rows = pl.ds(pl.multiple_of(pair * 128 + head * HEAD_DIM, HEAD_DIM), HEAD_DIM)
        next_top = sums = part = None
        for at in range(0, length, cut):
            here = slice(at, at + cut)
            scores = dot_nt(k_ref[here, lanes(next_pair)], q_next)
            scores_ref[1 - head, here] = scores
            new_top = top_rows(scores)
            raised = jnp.exp(scores_ref[head, here] - top)
            new_sums = jnp.sum(raised.reshape(cut // 8, 8, blk), axis=0)
            prob = raised.astype(BF16)
            prob_ref[head, here] = prob
            new_part = dot(vt_ref[rows, here], prob)
            next_top = new_top if next_top is None else jnp.maximum(next_top, new_top)
            sums = new_sums if sums is None else sums + new_sums
            part = new_part if part is None else part + new_part
        top_ref[1 - head] = next_top
        inverse = 1.0 / jnp.sum(sums, axis=0, keepdims=True)
        inv_ref[0, head : head + 1, :] = inverse
        out_ref[head * HEAD_DIM : (head + 1) * HEAD_DIM, :] = (part * inverse).astype(BF16)


def attend_call(order, tok, tok_o, cond, ada, adab, gain, qkv_weight, pos, pos_o, cot, absorbed):
    span, width = tok.shape
    length, hw = 2 * span, width // 2
    pairs, blk = hw // 128, 512
    freq = np.power(10000.0, -np.arange(0, HEAD_DIM, 2) / HEAD_DIM).astype(np.float32)[:, None]
    wspec = lambda j: pl.BlockSpec((width, hw), lambda p, i, s: (0, 2 * j + s[0]))
    col = pl.BlockSpec((length, 128), lambda p, i, s: (0, p))
    return order.call(
        attend_body,
        [hbm(tok), tok_o, hbm(cond), hbm(ada), hbm(adab), hbm(gain), *[hbm(qkv_weight)] * 3, hbm(pos), pos_o, hbm(jnp.asarray(freq)), hbm(cot), hbm(absorbed)],
        (pairs, length // blk),
        [whole(tok.shape), whole(tok.shape), whole(cond.shape), whole(ada.shape), whole(adab.shape), whole(gain.shape), wspec(0), wspec(1), wspec(2),
         whole(pos.shape), whole(pos.shape), whole(freq.shape), whole(cot.shape), whole(absorbed.shape)],
        [pl.BlockSpec((length // 4, width), lambda p, i, s: (jnp.minimum(p * (length // blk) + i, 3), 0)),
         col, col, col, whole((HEAD_DIM // 2, length)), whole((HEAD_DIM // 2, length)),
         pl.BlockSpec((128, blk), lambda p, i, s: (p, i)),
         pl.BlockSpec((2, length, blk), lambda p, i, s: (p, 0, i)),
         pl.BlockSpec((1, 8, blk), lambda p, i, s: (p, 0, i)), whole((8, ada.shape[1])), whole(tok.shape)],
        [sds((length, width), BF16)] + [sds((length, hw), BF16)] * 3
        + [sds((HEAD_DIM // 2, length), F32)] * 2
        + [sds((hw, length), BF16), pltpu.HBM((2 * pairs, length, length), BF16), sds((pairs, 8, length), F32),
           sds((8, ada.shape[1]), F32), sds(tok.shape, BF16)],
        scratch=[pltpu.VMEM((2, length, blk), F32), pltpu.VMEM((2, 8, blk), F32), pltpu.VMEM((hw, length), BF16),
                 pltpu.VMEM((length, width), BF16)] + [pltpu.VMEM((length, hw), BF16)] * 3,
        mb=40, us=20, name="attend",
    )


def swap_rows(x):
    half = HEAD_DIM // 2
    return jnp.concatenate([x[half * j : half * (j + 1)] for j in (1, 0, 3, 2)], axis=0)


def rotation(cos_h, sin_h):
    return jnp.concatenate([cos_h] * 4, axis=0), jnp.concatenate([-sin_h, sin_h, -sin_h, sin_h], axis=0)


def attn_bwd_body(
    r, s_ref, prob_ref, inv_ref, gt_ref, out_ref, q_ref, k_ref, v_ref, cost_ref, sint_ref, a_ref,
    mod_ref, gain_ref, wq_ref, wk_ref, wv_ref,
    g_ref, sum_ref, keep_ref, send_ref, vm_ref, kt_ref, dk_acc, dv_acc, acc_ref,
):
    step = pl.program_id(1)
    blk = q_ref.shape[0]

    @pl.when(step == 0)
    def _():
        values = v_ref[...]
        for head in (0, 1):
            vm_ref[head] = mask_half(values, head)
        kt_ref[...] = k_ref[...].T

    queries = q_ref[...]
    grad_t = gt_ref[...].astype(jnp.float32)
    row_id = lax.broadcasted_iota(jnp.int32, (128, blk), 0)
    inverse = jnp.where(row_id < HEAD_DIM, inv_ref[0, 0:1, :], inv_ref[0, 1:2, :])
    grad_t = grad_t * inverse
    product = grad_t * out_ref[...].astype(jnp.float32)
    grad_b = grad_t.astype(jnp.bfloat16)
    dk_new = None
    dq_parts = []
    for head in (0, 1):
        rows = slice(head * HEAD_DIM, (head + 1) * HEAD_DIM)
        delta = jnp.sum(product[rows], axis=0, keepdims=True)
        keep = (row_id < HEAD_DIM) if head == 0 else (row_id >= HEAD_DIM)
        grad_m = jnp.where(keep, grad_b, jnp.zeros_like(grad_b))
        grad_p = jnp.dot(vm_ref[head], grad_b, preferred_element_type=jnp.float32)
        prob = prob_ref[head]
        grad_s = (prob.astype(jnp.float32) * (grad_p - delta)).astype(jnp.bfloat16)
        dv_h = dot_nt(prob, grad_m)
        dk_h = dot(grad_s, mask_half(queries, head))
        if dk_new is None:
            dk_new, dv_new = dk_h, dv_h
        else:
            dk_new, dv_new = dk_new + dk_h, dv_new + dv_h
        dq_parts.append(dot(kt_ref[rows, :], grad_s) * SCORE_SCALE)
    dq_t = jnp.concatenate(dq_parts, axis=0)
    here = pl.ds(pl.multiple_of(step * blk, blk), blk)
    cos_t, sin_t = rotation(cost_ref[:, here], sint_ref[:, here])
    dq_t = dq_t * cos_t - swap_rows(dq_t) * sin_t
    g_ref[here, 0:128] = dq_t.T.astype(jnp.bfloat16)

    @pl.when(step == 0)
    def _():
        dk_acc[...] = dk_new
        dv_acc[...] = dv_new

    @pl.when(step > 0)
    def _():
        dk_acc[...] += dk_new
        dv_acc[...] += dv_new

    @pl.when(step == pl.num_programs(1) - 1)
    def _():
        dk = dk_acc[...]
        cos_t, sin_t = rotation(cost_ref[...], sint_ref[...])
        g_ref[:, 128:256] = (dk * cos_t.T - swap_lanes(dk) * sin_t.T).astype(jnp.bfloat16)
        g_ref[:, 256:384] = dv_acc[...].astype(jnp.bfloat16)
        grads = g_ref[...]
        product = dot_tn(a_ref[...], grads)
        width = a_ref.shape[1]
        column = lambda row: jnp.broadcast_to(row, (128, width)).T
        gain = column(gain_ref[...].astype(F32)[None, :] * (1.0 + mod_ref[0:1, width : 2 * width]))
        shift = column(mod_ref[0:1, 0:width])
        tokens = jnp.sum(grads.astype(F32), axis=0, keepdims=True)
        high = tokens.astype(BF16)
        low = (tokens - high.astype(F32)).astype(BF16)
        row_id = lax.broadcasted_iota(jnp.int32, (16, 384), 0)
        terms = jnp.where(row_id == 0, high, jnp.where(row_id == 1, low, jnp.zeros_like(high)))
        against = None
        for j, w_ref in enumerate((wq_ref, wk_ref, wv_ref)):
            at = slice(j * 128, (j + 1) * 128)
            part = product[:, at]
            acc_ref[:, at] = (part * gain + shift * tokens[:, at]).astype(BF16)
            weights = w_ref[...]
            scaled = part * weights.astype(F32)
            shifted = dot_nt(terms[:, at], weights)
            against = scaled if against is None else against + scaled
            shifts = shifted if j == 0 else shifts + shifted
        new = jnp.concatenate(
            [jnp.sum(shifts, axis=0, keepdims=True), jnp.sum(against.T, axis=0, keepdims=True)], axis=0
        )

        @pl.when(pl.program_id(0) == 0)
        def _():
            sum_ref[0:2, :] = new

        @pl.when(pl.program_id(0) > 0)
        def _():
            sum_ref[0:2, :] += new

        store_parts(s_ref, acc_ref, r, keep_ref, send_ref)


def attn_bwd(
    order, start, count, prob, inverse, grad_t, out_t, queries, keys, values, cos_t, sin_t, a_one,
    mod, gain, qkv_weight, old, block, blocks,
):
    length = keys.shape[0]
    width = a_one.shape[1]
    hw = width // 2
    wspec = lambda j: pl.BlockSpec((width, 128), lambda p, i, s: (0, (2 * j + s[0]) * (hw // 128) + p + start))
    blk = BWD_BLK
    r = width // 16
    col = pl.BlockSpec((length, 128), lambda p, i, s: (0, p + start))
    rowt = pl.BlockSpec((128, blk), lambda p, i, s: (p + start, i))
    out = pl.BlockSpec((2, 4, r, 384), lambda p, i, s: (0, 0, 0, p + block))
    args = [prob, inverse, grad_t, out_t, queries, keys, values, cos_t, sin_t, a_one, mod, gain, qkv_weight, qkv_weight, qkv_weight]
    aliases = {}
    after = []
    if old is not None:
        aliases = {1 + len(args) + j: 2 + j for j in range(2)}
        after = list(old)
    return order.call(
        functools.partial(attn_bwd_body, r), args, (count, length // blk),
        [
            pl.BlockSpec((2, length, blk), lambda p, i, s: (p + start, 0, i)),
            pl.BlockSpec((1, 8, blk), lambda p, i, s: (p + start, 0, i)),
            rowt, rowt,
            pl.BlockSpec((blk, 128), lambda p, i, s: (i, p + start)),
            col, col, whole(cos_t.shape), whole(cos_t.shape), whole(a_one.shape),
            whole(mod.shape), whole(gain.shape), wspec(0), wspec(1), wspec(2),
        ],
        [pl.BlockSpec((length, 384), lambda p, i, s: (0, p)), whole((8, width))] + [out] * 2,
        [sds((length, 384 * count), BF16), sds((8, width), F32)] + [sds((2, 4, r, 384 * blocks), BF16)] * 2,
        scratch=[
            pltpu.VMEM((2, length, 128), BF16),
            pltpu.VMEM((128, length), BF16),
            pltpu.VMEM((length, 128), F32),
            pltpu.VMEM((length, 128), F32),
            pltpu.VMEM((width, 384), BF16),
        ],
        mb=36, us=8.0 * count, aliases=aliases, after=after, name="attn_bwd",
    )


def mix_body(s_ref, own_ref, got_ref, mid_ref, mod_ref, bias_ref, out_ref):
    width = mid_ref.shape[1]
    branch = own_ref[...] + got_ref[...].astype(F32) + bias_ref[...].astype(F32)[None, :]
    out_ref[...] = (mid_ref[...] + mod_ref[0:1, 5 * width : 6 * width] * branch).astype(BF16)


def mix_call(order, own, got, mid, mod, bias):
    span, width = mid.shape
    blk = 256
    row = pl.BlockSpec((blk, width), lambda i, s: (i, 0))
    return order.call(
        mix_body, [own, got, mid, mod, bias], (span // blk,),
        [row] * 3 + [whole(mod.shape), whole(bias.shape)],
        [row], [sds((span, width), BF16)], mb=12, us=2.5, name="mix",
    )[0]


def post_body(s_ref, att_ref, oth_ref, wm_ref, wo_ref, tok_ref, mod_ref, gain_ref, mid_ref, br_ref, n2_ref):
    width = tok_ref.shape[1]
    branch = dot_tn(att_ref[...], wm_ref[...]) + dot_tn(oth_ref[...], wo_ref[...])
    br_ref[...] = branch
    middle = tok_ref[...].astype(F32) + mod_ref[0:1, 2 * width : 3 * width] * branch
    mid_ref[...] = middle
    a_two, _ = layer_stats(middle)
    scale = mod_ref[0:1, 4 * width : 5 * width]
    n2_ref[...] = (
        a_two * (gain_ref[...].astype(F32)[None, :] * (1.0 + scale)) + mod_ref[0:1, 3 * width : 4 * width]
    ).astype(BF16)


def post_call(order, att_t, att_o, out_weight, tok, mod, gain):
    span, width = tok.shape
    hw = width // 2
    blk = 512
    n = span // blk
    row = pl.BlockSpec((blk, width), lambda i, s: (i, 0))
    return order.call(
        post_body, [att_t, att_o, out_weight, out_weight, tok, mod, gain], (n,),
        [
            pl.BlockSpec((hw, blk), lambda i, s: (0, i)),
            pl.BlockSpec((hw, blk), lambda i, s: (0, i + n)),
            pl.BlockSpec((hw, width), lambda i, s: (s[0], 0)),
            pl.BlockSpec((hw, width), lambda i, s: (1 - s[0], 0)),
            row, whole(mod.shape), whole(gain.shape),
        ],
        [row, row, row],
        [sds((span, width), F32), sds((span, width), F32), sds((span, width), BF16)],
        mb=12, us=3, name="post",
    )


def mlp_body(
    s_ref, n2a_ref, n2b_ref, wa_ref, wb_ref, mod_ref, w1_ref, b1_ref, w2_ref,
    hid_ref, pre_ref, b1g_ref, b2g_ref,
):
    step = pl.program_id(0)
    first = step < pl.num_programs(0) // 2
    width = n2a_ref.shape[1]
    x = jnp.where(first, n2a_ref[...], n2b_ref[...])
    wtd = jnp.where(first, wa_ref[...], wb_ref[...]).astype(F32)
    g_mlp = (wtd * mod_ref[0:1, 5 * width : 6 * width]).astype(BF16)
    bias = b1_ref[...].astype(F32)[None, :]
    hf = w1_ref.shape[1]
    bias = jnp.where(s_ref[0] == 0, bias[:, :hf], bias[:, hf:])
    c0 = 0.7978845608028654
    c1 = c0 * 0.044715
    parts = []
    for at in range(0, hf, MLP_COLS):
        cols = slice(at, at + MLP_COLS)
        v = dot(x, w1_ref[:, cols]) + bias[:, cols]
        gh = dot_nt(g_mlp, w2_ref[cols, :])
        v2 = v * v
        th = jnp.tanh(v * (c0 + c1 * v2))
        up = 0.5 + 0.5 * th
        hid_ref[:, cols] = (v * up).astype(BF16)
        slope = up + v * (0.5 - 0.5 * (th * th)) * (c0 + 3.0 * c1 * v2)
        pre = (gh * slope).astype(BF16)
        pre_ref[:, cols] = pre
        parts.append(jnp.sum(pre.astype(F32), axis=0, keepdims=True))
    b1_part = jnp.concatenate(parts, axis=1)
    b2_part = jnp.sum(g_mlp.astype(F32), axis=0, keepdims=True)

    @pl.when(step == 0)
    def _():
        b1g_ref[...] = b1_part
        b2g_ref[...] = b2_part

    @pl.when(step > 0)
    def _():
        b1g_ref[...] += b1_part
        b2g_ref[...] += b2_part


def halves(blk, width, n):
    return [
        pl.BlockSpec((blk, width), lambda i, s: (jnp.minimum(i, n - 1), 0)),
        pl.BlockSpec((blk, width), lambda i, s: (jnp.maximum(i - n, 0), 0)),
    ]


def mlp_call(order, n2a, n2b, wa, wb, mod, w1, b1, w2):
    span, width = n2a.shape
    hf = w1.shape[1] // 2
    blk = 512
    n = span // blk
    row = lambda w: pl.BlockSpec((blk, w), lambda i, s: (i, 0))
    return order.call(
        mlp_body, [n2a, n2b, wa, wb, mod, w1, b1, w2], (2 * n,),
        halves(blk, width, n) + halves(blk, width, n)
        + [
            whole(mod.shape),
            pl.BlockSpec((width, hf), lambda i, s: (0, s[0])),
            whole(b1.shape),
            pl.BlockSpec((hf, width), lambda i, s: (s[0], 0)),
        ],
        [row(hf), row(hf), whole((1, hf)), whole((1, width))],
        [sds((2 * span, hf), BF16), sds((2 * span, hf), BF16),
         sds((1, hf), F32), sds((1, width), F32)],
        mb=24, us=9.6, name="mlp",
    )


def store_parts(s_ref, acc_ref, r, keep_ref, send_ref):
    for i in range(8):
        rest = sum(((i >> (2 - j)) & 1) * s_ref[6 + j] for j in range(3))
        for ref, bit in ((keep_ref, s_ref[1]), (send_ref, 1 - s_ref[1])):
            at = pl.ds(pl.multiple_of((rest + bit * s_ref[5]) * r, 16), r)
            ref[i // 4, i % 4] = acc_ref[at, :]


def wgrad_body(r, s_ref, la_ref, lb_ref, g_ref, keep_ref, send_ref, acc_ref):
    span = la_ref.shape[0]
    acc_ref[...] = (dot_tn(la_ref[...], g_ref[:span]) + dot_tn(lb_ref[...], g_ref[span:])).astype(BF16)
    store_parts(s_ref, acc_ref, r, keep_ref, send_ref)


def wgrad_call(order, left_a, left_b, right, blk):
    rows, cols = left_a.shape[1], right.shape[1]
    length = right.shape[0]
    r = rows // 16
    out = pl.BlockSpec((2, 4, r, blk), lambda i, s: (0, 0, 0, i))
    return order.call(
        functools.partial(wgrad_body, r), [left_a, left_b, right], (cols // blk,),
        [whole(left_a.shape), whole(left_b.shape), pl.BlockSpec((length, blk), lambda i, s: (0, i))],
        [out] * 2, [sds((2, 4, r, cols), BF16)] * 2,
        scratch=[pltpu.VMEM((rows, blk), BF16)], mb=16, us=4.2, name="wgrad_fc1",
    )


def wgrad2_body(
    r, s_ref, lm_ref, lo_ref, wa_ref, wb_ref, mod_ref, w2_ref, bias_ref, keep_ref, send_ref, gate_ref, acc_ref
):
    step, n = pl.program_id(0), pl.num_programs(0)
    mine = lax.div(step, n // 2) == s_ref[0]
    span, half = wa_ref.shape
    width = 2 * half
    here = pl.ds(pl.multiple_of(s_ref[0] * half, 128), half)
    own, oth = wa_ref[...], wb_ref[...]

    @pl.when(mine)
    def _():
        acc_ref[...] = dot_tn(lm_ref[:span], own) + dot_tn(lm_ref[span:], oth)

    @pl.when(jnp.logical_not(mine))
    def _():
        acc_ref[...] = dot_tn(lo_ref[:span], oth) + dot_tn(lo_ref[span:], own)

    part = jnp.sum(acc_ref[...] * w2_ref[...].astype(F32), axis=0, keepdims=True)

    @pl.when(step == 0)
    def _():
        tokens = jnp.sum(own.astype(F32), axis=0, keepdims=True) + jnp.sum(oth.astype(F32), axis=0, keepdims=True)
        bias = bias_ref[...].astype(F32)[None, :]
        gate_ref[...] = part + tokens * jnp.where(s_ref[0] == 0, bias[:, :half], bias[:, half:])

    @pl.when(step > 0)
    def _():
        gate_ref[...] += part

    gate = mod_ref[0:1, pl.ds(pl.multiple_of(5 * width + s_ref[0] * half, 128), half)]
    za, zb = lax.div(step, 2), lax.rem(step, 2)
    slot = jnp.where(s_ref[0] == 0, zb * 2 + za, za * 2 + zb)
    for other in range(2):
        for ref, bit in ((keep_ref, s_ref[1]), (send_ref, 1 - s_ref[1])):
            at = pl.ds(pl.multiple_of((other * s_ref[6] + bit * s_ref[5]) * r, 16), r)
            ref[other, slot] = (acc_ref[at, :] * gate).astype(BF16)


def wgrad2_call(order, hidden, hidden_o, wa, wb, mod, w2, bias):
    length, hf = hidden.shape
    span, width = wa.shape
    hw = width // 2
    r = hf // 8
    left = lambda first: pl.BlockSpec((length, 4 * r), lambda i, s: (0, jnp.clip(i - first(s[0]), 0, 1)))
    cols = pl.BlockSpec((span, hw), lambda i, s: (0, s[0]))
    return order.call(
        functools.partial(wgrad2_body, r), [hidden, hidden_o, wa, wb, mod, w2, bias], (4,),
        [left(lambda c: 2 * c), left(lambda c: 2 - 2 * c), cols, cols, whole(mod.shape), pl.BlockSpec((4 * r, hw), lambda i, s: (i, s[0])), whole(bias.shape)],
        [whole((2, 4, r, hw))] * 2 + [whole((1, hw))], [sds((2, 4, r, hw), BF16)] * 2 + [sds((1, hw), F32)],
        scratch=[pltpu.VMEM((4 * r, hw), F32)], mb=16, us=4.5, name="wgrad_fc2",
    )


def fold_body(s_ref, ka, ra, ks, rs, away_ref, stay_ref):
    away_ref[...] = ka[0] + ra[0]
    stay_ref[...] = ks[0] + rs[0]


def fold_call(order, step, keep, got):
    _, count, r, n = keep.shape
    blk = 768 if n % 768 == 0 else 384
    away = pl.BlockSpec((1, count, r, blk), lambda i, s: (1 - s[step], 0, 0, i))
    stay = pl.BlockSpec((1, count, r, blk), lambda i, s: (s[step], 0, 0, i))
    out = pl.BlockSpec((count, r, blk), lambda i, s: (0, 0, i))
    return order.call(
        fold_body, [keep, got, keep, got], (n // blk,), [away, away, stay, stay], [out] * 2,
        [sds((count, r, n), BF16)] * 2, mb=8, us=1.2, name="fold",
    )


def join_ff_body(s_ref, ka_ref, ga_ref, ks_ref, gs_ref, away_in, stay_in, away_ref, stay_ref):
    r = away_in.shape[1]
    width = ka_ref.shape[3]
    for out, one, k_ref, g_ref in ((away_ref, away_in, ka_ref, ga_ref), (stay_ref, stay_in, ks_ref, gs_ref)):
        out[:, :r] = one[...]
        two = k_ref[0] + g_ref[0]
        for q in range(two.shape[1] // r):
            out[:, r:, q * width : (q + 1) * width] = two[:, q * r : (q + 1) * r]


def join_ff_call(order, step, one, two):
    keep, got = two
    away_in, stay_in = one
    specs = []
    for away in (True, False):
        pick = (lambda i, s: (1 - s[step], 0, 0, 0)) if away else (lambda i, s: (s[step], 0, 0, 0))
        specs += [pl.BlockSpec((1,) + keep.shape[1:], pick)] * 2
    count, r, n = away_in.shape
    shape = (count, 2 * r, n)
    return order.call(
        join_ff_body, [keep, got, keep, got, away_in, stay_in], (1,),
        specs + [whole(away_in.shape)] * 2, [whole(shape)] * 2, [sds(shape, BF16)] * 2, mb=12, us=1.2, name="fold_ff",
    )


def fold_att_body(s_ref, *refs):
    for out, (k1, g1, k2, g2) in ((refs[8], refs[0:4]), (refs[9], refs[4:8])):
        n = k1.shape[3]
        out[:, :, :n] = k1[0] + g1[0]
        out[:, :, n:] = k2[0] + g2[0]


def fold_att_call(order, step, one, two):
    specs = []
    args = []
    for away in (True, False):
        for keep, got in (one, two):
            pick = (lambda i, s: (1 - s[step], 0, 0, 0)) if away else (lambda i, s: (s[step], 0, 0, 0))
            specs += [pl.BlockSpec((1,) + keep.shape[1:], pick)] * 2
            args += [keep, got]
    _, count, r, n = one[0].shape
    shape = (count, r, n + two[0].shape[3])
    return order.call(
        fold_att_body, args, (1,), specs, [whole(shape)] * 2, [sds(shape, BF16)] * 2, mb=12, us=1.2, name="fold_att"
    )


def add_body(s_ref, a_ref, b_ref, out_ref):
    out_ref[...] = a_ref[...] + b_ref[...]


def add_call(order, a, b):
    return order.call(
        add_body, [a, b], (1,), [whole(a.shape)] * 2, [whole(a.shape)], [sds(a.shape, BF16)], mb=8, us=1.0, name="add"
    )[0]


def place_ff_body(s_ref, mine_ref, other_ref, fc1_ref, fc2_ref):
    core = s_ref[0]
    r, n = fc1_ref.shape[0], mine_ref.shape[1]
    width = fc2_ref.shape[1] // 2
    for ref, at in ((mine_ref, core), (other_ref, 1 - core)):
        fc1_ref[:, pl.ds(pl.multiple_of(at * n, 128), n)] = ref[:r].astype(F32)
        cols = pl.ds(pl.multiple_of(at * width, 128), width)
        for q in range(n // width):
            fc2_ref[q * r : (q + 1) * r, cols] = ref[r:, q * width : (q + 1) * width].astype(F32)


def place_ff_call(order, mine, other, hw):
    r, n = mine.shape[0] // 2, mine.shape[1]
    shapes = [(r, 2 * n), (r * (n // hw), 2 * hw)]
    return order.call(
        place_ff_body, [mine, other], (1,), [whole(mine.shape)] * 2, [whole(x) for x in shapes],
        [sds(x, F32) for x in shapes], mb=8, us=1.0, name="place_ff",
    )


def place_att_body(s_ref, mine_ref, other_ref, out_ref, qkv_ref):
    core = s_ref[0]
    width = out_ref.shape[1]
    hw = width // 2
    for ref, at in ((mine_ref, core), (other_ref, 1 - core)):
        out_ref[:, pl.ds(pl.multiple_of(at * hw, 128), hw)] = ref[:, :hw].astype(F32)
        for p in range(hw // 128):
            for j in range(3):
                to = pl.ds(pl.multiple_of(j * width + at * hw + p * 128, 128), 128)
                src = hw + p * 384 + j * 128
                qkv_ref[:, to] = ref[:, src : src + 128].astype(F32)


def place_att_call(order, mine, other, width):
    r = mine.shape[0]
    shapes = [(r, width), (r, 3 * width)]
    return order.call(
        place_att_body, [mine, other], (1,), [whole(mine.shape)] * 2, [whole(x) for x in shapes],
        [sds(x, F32) for x in shapes], mb=8, us=1.0, name="place_att",
    )


def pack_body(
    s_ref, s1a_ref, s1b_ref, s2_ref, gate_ref, b1_ref, b2_ref, g1_ref, g2_ref, mod_ref, cond_ref, out_ref
):
    width = s2_ref.shape[1]
    h = width // 2
    core = s_ref[0]
    mine = jnp.where(core == 0, 1.0, 0.0)
    gain_one, gain_two = g1_ref[...].astype(F32)[None, :], g2_ref[...].astype(F32)[None, :]
    scale_one = 1.0 + mod_ref[0:1, width : 2 * width]
    scale_two = 1.0 + mod_ref[0:1, 4 * width : 5 * width]
    second_one, second_two = s1a_ref[1:2, :] + s1b_ref[1:2, :], s2_ref[1:2, :]
    gate = jnp.concatenate([gate_ref[...] * mine, gate_ref[...] * (1.0 - mine)], axis=1)
    flat = jnp.concatenate(
        [
            s1a_ref[0:1, :] + s1b_ref[0:1, :], second_one * gain_one, s2_ref[2:3, :],
            s2_ref[0:1, :], second_two * gain_two, gate,
        ],
        axis=1,
    )
    b1 = jnp.concatenate([b1_ref[...] * mine, b1_ref[...] * (1.0 - mine)], axis=1)
    sources = (flat, b1, second_one * scale_one, second_two * scale_two, 0.5 * b2_ref[...])
    out_ref[...] = jnp.zeros_like(out_ref)
    cond = 0.5 * cond_ref[...].astype(F32)
    ndp = out_ref.shape[0] - 2
    for d in range(ndp):
        for j, source in enumerate(sources):
            n = source.shape[1] // ndp
            out_ref[d, j : j + 1, 0:n] = source[:, d * n : (d + 1) * n]
        out_ref[d, 5:6, 0:128] = cond
    for j in range(12):
        out_ref[ndp + j // 8, j % 8 : j % 8 + 1, :] = flat[:, j * h : (j + 1) * h]


def pack_call(order, *args):
    h = args[2].shape[1] // 2
    shape = (18, 8, h)
    return order.call(
        pack_body, list(args), (1,), [whole(a.shape) for a in args], [whole(shape)], [sds(shape, F32)],
        mb=8, us=1.0, name="pack",
    )[0]


def deal_body(s_ref, a_ref, b_ref, ada_ref, cg_ref, keep_ref, send_ref, acc_ref):
    acc_ref[...] = a_ref[...] + b_ref[...]
    for i in range(8):
        rest = sum(((i >> (2 - j)) & 1) * s_ref[6 + j] for j in range(3))
        keep_ref[i] = acc_ref[rest + s_ref[1] * s_ref[5]]
        send_ref[i] = acc_ref[rest + (1 - s_ref[1]) * s_ref[5]]
    flat = jnp.concatenate([acc_ref[16 + j // 8, j % 8 : j % 8 + 1, :] for j in range(12)], axis=1)
    high = flat.astype(BF16)
    rest = flat - high.astype(F32)
    mid = rest.astype(BF16)
    low = (rest - mid.astype(F32)).astype(BF16)
    row_id = lax.broadcasted_iota(jnp.int32, (16, flat.shape[1]), 0)
    zero = jnp.zeros_like(high)
    terms = jnp.where(row_id == 0, high, jnp.where(row_id == 1, mid, jnp.where(row_id == 2, low, zero)))
    cg_ref[...] = jnp.sum(dot_nt(terms, ada_ref[...]), axis=0, keepdims=True)


def deal_call(order, mine, got, ada):
    shape = (8,) + mine.shape[1:]
    return order.call(
        deal_body, [mine, got, ada], (1,), [whole(mine.shape), whole(mine.shape), whole(ada.shape)],
        [whole((1, ada.shape[0])), whole(shape), whole(shape)],
        [sds((1, ada.shape[0]), F32), sds(shape, F32), sds(shape, F32)],
        scratch=[pltpu.VMEM(mine.shape, F32)], mb=8, us=1.0, name="deal",
    )


def relay_body(step, s_ref, keep_ref, got_ref, stay_ref, away_ref):
    sources, rest = 2 ** (step - 2), 2 ** (4 - step)
    mine = s_ref[step]
    for which, ref in enumerate((keep_ref, got_ref)):
        for src in range(sources):
            for k in range(rest):
                to = (which * sources + src) * rest + k
                at = src * 2 * rest + k
                stay_ref[to] = ref[at + mine * rest]
                away_ref[to] = ref[at + (1 - mine) * rest]


def relay_call(order, step, keep, got):
    return order.call(
        functools.partial(relay_body, step), [keep, got], (1,), [whole(keep.shape)] * 2, [whole(keep.shape)] * 2,
        [sds(keep.shape, F32)] * 2, mb=8, us=1.0, name="relay",
    )


def last_body(s_ref, keep_ref, got_ref, ada_ref, adab_ref, b1_ref, g1_ref, g2_ref, b2_ref):
    parts = [ref[k] for ref in (keep_ref, got_ref) for k in range(8)]
    sums = parts[0]
    for part in parts[1:]:
        sums = sums + part
    cond = jnp.concatenate([part[5:6, 0:128] for part in parts], axis=0)
    grads = jnp.concatenate([part[0:1] for part in parts], axis=0)
    ada = lax.dot_general(
        cond, grads, (((0,), (0,)), ((), ())), precision=lax.Precision.HIGHEST, preferred_element_type=F32
    )
    ada_ref[...] = ada[:, : ada_ref.shape[1]]
    for j, ref in enumerate((adab_ref, b1_ref, g1_ref, g2_ref, b2_ref)):
        ref[...] = sums[j : j + 1, : ref.shape[1]]


def last_call(order, keep, got, ndp):
    h = keep.shape[2]
    na, nb, nc = 12 * h // ndp, 2 * h // ndp, 8 * h // ndp
    shapes = [(128, na), (1, na), (1, nc), (1, nb), (1, nb), (1, nb)]
    return order.call(
        last_body, [keep, got], (1,), [whole(keep.shape)] * 2, [whole(x) for x in shapes],
        [sds(x, F32) for x in shapes], mb=8, us=1.0, name="small_last",
    )


def part_body(nt, s_ref, g_ref, w_ref, out_ref):
    part = dot_nt(g_ref[...], w_ref[...]) if nt else dot(g_ref[...], w_ref[...])
    out_ref[...] = part.astype(out_ref.dtype)


def part_call(order, nt, g, w, half):
    length, hf = g.shape
    span = length // 2
    width = w.shape[0] if nt else w.shape[1]
    wspec = (
        pl.BlockSpec((width, hf), lambda i, s: (0, s[0]))
        if nt
        else pl.BlockSpec((hf, width), lambda i, s: (s[0], 0))
    )
    return order.call(
        functools.partial(part_body, nt), [g, w], (1,),
        [pl.BlockSpec((span, hf), lambda i, s: (half, 0)), wspec],
        [whole((span, width))], [sds((span, width), BF16 if half else F32)], mb=12, us=2.0, name="part",
    )[0]


def norm2_body(s_ref, own_ref, got_ref, mid_ref, br_ref, wtd_ref, mod_ref, gain_ref, gmid_ref, gatt_ref, sum_ref):
    width = mid_ref.shape[1]
    g = own_ref[...] + got_ref[...].astype(F32)
    a_two, inv = layer_stats(mid_ref[...])
    ga = g * (gain_ref[...].astype(F32)[None, :] * (1.0 + mod_ref[0:1, 4 * width : 5 * width]))
    gaa = ga * a_two
    g_mid = wtd_ref[...].astype(F32) + inv * (
        ga - jnp.mean(ga, -1, keepdims=True) - a_two * jnp.mean(gaa, -1, keepdims=True)
    )
    gmid_ref[...] = g_mid
    gatt_ref[...] = (g_mid * mod_ref[0:1, 2 * width : 3 * width]).astype(BF16)
    sums = jnp.concatenate(
        [
            jnp.sum(g, axis=0, keepdims=True),
            jnp.sum(g * a_two, axis=0, keepdims=True),
            jnp.sum(g_mid * br_ref[...], axis=0, keepdims=True),
        ],
        axis=0,
    )

    @pl.when(pl.program_id(0) == 0)
    def _():
        sum_ref[...] = jnp.zeros_like(sum_ref)

    sum_ref[0:3, :] += sums


def norm2_call(order, own, got, mid, br, wtd, mod, gain):
    span, width = mid.shape
    blk = 512
    row = pl.BlockSpec((blk, width), lambda i, s: (i, 0))
    return order.call(
        norm2_body, [own, got, mid, br, wtd, mod, gain], (span // blk,),
        [row] * 5 + [whole(mod.shape), whole(gain.shape)],
        [row, row, whole((8, width))],
        [sds((span, width), F32), sds((span, width), BF16), sds((8, width), F32)],
        mb=12, us=3, name="norm2",
    )


def oproj_body(r, s_ref, w_ref, ga_ref, gb_ref, am_ref, ao_ref, gt_ref, keep_ref, send_ref, acc_ref):
    span = ga_ref.shape[0]
    half = am_ref.shape[0]
    core = s_ref[0]
    w = w_ref[...]
    gt_ref[:, :span] = dot_nt(w, ga_ref[...]).astype(BF16)
    gt_ref[:, span:] = dot_nt(w, gb_ref[...]).astype(BF16)
    cols = pl.ds(pl.multiple_of(core * half, 128), half)
    gac, gbc = ga_ref[:, cols], gb_ref[:, cols]
    mine = dot(am_ref[:, :span], gac) + dot(am_ref[:, span:], gbc)
    other = dot(ao_ref[:, span:], gac) + dot(ao_ref[:, :span], gbc)
    acc_ref[pl.ds(pl.multiple_of(core * half, 16), half), :] = mine.astype(BF16)
    acc_ref[pl.ds(pl.multiple_of((1 - core) * half, 16), half), :] = other.astype(BF16)
    store_parts(s_ref, acc_ref, r, keep_ref, send_ref)


def oproj_call(order, blocks, out_weight, ga, gb, att_t, att_o):
    span, width = ga.shape
    hw = width // 2
    r = width // 16
    out = pl.BlockSpec((2, 4, r, hw), lambda i, s: (0, 0, 0, 0))
    return order.call(
        functools.partial(oproj_body, r), [out_weight, ga, gb, att_t, att_o], (1,),
        [pl.BlockSpec((hw, width), lambda i, s: (s[0], 0)), whole(ga.shape), whole(ga.shape),
         whole(att_t.shape), whole(att_t.shape)],
        [whole((hw, 2 * span))] + [out] * 2,
        [sds((hw, 2 * span), BF16)] + [sds((2, 4, r, blocks * hw), BF16)] * 2,
        scratch=[pltpu.VMEM((width, hw), BF16)], mb=8, us=3, name="oproj",
    )


def norm1_body(s_ref, own_ref, got_ref, tok_ref, gmid_ref, mod_ref, gain_ref, out_ref):
    width = tok_ref.shape[1]
    g = own_ref[...] + got_ref[...].astype(F32)
    a_one, inv = layer_stats(tok_ref[...].astype(F32))
    ga = g * (gain_ref[...].astype(F32)[None, :] * (1.0 + mod_ref[0:1, width : 2 * width]))
    gaa = ga * a_one
    out_ref[...] = (
        gmid_ref[...]
        + inv * (ga - jnp.mean(ga, -1, keepdims=True) - a_one * jnp.mean(gaa, -1, keepdims=True))
    ).astype(BF16)


def norm1_call(order, own, got, tok, gmid, mod, gain):
    span, width = tok.shape
    blk = 256
    row = pl.BlockSpec((blk, width), lambda i, s: (i, 0))
    return order.call(
        norm1_body, [own, got, tok, gmid, mod, gain], (span // blk,),
        [row] * 4 + [whole(mod.shape), whole(gain.shape)], [row], [sds((span, width), BF16)],
        mb=12, us=3, name="norm1",
    )[0]


def dgrad_body(np_, s_ref, *refs):
    gs, (wq_ref, wk_ref, wv_ref), out_ref = refs[:np_], refs[np_ : np_ + 3], refs[np_ + 3]
    total = None
    for j, w_ref in enumerate((wq_ref, wk_ref, wv_ref)):
        left = jnp.concatenate(
            [g[:, at + j * 128 : at + (j + 1) * 128] for g in gs for at in range(0, g.shape[1], 384)], axis=1
        )
        part = dot_nt(left, w_ref[...])
        total = part if total is None else total + part
    out_ref[...] = total.astype(out_ref.dtype)


def dgrad_call(order, gs, qkv_weight, half):
    span = gs[0].shape[0] // 2
    width = qkv_weight.shape[0]
    hw = width // 2
    wspec = lambda j: pl.BlockSpec((width, hw), lambda i, s: (0, 2 * j + s[0]))
    return order.call(
        functools.partial(dgrad_body, len(gs)), [*gs, qkv_weight, qkv_weight, qkv_weight], (1,),
        [pl.BlockSpec((span, g.shape[1]), lambda i, s: (half, 0)) for g in gs] + [wspec(0), wspec(1), wspec(2)],
        [whole((span, width))], [sds((span, width), BF16 if half else F32)], mb=12, us=2.0, name="dgrad",
    )[0]


class Grid:
    ORDERS = ((1, 2, 4, 8), (2, 1, 8, 4))

    def __init__(self, ndp):
        self.index = lax.axis_index("dp")
        core = lax.axis_index("ctx")
        self.flip = lambda mask: [(i, i ^ mask) for i in range(ndp)]
        masks = [jnp.where(core == 0, a, b) for a, b in zip(*self.ORDERS)]
        bits = [jnp.where((self.index & m) > 0, 1, 0) for m in masks]
        self.place = jnp.stack([core, *bits, *masks, self.index // 4, self.index]).astype(jnp.int32)
        self.pairs = [
            [(2 * i + c, 2 * (i ^ self.ORDERS[c][step]) + c) for i in range(ndp) for c in range(2)] for step in range(4)
        ]


class Job:
    def __init__(self, pairs):
        self.pairs, self.step = pairs, 0

    def start(self, keep, send):
        self.keep = keep
        self.got = lax.ppermute(send, ("dp", "ctx"), self.pairs[self.step])
        self.step += 1

    def parts(self):
        shape = self.keep.shape
        if self.step > 1:
            shape = (2, shape[0] // 2) + shape[1:]
        return self.keep.reshape(shape), self.got.reshape(shape)

    def fold(self, order):
        away, stay = self.split(order)
        self.start(stay, away)

    def split(self, order):
        return fold_call(order, self.step + 1, *self.parts())

    def last(self):
        return self.keep[0], self.got[0]


def join(order, fold, one, two):
    job = Job(two.pairs)
    job.step = two.step
    away, stay = fold(order, job.step + 1, one if isinstance(one, tuple) else one.parts(), two.parts())
    job.start(stay, away)
    return job


def local_pair(
    tokens_in, cond_vec, positions, absorbed, cotangent, norm1_gain, qkv_weight, out_weight,
    norm2_gain, fc1_weight, fc1_bias, fc2_weight, fc2_bias, ada_weight, ada_bias, *, ndp,
):
    _, span, width = tokens_in.shape
    hw = width // 2
    grid = Grid(ndp)
    order = Order(grid.place)
    swap = lambda v: lax.ppermute(v, "ctx", [(0, 1), (1, 0)])

    tok = tokens_in[0]
    tok_o = swap(tok)
    pos_o = swap(positions)

    a_one, queries, keys, values, cos_t, sin_t, att_t, prob, inverse, mod, wtd = attend_call(
        order, tok, tok_o, cond_vec, ada_weight, ada_bias, norm1_gain, qkv_weight, positions, pos_o,
        cotangent[0], absorbed,
    )
    wtd_o = swap(wtd)
    att_o = swap(att_t)
    middle, branch, n2 = post_call(order, att_t, att_o, out_weight, hbm(tok), mod, norm2_gain)
    n2_o = swap(n2)
    hidden, g_pre, b1_sum, b2_sum = mlp_call(
        order, n2, n2_o, wtd, wtd_o, mod, fc1_weight, fc1_bias, fc2_weight
    )
    hidden_o = swap(hidden)
    fc1, fc2, rest, last = (Job(grid.pairs) for _ in range(4))
    fc1.start(*wgrad_call(order, n2, n2_o, g_pre, 768))
    pn_got = swap(part_call(order, True, g_pre, fc1_weight, 1))
    pn_own = part_call(order, True, g_pre, fc1_weight, 0)
    *bufs, gate_sum = wgrad2_call(order, hidden, hidden_o, wtd, wtd_o, mod, fc2_weight, fc2_bias)
    fc2.start(*bufs)
    pm_got = swap(part_call(order, False, hidden, fc2_weight, 1))
    pm_own = part_call(order, False, hidden, fc2_weight, 0)
    fc1.fold(order)
    g_mid, g_att, sums2 = norm2_call(order, pn_own, pn_got, middle, branch, wtd, mod, norm2_gain)
    g_att_o = swap(g_att)
    g_attn_t, *bufs = oproj_call(order, 3, out_weight, g_att, g_att_o, att_t, att_o)

    def back(start, count, old, block, blocks):
        return attn_bwd(
            order, start, count, hbm(prob), inverse, g_attn_t, att_t, queries, keys, values, cos_t, sin_t,
            a_one, mod, norm1_gain, qkv_weight, old, block, blocks,
        )

    pairs = hw // 128
    g_a, sums_a, *bufs = back(0, pairs - 1, bufs, 1, pairs)
    rest.start(*bufs)
    fc2.fold(order)
    fc1.fold(order)
    g_b, sums_b, *bufs = back(pairs - 1, 1, None, 0, 1)
    last.start(*bufs)
    mixed = mix_call(order, pm_own, pm_got, middle, mod, fc2_bias)
    d_got = swap(dgrad_call(order, [g_a, g_b], qkv_weight, 1))
    rest.fold(order)
    fc1_split = fc1.split(order)
    fc2.fold(order)
    last.fold(order)
    packet = pack_call(
        order, sums_a, sums_b, sums2, gate_sum, b1_sum, b2_sum, norm1_gain, norm2_gain, mod, cond_vec
    )
    packet_o = swap(packet)
    cond_grad, keep, send = deal_call(order, packet, packet_o, ada_weight)

    def small(step, keep, got):
        stay, away = relay_call(order, step, keep, got)
        return stay, lax.ppermute(away, ("dp", "ctx"), grid.pairs[step - 1])

    got = lax.ppermute(send, ("dp", "ctx"), grid.pairs[0])
    att = join(order, fold_att_call, rest, last)
    ff = join(order, join_ff_call, tuple(fc1_split), fc2)
    keep, got = small(2, keep, got)
    d_own = dgrad_call(order, [g_a, g_b], qkv_weight, 0)
    input_grad = norm1_call(order, d_own, d_got, tok, g_mid, mod, norm1_gain)
    keep, got = small(3, keep, got)
    att.fold(order)
    ff_sum = add_call(order, *ff.last())
    ff_other = swap(ff_sum)
    keep, got = small(4, keep, got)
    att_sum = add_call(order, *att.last())
    att_other = swap(att_sum)
    fc1_grad, fc2_grad = place_ff_call(order, ff_sum, ff_other, hw)
    ada_grad, ada_bias_grad, fc1_bias_grad, norm1_grad, norm2_grad, fc2_bias_grad = last_call(order, keep, got, ndp)
    out_grad, qkv_grad = place_att_call(order, att_sum, att_other, width)
    return (
        mixed[None], input_grad[None], cond_grad, norm1_grad[0], qkv_grad, out_grad, norm2_grad[0],
        fc1_grad, fc1_bias_grad[0], fc2_grad, fc2_bias_grad[0], ada_grad, ada_bias_grad[0],
    )


def layer_norm(stream):
    row_mean = jnp.mean(stream, axis=-1, keepdims=True)
    centred = stream - row_mean
    variance = jnp.mean(centred * centred, axis=-1, keepdims=True)
    return centred * lax.rsqrt(variance + EPS)


def pre_norm(stream, norm_gain, shift_vec, scale_vec):
    return layer_norm(stream) * norm_gain * (1.0 + scale_vec[:, None, :]) + shift_vec[:, None, :]


def gelu_tanh(stream):
    return jax.nn.gelu(stream, approximate=True)


def block_rows(row_count):
    size_now = row_count
    while size_now > 512 and size_now % 2 == 0:
        size_now = size_now // 2
    return size_now


def rotary_tables(positions):
    inv_freq = 10000.0 ** (-jnp.arange(0, HEAD_DIM, 2).astype(jnp.float32) / HEAD_DIM)
    angles = positions.astype(jnp.float32)[..., None] * inv_freq
    cos_table = jnp.concatenate([jnp.cos(angles), jnp.cos(angles)], axis=-1)[..., None, :]
    sin_table = jnp.concatenate([jnp.sin(angles), jnp.sin(angles)], axis=-1)[..., None, :]
    return (cos_table, sin_table)


def rotate_pos(stream, cos_table, sin_table):
    half_dim = stream.shape[-1] // 2
    turned = jnp.concatenate([-stream[..., half_dim:], stream[..., :half_dim]], axis=-1)
    return stream * cos_table + turned * sin_table


def over_blocks(step_fn, fold_state, pieces):
    row_count = pieces[0].shape[1]
    size_now = block_rows(row_count)

    def one_turn(turn_idx, inner_state):
        part_list = tuple(
            (
                lax.dynamic_slice_in_dim(member, turn_idx * size_now, size_now, 1)
                for member in pieces
            )
        )
        return step_fn(inner_state, part_list, turn_idx * size_now)

    return lax.fori_loop(0, row_count // size_now, one_turn, fold_state)


def score_grads(query_blk, key_blk, value_blk, grad_blk, top_blk, total_blk, delta_blk):
    scores = (
        jnp.einsum("sqhd,skhd->sqhk", query_blk, key_blk, preferred_element_type=jnp.float32)
        * SCORE_SCALE
    )
    probability = jnp.exp(scores - top_blk[..., None]) / total_blk[..., None]
    grad_prob = jnp.einsum(
        "sqhd,skhd->sqhk", grad_blk, value_blk, preferred_element_type=jnp.float32
    )
    grad_scores = (probability * (grad_prob - delta_blk[..., None])).astype(jnp.bfloat16)
    return (probability, grad_scores)


def local_any(
    tokens_in,
    cond_vec,
    positions,
    absorbed,
    cotangent,
    norm1_gain,
    qkv_weight,
    out_weight,
    norm2_gain,
    fc1_weight,
    fc1_bias,
    fc2_weight,
    fc2_bias,
    ada_weight,
    ada_bias,
):
    seqs_here, span_len, model_width = tokens_in.shape
    head_shape = (seqs_here, span_len, HEADS, HEAD_DIM)
    stream = tokens_in.astype(jnp.float32)
    modulation = jnp.dot(
        cond_vec, ada_weight, preferred_element_type=jnp.float32
    ) + ada_bias.astype(jnp.float32)
    shift_one, scale_one, gate_one, shift_two, scale_two, gate_two = jnp.split(
        modulation, 6, axis=-1
    )
    gain_one = norm1_gain.astype(jnp.float32)
    gain_two = norm2_gain.astype(jnp.float32)
    normed_f, pull_one = jax.vjp(pre_norm, stream, gain_one, shift_one, scale_one)
    normed_one = normed_f.astype(jnp.bfloat16)
    projected = jnp.dot(normed_one, qkv_weight, preferred_element_type=jnp.float32)
    cos_table, sin_table = rotary_tables(positions)
    turned_pair, pull_rot = jax.vjp(
        lambda query_pre, key_pre: (
            rotate_pos(query_pre, cos_table, sin_table),
            rotate_pos(key_pre, cos_table, sin_table),
        ),
        projected[..., :model_width].reshape(head_shape),
        projected[..., model_width : 2 * model_width].reshape(head_shape),
    )
    queries = turned_pair[0].astype(jnp.bfloat16)
    key_loc = turned_pair[1].astype(jnp.bfloat16).reshape(seqs_here, span_len, model_width)
    value_loc = projected[..., 2 * model_width :].astype(jnp.bfloat16)

    def forward_step(fold_state, part_list, offset):
        run_max, run_sum, run_acc = fold_state
        key_blk = part_list[0].reshape(seqs_here, -1, HEADS, HEAD_DIM)
        value_blk = part_list[1].reshape(seqs_here, -1, HEADS, HEAD_DIM)
        scores = (
            jnp.einsum("sqhd,skhd->sqhk", queries, key_blk, preferred_element_type=jnp.float32)
            * SCORE_SCALE
        )
        new_max = jnp.maximum(run_max, jnp.max(scores, axis=-1))
        raised = jnp.exp(scores - new_max[..., None])
        shrink = jnp.exp(run_max - new_max)
        run_sum = run_sum * shrink + jnp.sum(raised, axis=-1)
        run_acc = run_acc * shrink[..., None] + jnp.einsum(
            "sqhk,skhd->sqhd",
            raised.astype(jnp.bfloat16),
            value_blk,
            preferred_element_type=jnp.float32,
        )
        return (new_max, run_sum, run_acc)

    empty_state = (
        jnp.full((seqs_here, span_len, HEADS), NEG_START, jnp.float32),
        jnp.zeros((seqs_here, span_len, HEADS), jnp.float32),
        jnp.zeros(head_shape, jnp.float32),
    )
    final_max, final_sum, final_acc = over_blocks(
        forward_step,
        empty_state,
        (
            lax.all_gather(key_loc, "ctx", axis=1, tiled=True),
            lax.all_gather(value_loc, "ctx", axis=1, tiled=True),
        ),
    )
    attn_out = final_acc / final_sum[..., None]
    attended = attn_out.reshape(seqs_here, span_len, model_width).astype(jnp.bfloat16)
    branch_att = jnp.dot(attended, out_weight, preferred_element_type=jnp.float32)
    middle = stream + gate_one[:, None, :] * branch_att
    normed_f2, pull_two = jax.vjp(pre_norm, middle, gain_two, shift_two, scale_two)
    normed_two = normed_f2.astype(jnp.bfloat16)
    hidden_pre = jnp.dot(
        normed_two, fc1_weight, preferred_element_type=jnp.float32
    ) + fc1_bias.astype(jnp.float32)
    hidden_f, pull_gelu = jax.vjp(gelu_tanh, hidden_pre)
    hidden = hidden_f.astype(jnp.bfloat16)
    branch_mlp = jnp.dot(hidden, fc2_weight, preferred_element_type=jnp.float32) + fc2_bias.astype(
        jnp.float32
    )
    mixed = (middle + gate_two[:, None, :] * branch_mlp).astype(jnp.bfloat16)
    weighted = cotangent.astype(jnp.float32) * absorbed.astype(jnp.float32)[..., None]
    grad_gate_two = jnp.sum(weighted * branch_mlp, axis=1)
    grad_mlp = (weighted * gate_two[:, None, :]).astype(jnp.bfloat16)
    grad_fc2b = jnp.sum(grad_mlp.astype(jnp.float32), axis=(0, 1))
    grad_fc2 = jnp.einsum("scf,scd->fd", hidden, grad_mlp, preferred_element_type=jnp.float32)
    grad_hidden = jnp.einsum(
        "scd,fd->scf", grad_mlp, fc2_weight, preferred_element_type=jnp.float32
    )
    grad_pre = pull_gelu(grad_hidden)[0].astype(jnp.bfloat16)
    grad_fc1b = jnp.sum(grad_pre.astype(jnp.float32), axis=(0, 1))
    grad_fc1 = jnp.einsum("scd,scf->df", normed_two, grad_pre, preferred_element_type=jnp.float32)
    grad_normed_two = jnp.einsum(
        "scf,df->scd", grad_pre, fc1_weight, preferred_element_type=jnp.float32
    )
    grad_mid_part, grad_gain_two, grad_shift_two, grad_scale_two = pull_two(grad_normed_two)
    grad_middle = weighted + grad_mid_part
    grad_gate_one = jnp.sum(grad_middle * branch_att, axis=1)
    grad_att = (grad_middle * gate_one[:, None, :]).astype(jnp.bfloat16)
    grad_out = jnp.einsum("scd,sce->de", attended, grad_att, preferred_element_type=jnp.float32)
    grad_attended = (
        jnp.einsum("sce,de->scd", grad_att, out_weight, preferred_element_type=jnp.float32)
        .astype(jnp.bfloat16)
        .reshape(head_shape)
    )
    row_delta = jnp.sum(grad_attended.astype(jnp.float32) * attn_out, axis=-1)

    def query_only_step(fold_state, part_list, offset):
        piece_len = part_list[0].shape[1]
        key_blk = part_list[0].reshape(seqs_here, piece_len, HEADS, HEAD_DIM)
        value_blk = part_list[1].reshape(seqs_here, piece_len, HEADS, HEAD_DIM)
        probability, grad_scores = score_grads(
            queries, key_blk, value_blk, grad_attended, final_max, final_sum, row_delta
        )
        return (
            fold_state
            + jnp.einsum(
                "sqhk,skhd->sqhd", grad_scores, key_blk, preferred_element_type=jnp.float32
            )
            * SCORE_SCALE
        )

    start_state = jnp.zeros(head_shape, jnp.float32)
    back_state = over_blocks(
        query_only_step,
        start_state,
        (
            lax.all_gather(key_loc, "ctx", axis=1, tiled=True),
            lax.all_gather(value_loc, "ctx", axis=1, tiled=True),
        ),
    )
    key_heads = key_loc.reshape(head_shape)
    value_heads = value_loc.reshape(head_shape)

    def local_key_step(fold_state, part_list, offset):
        grad_key_loc, grad_value_loc = fold_state
        query_blk = part_list[0].astype(jnp.bfloat16)
        grad_blk = part_list[1].astype(jnp.bfloat16)
        probability, grad_scores = score_grads(
            query_blk, key_heads, value_heads, grad_blk, part_list[2], part_list[3], part_list[4]
        )
        grad_value_loc = grad_value_loc + jnp.einsum(
            "sqhk,sqhd->skhd",
            probability.astype(jnp.bfloat16),
            grad_blk,
            preferred_element_type=jnp.float32,
        )
        grad_key_loc = (
            grad_key_loc
            + jnp.einsum(
                "sqhk,sqhd->skhd", grad_scores, query_blk, preferred_element_type=jnp.float32
            )
            * SCORE_SCALE
        )
        return (grad_key_loc, grad_value_loc)

    key_start = (jnp.zeros(head_shape, jnp.float32), jnp.zeros(head_shape, jnp.float32))
    grad_key_h, grad_value_h = over_blocks(
        local_key_step,
        key_start,
        (
            lax.all_gather(queries.astype(jnp.float32), "ctx", axis=1, tiled=True),
            lax.all_gather(grad_attended.astype(jnp.float32), "ctx", axis=1, tiled=True),
            lax.all_gather(final_max, "ctx", axis=1, tiled=True),
            lax.all_gather(final_sum, "ctx", axis=1, tiled=True),
            lax.all_gather(row_delta, "ctx", axis=1, tiled=True),
        ),
    )
    grad_key_loc = grad_key_h.reshape(seqs_here, span_len, model_width)
    grad_value_loc = grad_value_h.reshape(seqs_here, span_len, model_width)
    grad_query_pre, grad_key_pre = pull_rot((back_state, grad_key_loc.reshape(head_shape)))
    grad_proj = jnp.concatenate(
        [
            grad_query_pre.reshape(seqs_here, span_len, model_width),
            grad_key_pre.reshape(seqs_here, span_len, model_width),
            grad_value_loc,
        ],
        axis=-1,
    ).astype(jnp.bfloat16)
    grad_qkv = jnp.einsum("scd,sce->de", normed_one, grad_proj, preferred_element_type=jnp.float32)
    grad_normed_one = jnp.einsum(
        "sce,de->scd", grad_proj, qkv_weight, preferred_element_type=jnp.float32
    )
    grad_in_part, grad_gain_one, grad_shift_one, grad_scale_one = pull_one(grad_normed_one)
    input_grad = (grad_middle + grad_in_part).astype(jnp.bfloat16)
    partial_mod = jnp.concatenate(
        [
            grad_shift_one,
            grad_scale_one,
            grad_gate_one,
            grad_shift_two,
            grad_scale_two,
            grad_gate_two,
        ],
        axis=-1,
    )
    grad_mod = lax.psum(partial_mod, "ctx")
    cond_grad = jnp.einsum(
        "se,ce->sc",
        grad_mod,
        ada_weight.astype(jnp.float32),
        precision=lax.Precision.HIGHEST,
        preferred_element_type=jnp.float32,
    )
    first_cycle = (lax.axis_index("ctx") == 0).astype(jnp.float32)
    grad_ada = (
        jnp.einsum(
            "sc,se->ce",
            cond_vec.astype(jnp.float32),
            grad_mod,
            precision=lax.Precision.HIGHEST,
            preferred_element_type=jnp.float32,
        )
        * first_cycle
    )
    grad_adab = jnp.sum(grad_mod, axis=0) * first_cycle
    (
        part_g1,
        part_qkv,
        part_out,
        part_g2,
        part_fc1,
        part_fc1b,
        part_fc2,
        part_fc2b,
        part_ada,
        part_adab,
    ) = (
        lax.psum_scatter(grad_gain_one, "dp", scatter_dimension=0, tiled=True),
        lax.psum_scatter(grad_qkv, "dp", scatter_dimension=0, tiled=True),
        lax.psum_scatter(grad_out, "dp", scatter_dimension=0, tiled=True),
        lax.psum_scatter(grad_gain_two, "dp", scatter_dimension=0, tiled=True),
        lax.psum_scatter(grad_fc1, "dp", scatter_dimension=0, tiled=True),
        lax.psum_scatter(grad_fc1b, "dp", scatter_dimension=0, tiled=True),
        lax.psum_scatter(grad_fc2, "dp", scatter_dimension=0, tiled=True),
        lax.psum_scatter(grad_fc2b, "dp", scatter_dimension=0, tiled=True),
        lax.psum_scatter(grad_ada, "dp", scatter_dimension=1, tiled=True),
        lax.psum_scatter(grad_adab, "dp", scatter_dimension=0, tiled=True),
    )
    summed = lax.psum(
        (
            part_g1,
            part_qkv,
            part_out,
            part_g2,
            part_fc1,
            part_fc1b,
            part_fc2,
            part_fc2b,
            part_ada,
            part_adab,
        ),
        "ctx",
    )
    return (mixed, input_grad, cond_grad) + tuple(summed)


def local(*args, ndp, nctx):
    seqs, span, _ = args[0].shape
    if nctx == 2 and seqs == 1 and ndp == 16 and span == 512:
        return local_pair(*args, ndp=ndp)
    return local_any(*args)


def solution(mesh):
    in_specs = (
        P("dp", "ctx", None),
        P("dp", None),
        P("dp", "ctx"),
        P("dp", "ctx"),
        P("dp", "ctx", None),
        P(),
        P(),
        P(),
        P(),
        P(),
        P(),
        P(),
        P(),
        P(),
        P(),
    )
    out_specs = (
        P("dp", "ctx", None),
        P("dp", "ctx", None),
        P("dp", None),
        P("dp"),
        P("dp", None),
        P("dp", None),
        P("dp"),
        P("dp", None),
        P("dp"),
        P("dp", None),
        P("dp"),
        P(None, "dp"),
        P("dp"),
    )
    step = functools.partial(local, ndp=mesh.shape["dp"], nctx=mesh.shape["ctx"])
    return jax.shard_map(step, mesh=mesh, in_specs=in_specs, out_specs=out_specs, check_vma=False)
```

```python
import functools

import jax
import jax.numpy as jnp
import numpy as np
from jax import lax
from jax.experimental import pallas as pl
from jax.experimental.pallas import tpu as pltpu
from jax.sharding import PartitionSpec as P

HEADS = 12
HEAD_DIM = 64
EPS = 1e-05
SCORE_SCALE = 0.125
NEG_START = -1e30
F32, BF16 = jnp.float32, jnp.bfloat16
COST = 2e8
MLP_COLS = 1536
BWD_BLK = 512


def dot(a, b):
    return jnp.dot(a, b, preferred_element_type=F32)


def dot_tn(a, b):
    return lax.dot_general(a, b, (((0,), (0,)), ((), ())), preferred_element_type=F32)


def dot_nt(a, b):
    return lax.dot_general(a, b, (((1,), (1,)), ((), ())), preferred_element_type=F32)


def sds(shape, dtype):
    return jax.ShapeDtypeStruct(shape, dtype)


def hbm(x):
    return pltpu.with_memory_space_constraint(x, pltpu.HBM)


class Order:
    def __init__(self, place):
        self.place, self.token = place, None

    def call(
        self, body, args, grid, in_specs, out_specs, out_shape, scratch=(), mb=32, us=1.0, aliases=None, after=(),
        name=None,
    ):
        after = list(after) + ([] if self.token is None else [self.token])
        extra, n_in, n_out = len(after), 1 + len(args), len(out_shape)

        def inner(*refs):
            outs = refs[n_in + extra :]
            body(*refs[:n_in], *outs[:n_out], *outs[n_out + 1 :])

        *outs, self.token = pl.pallas_call(
            inner,
            grid_spec=pltpu.PrefetchScalarGridSpec(
                num_scalar_prefetch=1,
                grid=grid,
                in_specs=list(in_specs) + [ANY] * extra,
                out_specs=list(out_specs) + [ANY],
                scratch_shapes=list(scratch),
            ),
            out_shape=list(out_shape) + [sds((8, 128), F32)],
            input_output_aliases=aliases or {},
            compiler_params=pltpu.CompilerParams(vmem_limit_bytes=mb << 20),
            cost_estimate=pl.CostEstimate(flops=int(us * COST), bytes_accessed=1 << 16, transcendentals=0),
            name=name,
        )(self.place, *args, *after)
        return outs


ANY = pl.BlockSpec(memory_space=pl.ANY)


def whole(shape):
    return pl.BlockSpec(shape, lambda *a: (0,) * len(shape))


def layer_stats(stream):
    row_mean = jnp.mean(stream, axis=-1, keepdims=True)
    centred = stream - row_mean
    variance = jnp.mean(centred * centred, axis=-1, keepdims=True)
    inv = lax.rsqrt(variance + EPS)
    return centred * inv, inv


def swap_lanes(x):
    lane = lax.broadcasted_iota(jnp.int32, x.shape, 1) % HEAD_DIM
    half = HEAD_DIM // 2
    return jnp.where(lane < half, pltpu.roll(x, 128 - half, 1), pltpu.roll(x, half, 1))


def mask_half(value, head):
    lane = lax.broadcasted_iota(jnp.int32, value.shape, 1)
    keep = (lane < HEAD_DIM) if head == 0 else (lane >= HEAD_DIM)
    return jnp.where(keep, value, jnp.zeros_like(value))


def attend_body(
    s_ref, ta_ref, tb_ref, cond_ref, ada_ref, adab_ref, gain_ref, wq_ref, wk_ref, wv_ref, pa_ref, pb_ref, freq_ref,
    cot_ref, abs_ref,
    n1_out, q_out, k_out, v_out, cost_ref, sint_ref,
    out_ref, prob_ref, inv_ref, mod_ref, wtd_ref, scores_ref, top_ref, vt_ref, n1_ref, q_ref, k_ref, v_ref,
):
    pair, step = pl.program_id(0), pl.program_id(1)
    span, width = ta_ref.shape
    blk = out_ref.shape[1]

    @pl.when((pair == 0) & (step == 0))
    def _():
        kept = jnp.broadcast_to(abs_ref[...].astype(F32), (128, span)).T[:, 0:1]
        wtd_ref[...] = (cot_ref[...].astype(F32) * kept).astype(BF16)
        cond = jnp.broadcast_to(cond_ref[...].astype(F32), (16, cond_ref.shape[1])).astype(BF16)
        mod_ref[...] = dot(cond, ada_ref[...])[:8] + adab_ref[...].astype(F32)[None, :]
        shift, scale = mod_ref[0:1, 0:width], mod_ref[0:1, width : 2 * width]
        gain = gain_ref[...].astype(F32)[None, :] * (1.0 + scale)
        for half, (t_ref, p_ref) in enumerate(((ta_ref, pa_ref), (tb_ref, pb_ref))):
            rows = slice(half * span, (half + 1) * span)
            angles = freq_ref[...] * p_ref[...].astype(F32)
            cos_h, sin_h = jnp.cos(angles), jnp.sin(angles)
            cos_t, sin_t = rotation(cos_h, sin_h)
            cost_ref[:, rows] = cos_h
            sint_ref[:, rows] = sin_h
            cos_n, sin_n = cos_t.T, sin_t.T
            a_one, _ = layer_stats(t_ref[...].astype(F32))
            normed = (a_one * gain + shift).astype(BF16)
            n1_ref[rows, :] = a_one.astype(BF16)
            q_pre = dot(normed, wq_ref[...])
            k_pre = dot(normed, wk_ref[...])
            v_ref[rows, :] = dot(normed, wv_ref[...]).astype(BF16)
            for p in range(q_pre.shape[1] // 128):
                at = slice(p * 128, (p + 1) * 128)
                part = q_pre[:, at]
                q_ref[rows, at] = (SCORE_SCALE * (part * cos_n + swap_lanes(part) * sin_n)).astype(BF16)
                part = k_pre[:, at]
                k_ref[rows, at] = (part * cos_n + swap_lanes(part) * sin_n).astype(BF16)

    pairs, blocks = pl.num_programs(0), pl.num_programs(1)
    lanes = lambda p: pl.ds(pl.multiple_of(p * 128, 128), 128)
    piece = jnp.minimum(pair * blocks + step, n1_ref.shape[0] // n1_out.shape[0] - 1)
    n1_out[...] = n1_ref[pl.ds(pl.multiple_of(piece * n1_out.shape[0], 128), n1_out.shape[0]), :]
    length = k_ref.shape[0]
    cut = 512

    def queries(p, i, head):
        return mask_half(q_ref[pl.ds(pl.multiple_of(i * blk, blk), blk), lanes(p)], head)

    def top_rows(scores):
        return jnp.max(scores.reshape(scores.shape[0] // 8, 8, blk), axis=0)

    @pl.when((pair == 0) & (step == 0))
    def _():
        vt_ref[...] = v_ref[...].T
        q_0 = queries(0, 0, 0)
        top = None
        for at in range(0, length, cut):
            scores = dot_nt(k_ref[at : at + cut, 0:128], q_0)
            scores_ref[0, at : at + cut] = scores
            top = top_rows(scores) if top is None else jnp.maximum(top, top_rows(scores))
        top_ref[0] = top

    @pl.when(step == 0)
    def _():
        q_out[...] = q_ref[:, lanes(pair)]
        k_out[...] = k_ref[:, lanes(pair)]
        v_out[...] = v_ref[:, lanes(pair)]

    for head in (0, 1):
        if head == 0:
            next_pair, next_step = pair, step
        else:
            wrap = step == blocks - 1
            next_step = jnp.where(wrap, 0, step + 1)
            next_pair = jnp.minimum(jnp.where(wrap, pair + 1, pair), pairs - 1)
        q_next = queries(next_pair, next_step, 1 - head)
        top = jnp.max(top_ref[head], axis=0, keepdims=True)
        rows = pl.ds(pl.multiple_of(pair * 128 + head * HEAD_DIM, HEAD_DIM), HEAD_DIM)
        next_top = sums = part = None
        for at in range(0, length, cut):
            here = slice(at, at + cut)
            scores = dot_nt(k_ref[here, lanes(next_pair)], q_next)
            scores_ref[1 - head, here] = scores
            new_top = top_rows(scores)
            raised = jnp.exp(scores_ref[head, here] - top)
            new_sums = jnp.sum(raised.reshape(cut // 8, 8, blk), axis=0)
            prob = raised.astype(BF16)
            prob_ref[head, here] = prob
            new_part = dot(vt_ref[rows, here], prob)
            next_top = new_top if next_top is None else jnp.maximum(next_top, new_top)
            sums = new_sums if sums is None else sums + new_sums
            part = new_part if part is None else part + new_part
        top_ref[1 - head] = next_top
        inverse = 1.0 / jnp.sum(sums, axis=0, keepdims=True)
        inv_ref[0, head : head + 1, :] = inverse
        out_ref[head * HEAD_DIM : (head + 1) * HEAD_DIM, :] = (part * inverse).astype(BF16)


def attend_call(order, tok, tok_o, cond, ada, adab, gain, qkv_weight, pos, pos_o, cot, absorbed):
    span, width = tok.shape
    length, hw = 2 * span, width // 2
    pairs, blk = hw // 128, 512
    freq = np.power(10000.0, -np.arange(0, HEAD_DIM, 2) / HEAD_DIM).astype(np.float32)[:, None]
    wspec = lambda j: pl.BlockSpec((width, hw), lambda p, i, s: (0, 2 * j + s[0]))
    col = pl.BlockSpec((length, 128), lambda p, i, s: (0, p))
    return order.call(
        attend_body,
        [hbm(tok), tok_o, hbm(cond), hbm(ada), hbm(adab), hbm(gain), *[hbm(qkv_weight)] * 3, hbm(pos), pos_o, hbm(jnp.asarray(freq)), hbm(cot), hbm(absorbed)],
        (pairs, length // blk),
        [whole(tok.shape), whole(tok.shape), whole(cond.shape), whole(ada.shape), whole(adab.shape), whole(gain.shape), wspec(0), wspec(1), wspec(2),
         whole(pos.shape), whole(pos.shape), whole(freq.shape), whole(cot.shape), whole(absorbed.shape)],
        [pl.BlockSpec((length // 4, width), lambda p, i, s: (jnp.minimum(p * (length // blk) + i, 3), 0)),
         col, col, col, whole((HEAD_DIM // 2, length)), whole((HEAD_DIM // 2, length)),
         pl.BlockSpec((128, blk), lambda p, i, s: (p, i)),
         pl.BlockSpec((2, length, blk), lambda p, i, s: (p, 0, i)),
         pl.BlockSpec((1, 8, blk), lambda p, i, s: (p, 0, i)), whole((8, ada.shape[1])), whole(tok.shape)],
        [sds((length, width), BF16)] + [sds((length, hw), BF16)] * 3
        + [sds((HEAD_DIM // 2, length), F32)] * 2
        + [sds((hw, length), BF16), pltpu.HBM((2 * pairs, length, length), BF16), sds((pairs, 8, length), F32),
           sds((8, ada.shape[1]), F32), sds(tok.shape, BF16)],
        scratch=[pltpu.VMEM((2, length, blk), F32), pltpu.VMEM((2, 8, blk), F32), pltpu.VMEM((hw, length), BF16),
                 pltpu.VMEM((length, width), BF16)] + [pltpu.VMEM((length, hw), BF16)] * 3,
        mb=40, us=20, name="attend",
    )


def swap_rows(x):
    half = HEAD_DIM // 2
    return jnp.concatenate([x[half * j : half * (j + 1)] for j in (1, 0, 3, 2)], axis=0)


def rotation(cos_h, sin_h):
    return jnp.concatenate([cos_h] * 4, axis=0), jnp.concatenate([-sin_h, sin_h, -sin_h, sin_h], axis=0)


def attn_bwd_body(
    r, s_ref, prob_ref, inv_ref, gt_ref, out_ref, q_ref, k_ref, v_ref, cost_ref, sint_ref, a_ref,
    mod_ref, gain_ref, wq_ref, wk_ref, wv_ref,
    g_ref, sum_ref, keep_ref, send_ref, vm_ref, kt_ref, dk_acc, dv_acc, acc_ref,
):
    step = pl.program_id(1)
    blk = q_ref.shape[0]

    @pl.when(step == 0)
    def _():
        values = v_ref[...]
        for head in (0, 1):
            vm_ref[head] = mask_half(values, head)
        kt_ref[...] = k_ref[...].T

    queries = q_ref[...]
    grad_t = gt_ref[...].astype(jnp.float32)
    row_id = lax.broadcasted_iota(jnp.int32, (128, blk), 0)
    inverse = jnp.where(row_id < HEAD_DIM, inv_ref[0, 0:1, :], inv_ref[0, 1:2, :])
    grad_t = grad_t * inverse
    product = grad_t * out_ref[...].astype(jnp.float32)
    grad_b = grad_t.astype(jnp.bfloat16)
    dk_new = None
    dq_parts = []
    for head in (0, 1):
        rows = slice(head * HEAD_DIM, (head + 1) * HEAD_DIM)
        delta = jnp.sum(product[rows], axis=0, keepdims=True)
        keep = (row_id < HEAD_DIM) if head == 0 else (row_id >= HEAD_DIM)
        grad_m = jnp.where(keep, grad_b, jnp.zeros_like(grad_b))
        grad_p = jnp.dot(vm_ref[head], grad_b, preferred_element_type=jnp.float32)
        prob = prob_ref[head]
        grad_s = (prob.astype(jnp.float32) * (grad_p - delta)).astype(jnp.bfloat16)
        dv_h = dot_nt(prob, grad_m)
        dk_h = dot(grad_s, mask_half(queries, head))
        if dk_new is None:
            dk_new, dv_new = dk_h, dv_h
        else:
            dk_new, dv_new = dk_new + dk_h, dv_new + dv_h
        dq_parts.append(dot(kt_ref[rows, :], grad_s) * SCORE_SCALE)
    dq_t = jnp.concatenate(dq_parts, axis=0)
    here = pl.ds(pl.multiple_of(step * blk, blk), blk)
    cos_t, sin_t = rotation(cost_ref[:, here], sint_ref[:, here])
    dq_t = dq_t * cos_t - swap_rows(dq_t) * sin_t
    g_ref[here, 0:128] = dq_t.T.astype(jnp.bfloat16)

    @pl.when(step == 0)
    def _():
        dk_acc[...] = dk_new
        dv_acc[...] = dv_new

    @pl.when(step > 0)
    def _():
        dk_acc[...] += dk_new
        dv_acc[...] += dv_new

    @pl.when(step == pl.num_programs(1) - 1)
    def _():
        dk = dk_acc[...]
        cos_t, sin_t = rotation(cost_ref[...], sint_ref[...])
        g_ref[:, 128:256] = (dk * cos_t.T - swap_lanes(dk) * sin_t.T).astype(jnp.bfloat16)
        g_ref[:, 256:384] = dv_acc[...].astype(jnp.bfloat16)
        grads = g_ref[...]
        product = dot_tn(a_ref[...], grads)
        width = a_ref.shape[1]
        column = lambda row: jnp.broadcast_to(row, (128, width)).T
        gain = column(gain_ref[...].astype(F32)[None, :] * (1.0 + mod_ref[0:1, width : 2 * width]))
        shift = column(mod_ref[0:1, 0:width])
        tokens = jnp.sum(grads.astype(F32), axis=0, keepdims=True)
        high = tokens.astype(BF16)
        low = (tokens - high.astype(F32)).astype(BF16)
        row_id = lax.broadcasted_iota(jnp.int32, (16, 384), 0)
        terms = jnp.where(row_id == 0, high, jnp.where(row_id == 1, low, jnp.zeros_like(high)))
        against = None
        for j, w_ref in enumerate((wq_ref, wk_ref, wv_ref)):
            at = slice(j * 128, (j + 1) * 128)
            part = product[:, at]
            acc_ref[:, at] = (part * gain + shift * tokens[:, at]).astype(BF16)
            weights = w_ref[...]
            scaled = part * weights.astype(F32)
            shifted = dot_nt(terms[:, at], weights)
            against = scaled if against is None else against + scaled
            shifts = shifted if j == 0 else shifts + shifted
        new = jnp.concatenate(
            [jnp.sum(shifts, axis=0, keepdims=True), jnp.sum(against.T, axis=0, keepdims=True)], axis=0
        )

        @pl.when(pl.program_id(0) == 0)
        def _():
            sum_ref[0:2, :] = new

        @pl.when(pl.program_id(0) > 0)
        def _():
            sum_ref[0:2, :] += new

        store_parts(s_ref, acc_ref, r, keep_ref, send_ref)


def attn_bwd(
    order, start, count, prob, inverse, grad_t, out_t, queries, keys, values, cos_t, sin_t, a_one,
    mod, gain, qkv_weight, old, block, blocks,
):
    length = keys.shape[0]
    width = a_one.shape[1]
    hw = width // 2
    wspec = lambda j: pl.BlockSpec((width, 128), lambda p, i, s: (0, (2 * j + s[0]) * (hw // 128) + p + start))
    blk = BWD_BLK
    r = width // 16
    col = pl.BlockSpec((length, 128), lambda p, i, s: (0, p + start))
    rowt = pl.BlockSpec((128, blk), lambda p, i, s: (p + start, i))
    out = pl.BlockSpec((2, 4, r, 384), lambda p, i, s: (0, 0, 0, p + block))
    args = [prob, inverse, grad_t, out_t, queries, keys, values, cos_t, sin_t, a_one, mod, gain, qkv_weight, qkv_weight, qkv_weight]
    aliases = {}
    after = []
    if old is not None:
        aliases = {1 + len(args) + j: 2 + j for j in range(2)}
        after = list(old)
    return order.call(
        functools.partial(attn_bwd_body, r), args, (count, length // blk),
        [
            pl.BlockSpec((2, length, blk), lambda p, i, s: (p + start, 0, i)),
            pl.BlockSpec((1, 8, blk), lambda p, i, s: (p + start, 0, i)),
            rowt, rowt,
            pl.BlockSpec((blk, 128), lambda p, i, s: (i, p + start)),
            col, col, whole(cos_t.shape), whole(cos_t.shape), whole(a_one.shape),
            whole(mod.shape), whole(gain.shape), wspec(0), wspec(1), wspec(2),
        ],
        [pl.BlockSpec((length, 384), lambda p, i, s: (0, p)), whole((8, width))] + [out] * 2,
        [sds((length, 384 * count), BF16), sds((8, width), F32)] + [sds((2, 4, r, 384 * blocks), BF16)] * 2,
        scratch=[
            pltpu.VMEM((2, length, 128), BF16),
            pltpu.VMEM((128, length), BF16),
            pltpu.VMEM((length, 128), F32),
            pltpu.VMEM((length, 128), F32),
            pltpu.VMEM((width, 384), BF16),
        ],
        mb=36, us=8.0 * count, aliases=aliases, after=after, name="attn_bwd",
    )


def mix_body(s_ref, own_ref, got_ref, mid_ref, mod_ref, bias_ref, out_ref):
    width = mid_ref.shape[1]
    branch = own_ref[...] + got_ref[...].astype(F32) + bias_ref[...].astype(F32)[None, :]
    out_ref[...] = (mid_ref[...] + mod_ref[0:1, 5 * width : 6 * width] * branch).astype(BF16)


def mix_call(order, own, got, mid, mod, bias):
    span, width = mid.shape
    blk = 256
    row = pl.BlockSpec((blk, width), lambda i, s: (i, 0))
    return order.call(
        mix_body, [own, got, mid, mod, bias], (span // blk,),
        [row] * 3 + [whole(mod.shape), whole(bias.shape)],
        [row], [sds((span, width), BF16)], mb=12, us=2.5, name="mix",
    )[0]


def post_body(s_ref, att_ref, oth_ref, wm_ref, wo_ref, tok_ref, mod_ref, gain_ref, mid_ref, br_ref, n2_ref):
    width = tok_ref.shape[1]
    branch = dot_tn(att_ref[...], wm_ref[...]) + dot_tn(oth_ref[...], wo_ref[...])
    br_ref[...] = branch
    middle = tok_ref[...].astype(F32) + mod_ref[0:1, 2 * width : 3 * width] * branch
    mid_ref[...] = middle
    a_two, _ = layer_stats(middle)
    scale = mod_ref[0:1, 4 * width : 5 * width]
    n2_ref[...] = (
        a_two * (gain_ref[...].astype(F32)[None, :] * (1.0 + scale)) + mod_ref[0:1, 3 * width : 4 * width]
    ).astype(BF16)


def post_call(order, att_t, att_o, out_weight, tok, mod, gain):
    span, width = tok.shape
    hw = width // 2
    blk = 512
    n = span // blk
    row = pl.BlockSpec((blk, width), lambda i, s: (i, 0))
    return order.call(
        post_body, [att_t, att_o, out_weight, out_weight, tok, mod, gain], (n,),
        [
            pl.BlockSpec((hw, blk), lambda i, s: (0, i)),
            pl.BlockSpec((hw, blk), lambda i, s: (0, i + n)),
            pl.BlockSpec((hw, width), lambda i, s: (s[0], 0)),
            pl.BlockSpec((hw, width), lambda i, s: (1 - s[0], 0)),
            row, whole(mod.shape), whole(gain.shape),
        ],
        [row, row, row],
        [sds((span, width), F32), sds((span, width), F32), sds((span, width), BF16)],
        mb=12, us=3, name="post",
    )


def mlp_body(
    s_ref, n2a_ref, n2b_ref, wa_ref, wb_ref, mod_ref, w1_ref, b1_ref, w2_ref,
    hid_ref, pre_ref, b1g_ref, b2g_ref,
):
    step = pl.program_id(0)
    first = step < pl.num_programs(0) // 2
    width = n2a_ref.shape[1]
    x = jnp.where(first, n2a_ref[...], n2b_ref[...])
    wtd = jnp.where(first, wa_ref[...], wb_ref[...]).astype(F32)
    g_mlp = (wtd * mod_ref[0:1, 5 * width : 6 * width]).astype(BF16)
    bias = b1_ref[...].astype(F32)[None, :]
    hf = w1_ref.shape[1]
    bias = jnp.where(s_ref[0] == 0, bias[:, :hf], bias[:, hf:])
    c0 = 0.7978845608028654
    c1 = c0 * 0.044715
    parts = []
    for at in range(0, hf, MLP_COLS):
        cols = slice(at, at + MLP_COLS)
        v = dot(x, w1_ref[:, cols]) + bias[:, cols]
        gh = dot_nt(g_mlp, w2_ref[cols, :])
        v2 = v * v
        th = jnp.tanh(v * (c0 + c1 * v2))
        up = 0.5 + 0.5 * th
        hid_ref[:, cols] = (v * up).astype(BF16)
        slope = up + v * (0.5 - 0.5 * (th * th)) * (c0 + 3.0 * c1 * v2)
        pre = (gh * slope).astype(BF16)
        pre_ref[:, cols] = pre
        parts.append(jnp.sum(pre.astype(F32), axis=0, keepdims=True))
    b1_part = jnp.concatenate(parts, axis=1)
    b2_part = jnp.sum(g_mlp.astype(F32), axis=0, keepdims=True)

    @pl.when(step == 0)
    def _():
        b1g_ref[...] = b1_part
        b2g_ref[...] = b2_part

    @pl.when(step > 0)
    def _():
        b1g_ref[...] += b1_part
        b2g_ref[...] += b2_part


def halves(blk, width, n):
    return [
        pl.BlockSpec((blk, width), lambda i, s: (jnp.minimum(i, n - 1), 0)),
        pl.BlockSpec((blk, width), lambda i, s: (jnp.maximum(i - n, 0), 0)),
    ]


def mlp_call(order, n2a, n2b, wa, wb, mod, w1, b1, w2):
    span, width = n2a.shape
    hf = w1.shape[1] // 2
    blk = 512
    n = span // blk
    row = lambda w: pl.BlockSpec((blk, w), lambda i, s: (i, 0))
    return order.call(
        mlp_body, [n2a, n2b, wa, wb, mod, w1, b1, w2], (2 * n,),
        halves(blk, width, n) + halves(blk, width, n)
        + [
            whole(mod.shape),
            pl.BlockSpec((width, hf), lambda i, s: (0, s[0])),
            whole(b1.shape),
            pl.BlockSpec((hf, width), lambda i, s: (s[0], 0)),
        ],
        [row(hf), row(hf), whole((1, hf)), whole((1, width))],
        [sds((2 * span, hf), BF16), sds((2 * span, hf), BF16),
         sds((1, hf), F32), sds((1, width), F32)],
        mb=24, us=9.6, name="mlp",
    )


def store_parts(s_ref, acc_ref, r, keep_ref, send_ref):
    for i in range(8):
        rest = sum(((i >> (2 - j)) & 1) * s_ref[6 + j] for j in range(3))
        for ref, bit in ((keep_ref, s_ref[1]), (send_ref, 1 - s_ref[1])):
            at = pl.ds(pl.multiple_of((rest + bit * s_ref[5]) * r, 16), r)
            ref[i // 4, i % 4] = acc_ref[at, :]


def wgrad_body(r, s_ref, la_ref, lb_ref, g_ref, keep_ref, send_ref, acc_ref):
    span = la_ref.shape[0]
    acc_ref[...] = (dot_tn(la_ref[...], g_ref[:span]) + dot_tn(lb_ref[...], g_ref[span:])).astype(BF16)
    store_parts(s_ref, acc_ref, r, keep_ref, send_ref)


def wgrad_call(order, left_a, left_b, right, blk):
    rows, cols = left_a.shape[1], right.shape[1]
    length = right.shape[0]
    r = rows // 16
    out = pl.BlockSpec((2, 4, r, blk), lambda i, s: (0, 0, 0, i))
    return order.call(
        functools.partial(wgrad_body, r), [left_a, left_b, right], (cols // blk,),
        [whole(left_a.shape), whole(left_b.shape), pl.BlockSpec((length, blk), lambda i, s: (0, i))],
        [out] * 2, [sds((2, 4, r, cols), BF16)] * 2,
        scratch=[pltpu.VMEM((rows, blk), BF16)], mb=16, us=4.2, name="wgrad_fc1",
    )


def wgrad2_body(
    r, s_ref, lm_ref, lo_ref, wa_ref, wb_ref, mod_ref, w2_ref, bias_ref, keep_ref, send_ref, gate_ref, acc_ref
):
    step, n = pl.program_id(0), pl.num_programs(0)
    mine = lax.div(step, n // 2) == s_ref[0]
    span, half = wa_ref.shape
    width = 2 * half
    here = pl.ds(pl.multiple_of(s_ref[0] * half, 128), half)
    own, oth = wa_ref[...], wb_ref[...]

    @pl.when(mine)
    def _():
        acc_ref[...] = dot_tn(lm_ref[:span], own) + dot_tn(lm_ref[span:], oth)

    @pl.when(jnp.logical_not(mine))
    def _():
        acc_ref[...] = dot_tn(lo_ref[:span], oth) + dot_tn(lo_ref[span:], own)

    part = jnp.sum(acc_ref[...] * w2_ref[...].astype(F32), axis=0, keepdims=True)

    @pl.when(step == 0)
    def _():
        tokens = jnp.sum(own.astype(F32), axis=0, keepdims=True) + jnp.sum(oth.astype(F32), axis=0, keepdims=True)
        bias = bias_ref[...].astype(F32)[None, :]
        gate_ref[...] = part + tokens * jnp.where(s_ref[0] == 0, bias[:, :half], bias[:, half:])

    @pl.when(step > 0)
    def _():
        gate_ref[...] += part

    gate = mod_ref[0:1, pl.ds(pl.multiple_of(5 * width + s_ref[0] * half, 128), half)]
    za, zb = lax.div(step, 2), lax.rem(step, 2)
    slot = jnp.where(s_ref[0] == 0, zb * 2 + za, za * 2 + zb)
    for other in range(2):
        for ref, bit in ((keep_ref, s_ref[1]), (send_ref, 1 - s_ref[1])):
            at = pl.ds(pl.multiple_of((other * s_ref[6] + bit * s_ref[5]) * r, 16), r)
            ref[other, slot] = (acc_ref[at, :] * gate).astype(BF16)


def wgrad2_call(order, hidden, hidden_o, wa, wb, mod, w2, bias):
    length, hf = hidden.shape
    span, width = wa.shape
    hw = width // 2
    r = hf // 8
    left = lambda first: pl.BlockSpec((length, 4 * r), lambda i, s: (0, jnp.clip(i - first(s[0]), 0, 1)))
    cols = pl.BlockSpec((span, hw), lambda i, s: (0, s[0]))
    return order.call(
        functools.partial(wgrad2_body, r), [hidden, hidden_o, wa, wb, mod, w2, bias], (4,),
        [left(lambda c: 2 * c), left(lambda c: 2 - 2 * c), cols, cols, whole(mod.shape), pl.BlockSpec((4 * r, hw), lambda i, s: (i, s[0])), whole(bias.shape)],
        [whole((2, 4, r, hw))] * 2 + [whole((1, hw))], [sds((2, 4, r, hw), BF16)] * 2 + [sds((1, hw), F32)],
        scratch=[pltpu.VMEM((4 * r, hw), F32)], mb=16, us=4.5, name="wgrad_fc2",
    )


def fold_body(s_ref, ka, ra, ks, rs, away_ref, stay_ref):
    away_ref[...] = ka[0] + ra[0]
    stay_ref[...] = ks[0] + rs[0]


def fold_call(order, step, keep, got):
    _, count, r, n = keep.shape
    blk = 768 if n % 768 == 0 else 384
    away = pl.BlockSpec((1, count, r, blk), lambda i, s: (1 - s[step], 0, 0, i))
    stay = pl.BlockSpec((1, count, r, blk), lambda i, s: (s[step], 0, 0, i))
    out = pl.BlockSpec((count, r, blk), lambda i, s: (0, 0, i))
    return order.call(
        fold_body, [keep, got, keep, got], (n // blk,), [away, away, stay, stay], [out] * 2,
        [sds((count, r, n), BF16)] * 2, mb=8, us=1.2, name="fold",
    )


def join_ff_body(s_ref, ka_ref, ga_ref, ks_ref, gs_ref, away_in, stay_in, away_ref, stay_ref):
    r = away_in.shape[1]
    width = ka_ref.shape[3]
    for out, one, k_ref, g_ref in ((away_ref, away_in, ka_ref, ga_ref), (stay_ref, stay_in, ks_ref, gs_ref)):
        out[:, :r] = one[...]
        two = k_ref[0] + g_ref[0]
        for q in range(two.shape[1] // r):
            out[:, r:, q * width : (q + 1) * width] = two[:, q * r : (q + 1) * r]


def join_ff_call(order, step, one, two):
    keep, got = two
    away_in, stay_in = one
    specs = []
    for away in (True, False):
        pick = (lambda i, s: (1 - s[step], 0, 0, 0)) if away else (lambda i, s: (s[step], 0, 0, 0))
        specs += [pl.BlockSpec((1,) + keep.shape[1:], pick)] * 2
    count, r, n = away_in.shape
    shape = (count, 2 * r, n)
    return order.call(
        join_ff_body, [keep, got, keep, got, away_in, stay_in], (1,),
        specs + [whole(away_in.shape)] * 2, [whole(shape)] * 2, [sds(shape, BF16)] * 2, mb=12, us=1.2, name="fold_ff",
    )


def relay(step, mine, keep, got):
    sources, rest = 2 ** (step - 2), 2 ** (4 - step)
    stay, away = [], []
    for read in (keep, got):
        for src in range(sources):
            both = [[read(src * 2 * rest + bit * rest + k) for k in range(rest)] for bit in range(2)]
            for k in range(rest):
                stay.append(jnp.where(mine == 0, both[0][k], both[1][k]))
                away.append(jnp.where(mine == 0, both[1][k], both[0][k]))
    return stay, away


def paired(packets):
    return [jnp.concatenate(packets[q : q + 2], axis=0).astype(BF16) for q in range(0, 8, 2)]


def single(pair):
    pairs = [pair(q).astype(F32) for q in range(4)]
    return lambda slot: pairs[slot // 2][(slot % 2) * 8 : (slot % 2) * 8 + 8]


def fold_last_body(s_ref, keep_ref, got_ref, sk_ref, sg_ref, away_ref, stay_ref, small_ref):
    mine = s_ref[2]
    r = keep_ref.shape[2]
    away_ref[:, :r] = keep_ref[1 - mine] + got_ref[1 - mine]
    stay_ref[...] = keep_ref[mine] + got_ref[mine]
    stay, away = relay(2, mine, lambda k: sk_ref[k], lambda k: sg_ref[k])
    for k in range(8):
        small_ref[k] = stay[k]
    for q, pair in enumerate(paired(away)):
        away_ref[q, r : r + 16] = pair


def fold_last_call(order, keep, got, small_keep, small_got):
    _, count, r, n = keep.shape
    args = [keep, got, small_keep, small_got]
    shapes = [((count, r + 16, n), BF16), ((count, r, n), BF16), (small_keep.shape, F32)]
    return order.call(
        fold_last_body, args, (1,), [whole(a.shape) for a in args], [whole(x) for x, _ in shapes],
        [sds(*x) for x in shapes], mb=14, us=1.2, name="fold_last",
    )


def fold_att_body(s_ref, k1_ref, g1_ref, k2_ref, g2_ref, sk_ref, away_ref, stay_ref, small_ref):
    mine = s_ref[3]
    count, r, n = k1_ref.shape[1:]
    for out, at in ((away_ref, 1 - mine), (stay_ref, mine)):
        for j in range(count):
            out[j * r : (j + 1) * r, :n] = k1_ref[at, j] + g1_ref[at, j]
            out[j * r : (j + 1) * r, n:] = k2_ref[at, j] + g2_ref[at * count + j, :r]
    got = single(lambda q: g2_ref[q, r : r + 16])
    stay, away = relay(3, mine, lambda k: sk_ref[k], got)
    for k in range(8):
        small_ref[k] = stay[k]
    w = sk_ref.shape[2]
    for q, pair in enumerate(paired(away)):
        away_ref[count * r :, q * w : (q + 1) * w] = pair


def fold_att_call(order, one, two, got, small_keep):
    _, count, r, n = one[0].shape
    full = n + two.shape[3]
    args = [*one, two, got, small_keep]
    shapes = [((count * r + 16, full), BF16), ((count * r, full), BF16), (small_keep.shape, F32)]
    return order.call(
        fold_att_body, args, (1,), [whole(a.shape) for a in args], [whole(x) for x, _ in shapes],
        [sds(*x) for x in shapes], mb=14, us=1.2, name="fold_att",
    )


def fold_end_body(s_ref, keep_ref, got_ref, sk_ref, away_ref, stay_ref, small_ref):
    mine = s_ref[4]
    r = stay_ref.shape[0]
    for out, at in ((away_ref, 1 - mine), (stay_ref, mine)):
        rows = pl.ds(pl.multiple_of(at * r, 16), r)
        out[:r] = keep_ref[rows] + got_ref[rows]
    w = sk_ref.shape[2]
    got = single(lambda q: got_ref[2 * r :, q * w : (q + 1) * w])
    stay, away = relay(4, mine, lambda k: sk_ref[k], got)
    for k in range(8):
        small_ref[k] = stay[k]
    for q, pair in enumerate(paired(away)):
        away_ref[r:, q * w : (q + 1) * w] = pair


def fold_end_call(order, keep, got, small_keep):
    r, n = keep.shape[0] // 2, keep.shape[1]
    args = [keep, got, small_keep]
    shapes = [((r + 16, n), BF16), ((r, n), BF16), (small_keep.shape, F32)]
    return order.call(
        fold_end_body, args, (1,), [whole(a.shape) for a in args], [whole(x) for x, _ in shapes],
        [sds(*x) for x in shapes], mb=14, us=1.2, name="fold_end",
    )


def add_body(s_ref, a_ref, b_ref, out_ref):
    out_ref[...] = a_ref[...] + b_ref[: out_ref.shape[0]]


def add_call(order, a, b):
    return order.call(
        add_body, [a, b], (1,), [whole(a.shape), whole(b.shape)], [whole(a.shape)], [sds(a.shape, BF16)], mb=8, us=1.0, name="add"
    )[0]


def place_ff_body(s_ref, mine_ref, other_ref, fc1_ref, fc2_ref):
    core = s_ref[0]
    r, n = fc1_ref.shape[0], mine_ref.shape[1]
    width = fc2_ref.shape[1] // 2
    for ref, at in ((mine_ref, core), (other_ref, 1 - core)):
        fc1_ref[:, pl.ds(pl.multiple_of(at * n, 128), n)] = ref[:r].astype(F32)
        cols = pl.ds(pl.multiple_of(at * width, 128), width)
        for q in range(n // width):
            fc2_ref[q * r : (q + 1) * r, cols] = ref[r:, q * width : (q + 1) * width].astype(F32)


def place_ff_call(order, mine, other, hw):
    r, n = mine.shape[0] // 2, mine.shape[1]
    shapes = [(r, 2 * n), (r * (n // hw), 2 * hw)]
    return order.call(
        place_ff_body, [mine, other], (1,), [whole(mine.shape)] * 2, [whole(x) for x in shapes],
        [sds(x, F32) for x in shapes], mb=8, us=1.0, name="place_ff",
    )


def place_att_body(s_ref, mine_ref, other_ref, out_ref, qkv_ref):
    core = s_ref[0]
    width = out_ref.shape[1]
    hw = width // 2
    for ref, at in ((mine_ref, core), (other_ref, 1 - core)):
        out_ref[:, pl.ds(pl.multiple_of(at * hw, 128), hw)] = ref[:, :hw].astype(F32)
        for p in range(hw // 128):
            for j in range(3):
                to = pl.ds(pl.multiple_of(j * width + at * hw + p * 128, 128), 128)
                src = hw + p * 384 + j * 128
                qkv_ref[:, to] = ref[:, src : src + 128].astype(F32)


def place_att_call(order, mine, other, width):
    r = mine.shape[0]
    shapes = [(r, width), (r, 3 * width)]
    return order.call(
        place_att_body, [mine, other], (1,), [whole(mine.shape)] * 2, [whole(x) for x in shapes],
        [sds(x, F32) for x in shapes], mb=8, us=1.0, name="place_att",
    )


def pack_body(
    s_ref, s1a_ref, s1b_ref, s2_ref, gate_ref, b1_ref, b2_ref, g1_ref, g2_ref, mod_ref, cond_ref, out_ref
):
    width = s2_ref.shape[1]
    h = width // 2
    core = s_ref[0]
    mine = jnp.where(core == 0, 1.0, 0.0)
    gain_one, gain_two = g1_ref[...].astype(F32)[None, :], g2_ref[...].astype(F32)[None, :]
    scale_one = 1.0 + mod_ref[0:1, width : 2 * width]
    scale_two = 1.0 + mod_ref[0:1, 4 * width : 5 * width]
    second_one, second_two = s1a_ref[1:2, :] + s1b_ref[1:2, :], s2_ref[1:2, :]
    gate = jnp.concatenate([gate_ref[...] * mine, gate_ref[...] * (1.0 - mine)], axis=1)
    flat = jnp.concatenate(
        [
            s1a_ref[0:1, :] + s1b_ref[0:1, :], second_one * gain_one, s2_ref[2:3, :],
            s2_ref[0:1, :], second_two * gain_two, gate,
        ],
        axis=1,
    )
    b1 = jnp.concatenate([b1_ref[...] * mine, b1_ref[...] * (1.0 - mine)], axis=1)
    sources = (flat, b1, second_one * scale_one, second_two * scale_two, 0.5 * b2_ref[...])
    out_ref[...] = jnp.zeros_like(out_ref)
    cond = 0.5 * cond_ref[...].astype(F32)
    ndp = out_ref.shape[0] - 2
    for d in range(ndp):
        for j, source in enumerate(sources):
            n = source.shape[1] // ndp
            out_ref[d, j : j + 1, 0:n] = source[:, d * n : (d + 1) * n]
        out_ref[d, 5:6, 0:128] = cond
    for j in range(12):
        out_ref[ndp + j // 8, j % 8 : j % 8 + 1, :] = flat[:, j * h : (j + 1) * h]


def pack_call(order, *args):
    h = args[2].shape[1] // 2
    shape = (18, 8, h)
    return order.call(
        pack_body, list(args), (1,), [whole(a.shape) for a in args], [whole(shape)], [sds(shape, F32)],
        mb=8, us=1.0, name="pack",
    )[0]


def deal_body(s_ref, a_ref, b_ref, ada_ref, cg_ref, keep_ref, send_ref, acc_ref):
    acc_ref[...] = a_ref[...] + b_ref[...]
    for i in range(8):
        rest = sum(((i >> (2 - j)) & 1) * s_ref[6 + j] for j in range(3))
        keep_ref[i] = acc_ref[rest + s_ref[1] * s_ref[5]]
        send_ref[i] = acc_ref[rest + (1 - s_ref[1]) * s_ref[5]]
    flat = jnp.concatenate([acc_ref[16 + j // 8, j % 8 : j % 8 + 1, :] for j in range(12)], axis=1)
    high = flat.astype(BF16)
    rest = flat - high.astype(F32)
    mid = rest.astype(BF16)
    low = (rest - mid.astype(F32)).astype(BF16)
    row_id = lax.broadcasted_iota(jnp.int32, (16, flat.shape[1]), 0)
    zero = jnp.zeros_like(high)
    terms = jnp.where(row_id == 0, high, jnp.where(row_id == 1, mid, jnp.where(row_id == 2, low, zero)))
    cg_ref[...] = jnp.sum(dot_nt(terms, ada_ref[...]), axis=0, keepdims=True)


def deal_call(order, mine, got, ada):
    shape = (8,) + mine.shape[1:]
    return order.call(
        deal_body, [mine, got, ada], (1,), [whole(mine.shape), whole(mine.shape), whole(ada.shape)],
        [whole((1, ada.shape[0])), whole(shape), whole(shape)],
        [sds((1, ada.shape[0]), F32), sds(shape, F32), sds(shape, F32)],
        scratch=[pltpu.VMEM(mine.shape, F32)], mb=8, us=1.0, name="deal",
    )


def last_body(s_ref, got_ref, sk_ref, ada_ref, adab_ref, b1_ref, g1_ref, g2_ref, b2_ref):
    r, w = got_ref.shape[0] - 16, sk_ref.shape[2]
    got = single(lambda q: got_ref[r:, q * w : (q + 1) * w])
    parts = [sk_ref[k] for k in range(8)] + [got(k) for k in range(8)]
    sums = parts[0]
    for part in parts[1:]:
        sums = sums + part
    cond = jnp.concatenate([part[5:6, 0:128] for part in parts], axis=0)
    grads = jnp.concatenate([part[0:1] for part in parts], axis=0)
    ada = lax.dot_general(
        cond, grads, (((0,), (0,)), ((), ())), precision=lax.Precision.HIGHEST, preferred_element_type=F32
    )
    ada_ref[...] = ada[:, : ada_ref.shape[1]]
    for j, ref in enumerate((adab_ref, b1_ref, g1_ref, g2_ref, b2_ref)):
        ref[...] = sums[j : j + 1, : ref.shape[1]]


def last_call(order, got, small_keep, ndp):
    h = small_keep.shape[2]
    na, nb, nc = 12 * h // ndp, 2 * h // ndp, 8 * h // ndp
    shapes = [(128, na), (1, na), (1, nc), (1, nb), (1, nb), (1, nb)]
    args = [got, small_keep]
    return order.call(
        last_body, args, (1,), [whole(a.shape) for a in args], [whole(x) for x in shapes],
        [sds(x, F32) for x in shapes], mb=8, us=1.0, name="small_last",
    )


def part_body(nt, s_ref, g_ref, w_ref, own_ref, oth_ref):
    step = pl.program_id(0)
    half = pl.num_programs(0) // 2
    part = dot_nt(g_ref[...], w_ref[...]) if nt else dot(g_ref[...], w_ref[...])

    @pl.when(step < half)
    def _():
        oth_ref[...] = part.astype(BF16)

    @pl.when(step >= half)
    def _():
        own_ref[...] = part


def part_call(order, nt, g, w):
    length, hf = g.shape
    width = w.shape[0] if nt else w.shape[1]
    blk = 512
    n = length // 2 // blk
    wspec = (
        pl.BlockSpec((width, hf), lambda i, s: (0, s[0]))
        if nt
        else pl.BlockSpec((hf, width), lambda i, s: (s[0], 0))
    )
    return order.call(
        functools.partial(part_body, nt), [g, w], (2 * n,),
        [pl.BlockSpec((blk, hf), lambda i, s: ((i + n) % (2 * n), 0)), wspec],
        [
            pl.BlockSpec((blk, width), lambda i, s: (jnp.maximum(i - n, 0), 0)),
            pl.BlockSpec((blk, width), lambda i, s: (jnp.minimum(i, n - 1), 0)),
        ],
        [sds((length // 2, width), F32), sds((length // 2, width), BF16)],
        mb=12, us=4.2, name="part",
    )


def norm2_body(s_ref, own_ref, got_ref, mid_ref, br_ref, wtd_ref, mod_ref, gain_ref, gmid_ref, gatt_ref, sum_ref):
    width = mid_ref.shape[1]
    g = own_ref[...] + got_ref[...].astype(F32)
    a_two, inv = layer_stats(mid_ref[...])
    ga = g * (gain_ref[...].astype(F32)[None, :] * (1.0 + mod_ref[0:1, 4 * width : 5 * width]))
    gaa = ga * a_two
    g_mid = wtd_ref[...].astype(F32) + inv * (
        ga - jnp.mean(ga, -1, keepdims=True) - a_two * jnp.mean(gaa, -1, keepdims=True)
    )
    gmid_ref[...] = g_mid
    gatt_ref[...] = (g_mid * mod_ref[0:1, 2 * width : 3 * width]).astype(BF16)
    sums = jnp.concatenate(
        [
            jnp.sum(g, axis=0, keepdims=True),
            jnp.sum(g * a_two, axis=0, keepdims=True),
            jnp.sum(g_mid * br_ref[...], axis=0, keepdims=True),
        ],
        axis=0,
    )

    @pl.when(pl.program_id(0) == 0)
    def _():
        sum_ref[...] = jnp.zeros_like(sum_ref)

    sum_ref[0:3, :] += sums


def norm2_call(order, own, got, mid, br, wtd, mod, gain):
    span, width = mid.shape
    blk = 512
    row = pl.BlockSpec((blk, width), lambda i, s: (i, 0))
    return order.call(
        norm2_body, [own, got, mid, br, wtd, mod, gain], (span // blk,),
        [row] * 5 + [whole(mod.shape), whole(gain.shape)],
        [row, row, whole((8, width))],
        [sds((span, width), F32), sds((span, width), BF16), sds((8, width), F32)],
        mb=12, us=3, name="norm2",
    )


def oproj_body(r, s_ref, w_ref, ga_ref, gb_ref, am_ref, ao_ref, gt_ref, keep_ref, send_ref, acc_ref):
    span = ga_ref.shape[0]
    half = am_ref.shape[0]
    core = s_ref[0]
    w = w_ref[...]
    gt_ref[:, :span] = dot_nt(w, ga_ref[...]).astype(BF16)
    gt_ref[:, span:] = dot_nt(w, gb_ref[...]).astype(BF16)
    cols = pl.ds(pl.multiple_of(core * half, 128), half)
    gac, gbc = ga_ref[:, cols], gb_ref[:, cols]
    mine = dot(am_ref[:, :span], gac) + dot(am_ref[:, span:], gbc)
    other = dot(ao_ref[:, span:], gac) + dot(ao_ref[:, :span], gbc)
    acc_ref[pl.ds(pl.multiple_of(core * half, 16), half), :] = mine.astype(BF16)
    acc_ref[pl.ds(pl.multiple_of((1 - core) * half, 16), half), :] = other.astype(BF16)
    store_parts(s_ref, acc_ref, r, keep_ref, send_ref)


def oproj_call(order, blocks, out_weight, ga, gb, att_t, att_o):
    span, width = ga.shape
    hw = width // 2
    r = width // 16
    out = pl.BlockSpec((2, 4, r, hw), lambda i, s: (0, 0, 0, 0))
    return order.call(
        functools.partial(oproj_body, r), [out_weight, ga, gb, att_t, att_o], (1,),
        [pl.BlockSpec((hw, width), lambda i, s: (s[0], 0)), whole(ga.shape), whole(ga.shape),
         whole(att_t.shape), whole(att_t.shape)],
        [whole((hw, 2 * span))] + [out] * 2,
        [sds((hw, 2 * span), BF16)] + [sds((2, 4, r, blocks * hw), BF16)] * 2,
        scratch=[pltpu.VMEM((width, hw), BF16)], mb=8, us=3, name="oproj",
    )


def norm1_body(s_ref, own_ref, got_ref, tok_ref, gmid_ref, mod_ref, gain_ref, out_ref):
    width = tok_ref.shape[1]
    g = own_ref[...] + got_ref[...].astype(F32)
    a_one, inv = layer_stats(tok_ref[...].astype(F32))
    ga = g * (gain_ref[...].astype(F32)[None, :] * (1.0 + mod_ref[0:1, width : 2 * width]))
    gaa = ga * a_one
    out_ref[...] = (
        gmid_ref[...]
        + inv * (ga - jnp.mean(ga, -1, keepdims=True) - a_one * jnp.mean(gaa, -1, keepdims=True))
    ).astype(BF16)


def norm1_call(order, own, got, tok, gmid, mod, gain):
    span, width = tok.shape
    blk = 256
    row = pl.BlockSpec((blk, width), lambda i, s: (i, 0))
    return order.call(
        norm1_body, [own, got, tok, gmid, mod, gain], (span // blk,),
        [row] * 4 + [whole(mod.shape), whole(gain.shape)], [row], [sds((span, width), BF16)],
        mb=12, us=3, name="norm1",
    )[0]


def dgrad_body(np_, s_ref, *refs):
    gs, (wq_ref, wk_ref, wv_ref), out_ref = refs[:np_], refs[np_ : np_ + 3], refs[np_ + 3]
    total = None
    for j, w_ref in enumerate((wq_ref, wk_ref, wv_ref)):
        left = jnp.concatenate(
            [g[:, at + j * 128 : at + (j + 1) * 128] for g in gs for at in range(0, g.shape[1], 384)], axis=1
        )
        part = dot_nt(left, w_ref[...])
        total = part if total is None else total + part
    out_ref[...] = total.astype(out_ref.dtype)


def dgrad_call(order, gs, qkv_weight, half):
    span = gs[0].shape[0] // 2
    width = qkv_weight.shape[0]
    hw = width // 2
    wspec = lambda j: pl.BlockSpec((width, hw), lambda i, s: (0, 2 * j + s[0]))
    return order.call(
        functools.partial(dgrad_body, len(gs)), [*gs, qkv_weight, qkv_weight, qkv_weight], (1,),
        [pl.BlockSpec((span, g.shape[1]), lambda i, s: (half, 0)) for g in gs] + [wspec(0), wspec(1), wspec(2)],
        [whole((span, width))], [sds((span, width), BF16 if half else F32)], mb=12, us=2.0, name="dgrad",
    )[0]


class Grid:
    ORDERS = ((1, 2, 4, 8), (2, 1, 8, 4))

    def __init__(self, ndp):
        self.index = lax.axis_index("dp")
        core = lax.axis_index("ctx")
        self.flip = lambda mask: [(i, i ^ mask) for i in range(ndp)]
        masks = [jnp.where(core == 0, a, b) for a, b in zip(*self.ORDERS)]
        bits = [jnp.where((self.index & m) > 0, 1, 0) for m in masks]
        self.place = jnp.stack([core, *bits, *masks, self.index // 4, self.index]).astype(jnp.int32)
        self.pairs = [
            [(2 * i + c, 2 * (i ^ self.ORDERS[c][step]) + c) for i in range(ndp) for c in range(2)] for step in range(4)
        ]


class Job:
    def __init__(self, pairs):
        self.pairs, self.step = pairs, 0

    def start(self, keep, send):
        self.keep = keep
        self.got = lax.ppermute(send, ("dp", "ctx"), self.pairs[self.step])
        self.step += 1

    def parts(self):
        shape = self.keep.shape
        if self.step > 1:
            shape = (2, shape[0] // 2) + shape[1:]
        return self.keep.reshape(shape), self.got.reshape(shape)

    def fold(self, order):
        away, stay = self.split(order)
        self.start(stay, away)

    def split(self, order):
        return fold_call(order, self.step + 1, *self.parts())

    def last(self):
        return self.keep[0], self.got[0]


def join(order, fold, one, two):
    job = Job(two.pairs)
    job.step = two.step
    away, stay = fold(order, job.step + 1, one if isinstance(one, tuple) else one.parts(), two.parts())
    job.start(stay, away)
    return job


def local_pair(
    tokens_in, cond_vec, positions, absorbed, cotangent, norm1_gain, qkv_weight, out_weight,
    norm2_gain, fc1_weight, fc1_bias, fc2_weight, fc2_bias, ada_weight, ada_bias, *, ndp,
):
    _, span, width = tokens_in.shape
    hw = width // 2
    grid = Grid(ndp)
    order = Order(grid.place)
    swap = lambda v: lax.ppermute(v, "ctx", [(0, 1), (1, 0)])

    tok = tokens_in[0]
    tok_o = swap(tok)
    pos_o = swap(positions)

    a_one, queries, keys, values, cos_t, sin_t, att_t, prob, inverse, mod, wtd = attend_call(
        order, tok, tok_o, cond_vec, ada_weight, ada_bias, norm1_gain, qkv_weight, positions, pos_o,
        cotangent[0], absorbed,
    )
    wtd_o = swap(wtd)
    att_o = swap(att_t)
    middle, branch, n2 = post_call(order, att_t, att_o, out_weight, hbm(tok), mod, norm2_gain)
    n2_o = swap(n2)
    hidden, g_pre, b1_sum, b2_sum = mlp_call(
        order, n2, n2_o, wtd, wtd_o, mod, fc1_weight, fc1_bias, fc2_weight
    )
    hidden_o = swap(hidden)
    fc1, fc2, rest, last = (Job(grid.pairs) for _ in range(4))
    fc1.start(*wgrad_call(order, n2, n2_o, g_pre, 768))
    pn_own, pn_oth = part_call(order, True, g_pre, fc1_weight)
    pn_got = swap(pn_oth)
    *bufs, gate_sum = wgrad2_call(order, hidden, hidden_o, wtd, wtd_o, mod, fc2_weight, fc2_bias)
    fc2.start(*bufs)
    pm_own, pm_oth = part_call(order, False, hidden, fc2_weight)
    pm_got = swap(pm_oth)
    fc1.fold(order)
    g_mid, g_att, sums2 = norm2_call(order, pn_own, pn_got, middle, branch, wtd, mod, norm2_gain)
    g_att_o = swap(g_att)
    g_attn_t, *bufs = oproj_call(order, 3, out_weight, g_att, g_att_o, att_t, att_o)

    def back(start, count, old, block, blocks):
        return attn_bwd(
            order, start, count, hbm(prob), inverse, g_attn_t, att_t, queries, keys, values, cos_t, sin_t,
            a_one, mod, norm1_gain, qkv_weight, old, block, blocks,
        )

    pairs = hw // 128
    g_a, sums_a, *bufs = back(0, pairs - 1, bufs, 1, pairs)
    rest.start(*bufs)
    fc2.fold(order)
    fc1.fold(order)
    g_b, sums_b, *bufs = back(pairs - 1, 1, None, 0, 1)
    last.start(*bufs)
    mixed = mix_call(order, pm_own, pm_got, middle, mod, fc2_bias)
    fc1_split = fc1.split(order)
    packet = pack_call(
        order, sums_a, sums_b, sums2, gate_sum, b1_sum, b2_sum, norm1_gain, norm2_gain, mod, cond_vec
    )
    packet_o = swap(packet)
    d_got = swap(dgrad_call(order, [g_a, g_b], qkv_weight, 1))
    fc2.fold(order)
    rest.fold(order)
    cond_grad, small_keep, send = deal_call(order, packet, packet_o, ada_weight)
    along = lambda step, v: lax.ppermute(v, ("dp", "ctx"), grid.pairs[step - 1])
    small_got = along(1, send)
    ff = join(order, join_ff_call, tuple(fc1_split), fc2)
    away, last_keep, small_keep = fold_last_call(order, *last.parts(), small_keep, small_got)
    last_got = along(2, away)
    d_own = dgrad_call(order, [g_a, g_b], qkv_weight, 0)
    input_grad = norm1_call(order, d_own, d_got, tok, g_mid, mod, norm1_gain)
    ff_sum = add_call(order, *ff.last())
    ff_other = swap(ff_sum)
    away, keep, small_keep = fold_att_call(
        order, rest.parts(), last_keep.reshape((2, 2) + last_keep.shape[1:]), last_got, small_keep
    )
    got = along(3, away)
    fc1_grad, fc2_grad = place_ff_call(order, ff_sum, ff_other, hw)
    away, keep, small_keep = fold_end_call(order, keep, got, small_keep)
    got = along(4, away)
    att_sum = add_call(order, keep, got)
    att_other = swap(att_sum)
    ada_grad, ada_bias_grad, fc1_bias_grad, norm1_grad, norm2_grad, fc2_bias_grad = last_call(
        order, got, small_keep, ndp
    )
    out_grad, qkv_grad = place_att_call(order, att_sum, att_other, width)
    return (
        mixed[None], input_grad[None], cond_grad, norm1_grad[0], qkv_grad, out_grad, norm2_grad[0],
        fc1_grad, fc1_bias_grad[0], fc2_grad, fc2_bias_grad[0], ada_grad, ada_bias_grad[0],
    )


def layer_norm(stream):
    row_mean = jnp.mean(stream, axis=-1, keepdims=True)
    centred = stream - row_mean
    variance = jnp.mean(centred * centred, axis=-1, keepdims=True)
    return centred * lax.rsqrt(variance + EPS)


def pre_norm(stream, norm_gain, shift_vec, scale_vec):
    return layer_norm(stream) * norm_gain * (1.0 + scale_vec[:, None, :]) + shift_vec[:, None, :]


def gelu_tanh(stream):
    return jax.nn.gelu(stream, approximate=True)


def block_rows(row_count):
    size_now = row_count
    while size_now > 512 and size_now % 2 == 0:
        size_now = size_now // 2
    return size_now


def rotary_tables(positions):
    inv_freq = 10000.0 ** (-jnp.arange(0, HEAD_DIM, 2).astype(jnp.float32) / HEAD_DIM)
    angles = positions.astype(jnp.float32)[..., None] * inv_freq
    cos_table = jnp.concatenate([jnp.cos(angles), jnp.cos(angles)], axis=-1)[..., None, :]
    sin_table = jnp.concatenate([jnp.sin(angles), jnp.sin(angles)], axis=-1)[..., None, :]
    return (cos_table, sin_table)


def rotate_pos(stream, cos_table, sin_table):
    half_dim = stream.shape[-1] // 2
    turned = jnp.concatenate([-stream[..., half_dim:], stream[..., :half_dim]], axis=-1)
    return stream * cos_table + turned * sin_table


def over_blocks(step_fn, fold_state, pieces):
    row_count = pieces[0].shape[1]
    size_now = block_rows(row_count)

    def one_turn(turn_idx, inner_state):
        part_list = tuple(
            (
                lax.dynamic_slice_in_dim(member, turn_idx * size_now, size_now, 1)
                for member in pieces
            )
        )
        return step_fn(inner_state, part_list, turn_idx * size_now)

    return lax.fori_loop(0, row_count // size_now, one_turn, fold_state)


def score_grads(query_blk, key_blk, value_blk, grad_blk, top_blk, total_blk, delta_blk):
    scores = (
        jnp.einsum("sqhd,skhd->sqhk", query_blk, key_blk, preferred_element_type=jnp.float32)
        * SCORE_SCALE
    )
    probability = jnp.exp(scores - top_blk[..., None]) / total_blk[..., None]
    grad_prob = jnp.einsum(
        "sqhd,skhd->sqhk", grad_blk, value_blk, preferred_element_type=jnp.float32
    )
    grad_scores = (probability * (grad_prob - delta_blk[..., None])).astype(jnp.bfloat16)
    return (probability, grad_scores)


def local_any(
    tokens_in,
    cond_vec,
    positions,
    absorbed,
    cotangent,
    norm1_gain,
    qkv_weight,
    out_weight,
    norm2_gain,
    fc1_weight,
    fc1_bias,
    fc2_weight,
    fc2_bias,
    ada_weight,
    ada_bias,
):
    seqs_here, span_len, model_width = tokens_in.shape
    head_shape = (seqs_here, span_len, HEADS, HEAD_DIM)
    stream = tokens_in.astype(jnp.float32)
    modulation = jnp.dot(
        cond_vec, ada_weight, preferred_element_type=jnp.float32
    ) + ada_bias.astype(jnp.float32)
    shift_one, scale_one, gate_one, shift_two, scale_two, gate_two = jnp.split(
        modulation, 6, axis=-1
    )
    gain_one = norm1_gain.astype(jnp.float32)
    gain_two = norm2_gain.astype(jnp.float32)
    normed_f, pull_one = jax.vjp(pre_norm, stream, gain_one, shift_one, scale_one)
    normed_one = normed_f.astype(jnp.bfloat16)
    projected = jnp.dot(normed_one, qkv_weight, preferred_element_type=jnp.float32)
    cos_table, sin_table = rotary_tables(positions)
    turned_pair, pull_rot = jax.vjp(
        lambda query_pre, key_pre: (
            rotate_pos(query_pre, cos_table, sin_table),
            rotate_pos(key_pre, cos_table, sin_table),
        ),
        projected[..., :model_width].reshape(head_shape),
        projected[..., model_width : 2 * model_width].reshape(head_shape),
    )
    queries = turned_pair[0].astype(jnp.bfloat16)
    key_loc = turned_pair[1].astype(jnp.bfloat16).reshape(seqs_here, span_len, model_width)
    value_loc = projected[..., 2 * model_width :].astype(jnp.bfloat16)

    def forward_step(fold_state, part_list, offset):
        run_max, run_sum, run_acc = fold_state
        key_blk = part_list[0].reshape(seqs_here, -1, HEADS, HEAD_DIM)
        value_blk = part_list[1].reshape(seqs_here, -1, HEADS, HEAD_DIM)
        scores = (
            jnp.einsum("sqhd,skhd->sqhk", queries, key_blk, preferred_element_type=jnp.float32)
            * SCORE_SCALE
        )
        new_max = jnp.maximum(run_max, jnp.max(scores, axis=-1))
        raised = jnp.exp(scores - new_max[..., None])
        shrink = jnp.exp(run_max - new_max)
        run_sum = run_sum * shrink + jnp.sum(raised, axis=-1)
        run_acc = run_acc * shrink[..., None] + jnp.einsum(
            "sqhk,skhd->sqhd",
            raised.astype(jnp.bfloat16),
            value_blk,
            preferred_element_type=jnp.float32,
        )
        return (new_max, run_sum, run_acc)

    empty_state = (
        jnp.full((seqs_here, span_len, HEADS), NEG_START, jnp.float32),
        jnp.zeros((seqs_here, span_len, HEADS), jnp.float32),
        jnp.zeros(head_shape, jnp.float32),
    )
    final_max, final_sum, final_acc = over_blocks(
        forward_step,
        empty_state,
        (
            lax.all_gather(key_loc, "ctx", axis=1, tiled=True),
            lax.all_gather(value_loc, "ctx", axis=1, tiled=True),
        ),
    )
    attn_out = final_acc / final_sum[..., None]
    attended = attn_out.reshape(seqs_here, span_len, model_width).astype(jnp.bfloat16)
    branch_att = jnp.dot(attended, out_weight, preferred_element_type=jnp.float32)
    middle = stream + gate_one[:, None, :] * branch_att
    normed_f2, pull_two = jax.vjp(pre_norm, middle, gain_two, shift_two, scale_two)
    normed_two = normed_f2.astype(jnp.bfloat16)
    hidden_pre = jnp.dot(
        normed_two, fc1_weight, preferred_element_type=jnp.float32
    ) + fc1_bias.astype(jnp.float32)
    hidden_f, pull_gelu = jax.vjp(gelu_tanh, hidden_pre)
    hidden = hidden_f.astype(jnp.bfloat16)
    branch_mlp = jnp.dot(hidden, fc2_weight, preferred_element_type=jnp.float32) + fc2_bias.astype(
        jnp.float32
    )
    mixed = (middle + gate_two[:, None, :] * branch_mlp).astype(jnp.bfloat16)
    weighted = cotangent.astype(jnp.float32) * absorbed.astype(jnp.float32)[..., None]
    grad_gate_two = jnp.sum(weighted * branch_mlp, axis=1)
    grad_mlp = (weighted * gate_two[:, None, :]).astype(jnp.bfloat16)
    grad_fc2b = jnp.sum(grad_mlp.astype(jnp.float32), axis=(0, 1))
    grad_fc2 = jnp.einsum("scf,scd->fd", hidden, grad_mlp, preferred_element_type=jnp.float32)
    grad_hidden = jnp.einsum(
        "scd,fd->scf", grad_mlp, fc2_weight, preferred_element_type=jnp.float32
    )
    grad_pre = pull_gelu(grad_hidden)[0].astype(jnp.bfloat16)
    grad_fc1b = jnp.sum(grad_pre.astype(jnp.float32), axis=(0, 1))
    grad_fc1 = jnp.einsum("scd,scf->df", normed_two, grad_pre, preferred_element_type=jnp.float32)
    grad_normed_two = jnp.einsum(
        "scf,df->scd", grad_pre, fc1_weight, preferred_element_type=jnp.float32
    )
    grad_mid_part, grad_gain_two, grad_shift_two, grad_scale_two = pull_two(grad_normed_two)
    grad_middle = weighted + grad_mid_part
    grad_gate_one = jnp.sum(grad_middle * branch_att, axis=1)
    grad_att = (grad_middle * gate_one[:, None, :]).astype(jnp.bfloat16)
    grad_out = jnp.einsum("scd,sce->de", attended, grad_att, preferred_element_type=jnp.float32)
    grad_attended = (
        jnp.einsum("sce,de->scd", grad_att, out_weight, preferred_element_type=jnp.float32)
        .astype(jnp.bfloat16)
        .reshape(head_shape)
    )
    row_delta = jnp.sum(grad_attended.astype(jnp.float32) * attn_out, axis=-1)

    def query_only_step(fold_state, part_list, offset):
        piece_len = part_list[0].shape[1]
        key_blk = part_list[0].reshape(seqs_here, piece_len, HEADS, HEAD_DIM)
        value_blk = part_list[1].reshape(seqs_here, piece_len, HEADS, HEAD_DIM)
        probability, grad_scores = score_grads(
            queries, key_blk, value_blk, grad_attended, final_max, final_sum, row_delta
        )
        return (
            fold_state
            + jnp.einsum(
                "sqhk,skhd->sqhd", grad_scores, key_blk, preferred_element_type=jnp.float32
            )
            * SCORE_SCALE
        )

    start_state = jnp.zeros(head_shape, jnp.float32)
    back_state = over_blocks(
        query_only_step,
        start_state,
        (
            lax.all_gather(key_loc, "ctx", axis=1, tiled=True),
            lax.all_gather(value_loc, "ctx", axis=1, tiled=True),
        ),
    )
    key_heads = key_loc.reshape(head_shape)
    value_heads = value_loc.reshape(head_shape)

    def local_key_step(fold_state, part_list, offset):
        grad_key_loc, grad_value_loc = fold_state
        query_blk = part_list[0].astype(jnp.bfloat16)
        grad_blk = part_list[1].astype(jnp.bfloat16)
        probability, grad_scores = score_grads(
            query_blk, key_heads, value_heads, grad_blk, part_list[2], part_list[3], part_list[4]
        )
        grad_value_loc = grad_value_loc + jnp.einsum(
            "sqhk,sqhd->skhd",
            probability.astype(jnp.bfloat16),
            grad_blk,
            preferred_element_type=jnp.float32,
        )
        grad_key_loc = (
            grad_key_loc
            + jnp.einsum(
                "sqhk,sqhd->skhd", grad_scores, query_blk, preferred_element_type=jnp.float32
            )
            * SCORE_SCALE
        )
        return (grad_key_loc, grad_value_loc)

    key_start = (jnp.zeros(head_shape, jnp.float32), jnp.zeros(head_shape, jnp.float32))
    grad_key_h, grad_value_h = over_blocks(
        local_key_step,
        key_start,
        (
            lax.all_gather(queries.astype(jnp.float32), "ctx", axis=1, tiled=True),
            lax.all_gather(grad_attended.astype(jnp.float32), "ctx", axis=1, tiled=True),
            lax.all_gather(final_max, "ctx", axis=1, tiled=True),
            lax.all_gather(final_sum, "ctx", axis=1, tiled=True),
            lax.all_gather(row_delta, "ctx", axis=1, tiled=True),
        ),
    )
    grad_key_loc = grad_key_h.reshape(seqs_here, span_len, model_width)
    grad_value_loc = grad_value_h.reshape(seqs_here, span_len, model_width)
    grad_query_pre, grad_key_pre = pull_rot((back_state, grad_key_loc.reshape(head_shape)))
    grad_proj = jnp.concatenate(
        [
            grad_query_pre.reshape(seqs_here, span_len, model_width),
            grad_key_pre.reshape(seqs_here, span_len, model_width),
            grad_value_loc,
        ],
        axis=-1,
    ).astype(jnp.bfloat16)
    grad_qkv = jnp.einsum("scd,sce->de", normed_one, grad_proj, preferred_element_type=jnp.float32)
    grad_normed_one = jnp.einsum(
        "sce,de->scd", grad_proj, qkv_weight, preferred_element_type=jnp.float32
    )
    grad_in_part, grad_gain_one, grad_shift_one, grad_scale_one = pull_one(grad_normed_one)
    input_grad = (grad_middle + grad_in_part).astype(jnp.bfloat16)
    partial_mod = jnp.concatenate(
        [
            grad_shift_one,
            grad_scale_one,
            grad_gate_one,
            grad_shift_two,
            grad_scale_two,
            grad_gate_two,
        ],
        axis=-1,
    )
    grad_mod = lax.psum(partial_mod, "ctx")
    cond_grad = jnp.einsum(
        "se,ce->sc",
        grad_mod,
        ada_weight.astype(jnp.float32),
        precision=lax.Precision.HIGHEST,
        preferred_element_type=jnp.float32,
    )
    first_cycle = (lax.axis_index("ctx") == 0).astype(jnp.float32)
    grad_ada = (
        jnp.einsum(
            "sc,se->ce",
            cond_vec.astype(jnp.float32),
            grad_mod,
            precision=lax.Precision.HIGHEST,
            preferred_element_type=jnp.float32,
        )
        * first_cycle
    )
    grad_adab = jnp.sum(grad_mod, axis=0) * first_cycle
    (
        part_g1,
        part_qkv,
        part_out,
        part_g2,
        part_fc1,
        part_fc1b,
        part_fc2,
        part_fc2b,
        part_ada,
        part_adab,
    ) = (
        lax.psum_scatter(grad_gain_one, "dp", scatter_dimension=0, tiled=True),
        lax.psum_scatter(grad_qkv, "dp", scatter_dimension=0, tiled=True),
        lax.psum_scatter(grad_out, "dp", scatter_dimension=0, tiled=True),
        lax.psum_scatter(grad_gain_two, "dp", scatter_dimension=0, tiled=True),
        lax.psum_scatter(grad_fc1, "dp", scatter_dimension=0, tiled=True),
        lax.psum_scatter(grad_fc1b, "dp", scatter_dimension=0, tiled=True),
        lax.psum_scatter(grad_fc2, "dp", scatter_dimension=0, tiled=True),
        lax.psum_scatter(grad_fc2b, "dp", scatter_dimension=0, tiled=True),
        lax.psum_scatter(grad_ada, "dp", scatter_dimension=1, tiled=True),
        lax.psum_scatter(grad_adab, "dp", scatter_dimension=0, tiled=True),
    )
    summed = lax.psum(
        (
            part_g1,
            part_qkv,
            part_out,
            part_g2,
            part_fc1,
            part_fc1b,
            part_fc2,
            part_fc2b,
            part_ada,
            part_adab,
        ),
        "ctx",
    )
    return (mixed, input_grad, cond_grad) + tuple(summed)


def local(*args, ndp, nctx):
    seqs, span, _ = args[0].shape
    if nctx == 2 and seqs == 1 and ndp == 16 and span == 512:
        return local_pair(*args, ndp=ndp)
    return local_any(*args)


def solution(mesh):
    in_specs = (
        P("dp", "ctx", None),
        P("dp", None),
        P("dp", "ctx"),
        P("dp", "ctx"),
        P("dp", "ctx", None),
        P(),
        P(),
        P(),
        P(),
        P(),
        P(),
        P(),
        P(),
        P(),
        P(),
    )
    out_specs = (
        P("dp", "ctx", None),
        P("dp", "ctx", None),
        P("dp", None),
        P("dp"),
        P("dp", None),
        P("dp", None),
        P("dp"),
        P("dp", None),
        P("dp"),
        P("dp", None),
        P("dp"),
        P(None, "dp"),
        P("dp"),
    )
    step = functools.partial(local, ndp=mesh.shape["dp"], nctx=mesh.shape["ctx"])
    return jax.shard_map(step, mesh=mesh, in_specs=in_specs, out_specs=out_specs, check_vma=False)
```

```python
import functools

import jax
import jax.numpy as jnp
import numpy as np
from jax import lax
from jax.experimental import pallas as pl
from jax.experimental.pallas import tpu as pltpu
from jax.sharding import PartitionSpec as P

HEADS = 12
HEAD_DIM = 64
EPS = 1e-05
SCORE_SCALE = 0.125
NEG_START = -1e30
F32, BF16 = jnp.float32, jnp.bfloat16
COST = 2e8
FF = 10
MLP_COLS = 1536
BWD_BLK = 1024


def dot(a, b):
    return jnp.dot(a, b, preferred_element_type=F32)


def dot_tn(a, b):
    return lax.dot_general(a, b, (((0,), (0,)), ((), ())), preferred_element_type=F32)


def dot_nt(a, b):
    return lax.dot_general(a, b, (((1,), (1,)), ((), ())), preferred_element_type=F32)


def sds(shape, dtype):
    return jax.ShapeDtypeStruct(shape, dtype)


def hbm(x):
    return pltpu.with_memory_space_constraint(x, pltpu.HBM)


class Order:
    def __init__(self, place):
        self.place, self.token = place, None

    def call(
        self, body, args, grid, in_specs, out_specs, out_shape, scratch=(), mb=32, us=1.0, aliases=None, after=(),
        name=None,
    ):
        after = list(after) + ([] if self.token is None else [self.token])
        extra, n_in, n_out = len(after), 1 + len(args), len(out_shape)

        def inner(*refs):
            outs = refs[n_in + extra :]
            body(*refs[:n_in], *outs[:n_out], *outs[n_out + 1 :])

        *outs, self.token = pl.pallas_call(
            inner,
            grid_spec=pltpu.PrefetchScalarGridSpec(
                num_scalar_prefetch=1,
                grid=grid,
                in_specs=list(in_specs) + [ANY] * extra,
                out_specs=list(out_specs) + [ANY],
                scratch_shapes=list(scratch),
            ),
            out_shape=list(out_shape) + [sds((8, 128), F32)],
            input_output_aliases=aliases or {},
            compiler_params=pltpu.CompilerParams(vmem_limit_bytes=mb << 20),
            cost_estimate=pl.CostEstimate(flops=int(us * COST), bytes_accessed=1 << 16, transcendentals=0),
            name=name,
        )(self.place, *args, *after)
        return outs


ANY = pl.BlockSpec(memory_space=pl.ANY)


def whole(shape):
    return pl.BlockSpec(shape, lambda *a: (0,) * len(shape))


def layer_stats(stream):
    row_mean = jnp.mean(stream, axis=-1, keepdims=True)
    centred = stream - row_mean
    variance = jnp.mean(centred * centred, axis=-1, keepdims=True)
    inv = lax.rsqrt(variance + EPS)
    return centred * inv, inv


def swap_lanes(x):
    lane = lax.broadcasted_iota(jnp.int32, x.shape, 1) % HEAD_DIM
    half = HEAD_DIM // 2
    return jnp.where(lane < half, pltpu.roll(x, 128 - half, 1), pltpu.roll(x, half, 1))


def mask_half(value, head):
    lane = lax.broadcasted_iota(jnp.int32, value.shape, 1)
    keep = (lane < HEAD_DIM) if head == 0 else (lane >= HEAD_DIM)
    return jnp.where(keep, value, jnp.zeros_like(value))


def attend_body(
    s_ref, ta_ref, tb_ref, cond_ref, ada_ref, adab_ref, gain_ref, wq_ref, wk_ref, wv_ref, pa_ref, pb_ref, freq_ref,
    cot_ref, abs_ref,
    n1_out, q_out, k_out, v_out, cost_ref, sint_ref,
    out_ref, prob_ref, inv_ref, mod_ref, wtd_ref, scores_ref, top_ref, vt_ref, n1_ref, q_ref, k_ref, v_ref,
):
    pair, step = pl.program_id(0), pl.program_id(1)
    span, width = ta_ref.shape
    blk = out_ref.shape[1]

    @pl.when((pair == 0) & (step == 0))
    def _():
        kept = jnp.broadcast_to(abs_ref[...].astype(F32), (128, span)).T[:, 0:1]
        wtd_ref[...] = (cot_ref[...].astype(F32) * kept).astype(BF16)
        cond = jnp.broadcast_to(cond_ref[...].astype(F32), (16, cond_ref.shape[1])).astype(BF16)
        mod_ref[...] = dot(cond, ada_ref[...])[:8] + adab_ref[...].astype(F32)[None, :]
        shift, scale = mod_ref[0:1, 0:width], mod_ref[0:1, width : 2 * width]
        gain = gain_ref[...].astype(F32)[None, :] * (1.0 + scale)
        for half, (t_ref, p_ref) in enumerate(((ta_ref, pa_ref), (tb_ref, pb_ref))):
            rows = slice(half * span, (half + 1) * span)
            angles = freq_ref[...] * p_ref[...].astype(F32)
            cos_h, sin_h = jnp.cos(angles), jnp.sin(angles)
            cos_t, sin_t = rotation(cos_h, sin_h)
            cost_ref[:, rows] = cos_h
            sint_ref[:, rows] = sin_h
            cos_n, sin_n = cos_t.T, sin_t.T
            a_one, _ = layer_stats(t_ref[...].astype(F32))
            normed = (a_one * gain + shift).astype(BF16)
            n1_ref[rows, :] = a_one.astype(BF16)
            q_pre = dot(normed, wq_ref[...])
            k_pre = dot(normed, wk_ref[...])
            v_ref[rows, :] = dot(normed, wv_ref[...]).astype(BF16)
            for p in range(q_pre.shape[1] // 128):
                at = slice(p * 128, (p + 1) * 128)
                part = q_pre[:, at]
                q_ref[rows, at] = (SCORE_SCALE * (part * cos_n + swap_lanes(part) * sin_n)).astype(BF16)
                part = k_pre[:, at]
                k_ref[rows, at] = (part * cos_n + swap_lanes(part) * sin_n).astype(BF16)

    pairs, blocks = pl.num_programs(0), pl.num_programs(1)
    lanes = lambda p: pl.ds(pl.multiple_of(p * 128, 128), 128)
    piece = jnp.minimum(pair * blocks + step, n1_ref.shape[0] // n1_out.shape[0] - 1)
    n1_out[...] = n1_ref[pl.ds(pl.multiple_of(piece * n1_out.shape[0], 128), n1_out.shape[0]), :]
    length = k_ref.shape[0]
    cut = 512

    def queries(p, i, head):
        return mask_half(q_ref[pl.ds(pl.multiple_of(i * blk, blk), blk), lanes(p)], head)

    def top_rows(scores):
        return jnp.max(scores.reshape(scores.shape[0] // 8, 8, blk), axis=0)

    @pl.when((pair == 0) & (step == 0))
    def _():
        vt_ref[...] = v_ref[...].T
        q_0 = queries(0, 0, 0)
        top = None
        for at in range(0, length, cut):
            scores = dot_nt(k_ref[at : at + cut, 0:128], q_0)
            scores_ref[0, at : at + cut] = scores
            top = top_rows(scores) if top is None else jnp.maximum(top, top_rows(scores))
        top_ref[0] = top

    @pl.when(step == 0)
    def _():
        q_out[...] = q_ref[:, lanes(pair)]
        k_out[...] = k_ref[:, lanes(pair)]
        v_out[...] = v_ref[:, lanes(pair)]

    for head in (0, 1):
        if head == 0:
            next_pair, next_step = pair, step
        else:
            wrap = step == blocks - 1
            next_step = jnp.where(wrap, 0, step + 1)
            next_pair = jnp.minimum(jnp.where(wrap, pair + 1, pair), pairs - 1)
        q_next = queries(next_pair, next_step, 1 - head)
        top = jnp.max(top_ref[head], axis=0, keepdims=True)
        rows = pl.ds(pl.multiple_of(pair * 128 + head * HEAD_DIM, HEAD_DIM), HEAD_DIM)
        next_top = sums = part = None
        for at in range(0, length, cut):
            here = slice(at, at + cut)
            scores = dot_nt(k_ref[here, lanes(next_pair)], q_next)
            scores_ref[1 - head, here] = scores
            new_top = top_rows(scores)
            raised = jnp.exp(scores_ref[head, here] - top)
            new_sums = jnp.sum(raised.reshape(cut // 8, 8, blk), axis=0)
            prob = raised.astype(BF16)
            prob_ref[head, here] = prob
            new_part = dot(vt_ref[rows, here], prob)
            next_top = new_top if next_top is None else jnp.maximum(next_top, new_top)
            sums = new_sums if sums is None else sums + new_sums
            part = new_part if part is None else part + new_part
        top_ref[1 - head] = next_top
        inverse = 1.0 / jnp.sum(sums, axis=0, keepdims=True)
        inv_ref[0, head : head + 1, :] = inverse
        out_ref[head * HEAD_DIM : (head + 1) * HEAD_DIM, :] = (part * inverse).astype(BF16)


def attend_call(order, tok, tok_o, cond, ada, adab, gain, qkv_weight, pos, pos_o, cot, absorbed):
    span, width = tok.shape
    length, hw = 2 * span, width // 2
    pairs, blk = hw // 128, 512
    freq = np.power(10000.0, -np.arange(0, HEAD_DIM, 2) / HEAD_DIM).astype(np.float32)[:, None]
    wspec = lambda j: pl.BlockSpec((width, hw), lambda p, i, s: (0, 2 * j + s[0]))
    col = pl.BlockSpec((length, 128), lambda p, i, s: (0, p))
    return order.call(
        attend_body,
        [hbm(tok), tok_o, hbm(cond), hbm(ada), hbm(adab), hbm(gain), *[hbm(qkv_weight)] * 3, hbm(pos), pos_o, hbm(jnp.asarray(freq)), hbm(cot), hbm(absorbed)],
        (pairs, length // blk),
        [whole(tok.shape), whole(tok.shape), whole(cond.shape), whole(ada.shape), whole(adab.shape), whole(gain.shape), wspec(0), wspec(1), wspec(2),
         whole(pos.shape), whole(pos.shape), whole(freq.shape), whole(cot.shape), whole(absorbed.shape)],
        [pl.BlockSpec((length // 4, width), lambda p, i, s: (jnp.minimum(p * (length // blk) + i, 3), 0)),
         col, col, col, whole((HEAD_DIM // 2, length)), whole((HEAD_DIM // 2, length)),
         pl.BlockSpec((128, blk), lambda p, i, s: (p, i)),
         pl.BlockSpec((2, length, blk), lambda p, i, s: (p, 0, i)),
         pl.BlockSpec((1, 8, blk), lambda p, i, s: (p, 0, i)), whole((8, ada.shape[1])), whole(tok.shape)],
        [sds((length, width), BF16)] + [sds((length, hw), BF16)] * 3
        + [sds((HEAD_DIM // 2, length), F32)] * 2
        + [sds((hw, length), BF16), pltpu.HBM((2 * pairs, length, length), BF16), sds((pairs, 8, length), F32),
           sds((8, ada.shape[1]), F32), sds(tok.shape, BF16)],
        scratch=[pltpu.VMEM((2, length, blk), F32), pltpu.VMEM((2, 8, blk), F32), pltpu.VMEM((hw, length), BF16),
                 pltpu.VMEM((length, width), BF16)] + [pltpu.VMEM((length, hw), BF16)] * 3,
        mb=40, us=20, name="attend",
    )


def swap_rows(x):
    half = HEAD_DIM // 2
    return jnp.concatenate([x[half * j : half * (j + 1)] for j in (1, 0, 3, 2)], axis=0)


def rotation(cos_h, sin_h):
    return jnp.concatenate([cos_h] * 4, axis=0), jnp.concatenate([-sin_h, sin_h, -sin_h, sin_h], axis=0)


def attn_bwd_body(
    r, s_ref, prob_ref, inv_ref, gt_ref, out_ref, q_ref, k_ref, v_ref, cost_ref, sint_ref, a_ref,
    mod_ref, gain_ref, wq_ref, wk_ref, wv_ref,
    g_ref, sum_ref, keep_ref, send_ref, vm_ref, kt_ref, dk_acc, dv_acc, acc_ref,
):
    step = pl.program_id(1)
    blk = q_ref.shape[0]

    @pl.when(step == 0)
    def _():
        values = v_ref[...]
        for head in (0, 1):
            vm_ref[head] = mask_half(values, head)
        kt_ref[...] = k_ref[...].T

    queries = q_ref[...]
    grad_t = gt_ref[...].astype(jnp.float32)
    row_id = lax.broadcasted_iota(jnp.int32, (128, blk), 0)
    inverse = jnp.where(row_id < HEAD_DIM, inv_ref[0, 0:1, :], inv_ref[0, 1:2, :])
    grad_t = grad_t * inverse
    product = grad_t * out_ref[...].astype(jnp.float32)
    grad_b = grad_t.astype(jnp.bfloat16)
    dk_new = None
    dq_parts = []
    for head in (0, 1):
        rows = slice(head * HEAD_DIM, (head + 1) * HEAD_DIM)
        delta = jnp.sum(product[rows], axis=0, keepdims=True)
        keep = (row_id < HEAD_DIM) if head == 0 else (row_id >= HEAD_DIM)
        grad_m = jnp.where(keep, grad_b, jnp.zeros_like(grad_b))
        grad_p = jnp.dot(vm_ref[head], grad_b, preferred_element_type=jnp.float32)
        prob = prob_ref[head]
        grad_s = (prob.astype(jnp.float32) * (grad_p - delta)).astype(jnp.bfloat16)
        dv_h = dot_nt(prob, grad_m)
        dk_h = dot(grad_s, mask_half(queries, head))
        if dk_new is None:
            dk_new, dv_new = dk_h, dv_h
        else:
            dk_new, dv_new = dk_new + dk_h, dv_new + dv_h
        dq_parts.append(dot(kt_ref[rows, :], grad_s) * SCORE_SCALE)
    dq_t = jnp.concatenate(dq_parts, axis=0)
    here = pl.ds(pl.multiple_of(step * blk, blk), blk)
    cos_t, sin_t = rotation(cost_ref[:, here], sint_ref[:, here])
    dq_t = dq_t * cos_t - swap_rows(dq_t) * sin_t
    g_ref[here, 0:128] = dq_t.T.astype(jnp.bfloat16)

    @pl.when(step == 0)
    def _():
        dk_acc[...] = dk_new
        dv_acc[...] = dv_new

    @pl.when(step > 0)
    def _():
        dk_acc[...] += dk_new
        dv_acc[...] += dv_new

    @pl.when(step == pl.num_programs(1) - 1)
    def _():
        dk = dk_acc[...]
        cos_t, sin_t = rotation(cost_ref[...], sint_ref[...])
        g_ref[:, 128:256] = (dk * cos_t.T - swap_lanes(dk) * sin_t.T).astype(jnp.bfloat16)
        g_ref[:, 256:384] = dv_acc[...].astype(jnp.bfloat16)
        grads = g_ref[...]
        product = dot_tn(a_ref[...], grads)
        width = a_ref.shape[1]
        column = lambda row: jnp.broadcast_to(row, (128, width)).T
        gain = column(gain_ref[...].astype(F32)[None, :] * (1.0 + mod_ref[0:1, width : 2 * width]))
        shift = column(mod_ref[0:1, 0:width])
        tokens = jnp.sum(grads.astype(F32), axis=0, keepdims=True)
        high = tokens.astype(BF16)
        low = (tokens - high.astype(F32)).astype(BF16)
        row_id = lax.broadcasted_iota(jnp.int32, (16, 384), 0)
        terms = jnp.where(row_id == 0, high, jnp.where(row_id == 1, low, jnp.zeros_like(high)))
        against = None
        for j, w_ref in enumerate((wq_ref, wk_ref, wv_ref)):
            at = slice(j * 128, (j + 1) * 128)
            part = product[:, at]
            acc_ref[:, at] = (part * gain + shift * tokens[:, at]).astype(BF16)
            weights = w_ref[...]
            scaled = part * weights.astype(F32)
            shifted = dot_nt(terms[:, at], weights)
            against = scaled if against is None else against + scaled
            shifts = shifted if j == 0 else shifts + shifted
        new = jnp.concatenate(
            [jnp.sum(shifts, axis=0, keepdims=True), jnp.sum(against.T, axis=0, keepdims=True)], axis=0
        )

        @pl.when(pl.program_id(0) == 0)
        def _():
            sum_ref[0:2, :] = new

        @pl.when(pl.program_id(0) > 0)
        def _():
            sum_ref[0:2, :] += new

        store_parts(s_ref, acc_ref, r, keep_ref, send_ref)


def attn_bwd(
    order, start, count, prob, inverse, grad_t, out_t, queries, keys, values, cos_t, sin_t, a_one,
    mod, gain, qkv_weight, old, block, blocks,
):
    length = keys.shape[0]
    width = a_one.shape[1]
    hw = width // 2
    wspec = lambda j: pl.BlockSpec((width, 128), lambda p, i, s: (0, (2 * j + s[0]) * (hw // 128) + p + start))
    blk = BWD_BLK
    r = width // 16
    col = pl.BlockSpec((length, 128), lambda p, i, s: (0, p + start))
    rowt = pl.BlockSpec((128, blk), lambda p, i, s: (p + start, i))
    out = pl.BlockSpec((2, 4, r, 384), lambda p, i, s: (0, 0, 0, p + block))
    args = [prob, inverse, grad_t, out_t, queries, keys, values, cos_t, sin_t, a_one, mod, gain, qkv_weight, qkv_weight, qkv_weight]
    aliases = {}
    after = []
    if old is not None:
        aliases = {1 + len(args) + j: 2 + j for j in range(2)}
        after = list(old)
    return order.call(
        functools.partial(attn_bwd_body, r), args, (count, length // blk),
        [
            pl.BlockSpec((2, length, blk), lambda p, i, s: (p + start, 0, i)),
            pl.BlockSpec((1, 8, blk), lambda p, i, s: (p + start, 0, i)),
            rowt, rowt,
            pl.BlockSpec((blk, 128), lambda p, i, s: (i, p + start)),
            col, col, whole(cos_t.shape), whole(cos_t.shape), whole(a_one.shape),
            whole(mod.shape), whole(gain.shape), wspec(0), wspec(1), wspec(2),
        ],
        [pl.BlockSpec((length, 384), lambda p, i, s: (0, p)), whole((8, width))] + [out] * 2,
        [sds((length, 384 * count), BF16), sds((8, width), F32)] + [sds((2, 4, r, 384 * blocks), BF16)] * 2,
        scratch=[
            pltpu.VMEM((2, length, 128), BF16),
            pltpu.VMEM((128, length), BF16),
            pltpu.VMEM((length, 128), F32),
            pltpu.VMEM((length, 128), F32),
            pltpu.VMEM((width, 384), BF16),
        ],
        mb=40, us=8.0 * count, aliases=aliases, after=after, name="attn_bwd",
    )


def mix_body(s_ref, own_ref, got_ref, mid_ref, mod_ref, bias_ref, out_ref):
    width = mid_ref.shape[1]
    branch = own_ref[...] + got_ref[...].astype(F32) + bias_ref[...].astype(F32)[None, :]
    out_ref[...] = (mid_ref[...] + mod_ref[0:1, 5 * width : 6 * width] * branch).astype(BF16)


def mix_call(order, own, got, mid, mod, bias):
    span, width = mid.shape
    blk = 256
    row = pl.BlockSpec((blk, width), lambda i, s: (i, 0))
    return order.call(
        mix_body, [own, got, mid, mod, bias], (span // blk,),
        [row] * 3 + [whole(mod.shape), whole(bias.shape)],
        [row], [sds((span, width), BF16)], mb=12, us=2.5, name="mix",
    )[0]


def post_body(s_ref, att_ref, oth_ref, wm_ref, wo_ref, tok_ref, mod_ref, gain_ref, mid_ref, br_ref, n2_ref):
    width = tok_ref.shape[1]
    branch = dot_tn(att_ref[...], wm_ref[...]) + dot_tn(oth_ref[...], wo_ref[...])
    br_ref[...] = branch
    middle = tok_ref[...].astype(F32) + mod_ref[0:1, 2 * width : 3 * width] * branch
    mid_ref[...] = middle
    a_two, _ = layer_stats(middle)
    scale = mod_ref[0:1, 4 * width : 5 * width]
    n2_ref[...] = (
        a_two * (gain_ref[...].astype(F32)[None, :] * (1.0 + scale)) + mod_ref[0:1, 3 * width : 4 * width]
    ).astype(BF16)


def post_call(order, att_t, att_o, out_weight, tok, mod, gain):
    span, width = tok.shape
    hw = width // 2
    blk = 512
    n = span // blk
    row = pl.BlockSpec((blk, width), lambda i, s: (i, 0))
    return order.call(
        post_body, [att_t, att_o, out_weight, out_weight, tok, mod, gain], (n,),
        [
            pl.BlockSpec((hw, blk), lambda i, s: (0, i)),
            pl.BlockSpec((hw, blk), lambda i, s: (0, i + n)),
            pl.BlockSpec((hw, width), lambda i, s: (s[0], 0)),
            pl.BlockSpec((hw, width), lambda i, s: (1 - s[0], 0)),
            row, whole(mod.shape), whole(gain.shape),
        ],
        [row, row, row],
        [sds((span, width), F32), sds((span, width), F32), sds((span, width), BF16)],
        mb=12, us=3, name="post",
    )


def mlp_body(
    s_ref, n2a_ref, n2b_ref, wa_ref, wb_ref, mod_ref, w1_ref, b1_ref, w2_ref,
    hid_ref, pre_ref, b1g_ref, b2g_ref,
):
    step = pl.program_id(0)
    first = step < pl.num_programs(0) // 2
    width = n2a_ref.shape[1]
    x = jnp.where(first, n2a_ref[...], n2b_ref[...])
    wtd = jnp.where(first, wa_ref[...], wb_ref[...]).astype(F32)
    g_mlp = (wtd * mod_ref[0:1, 5 * width : 6 * width]).astype(BF16)
    bias = b1_ref[...].astype(F32)[None, :]
    hf = w1_ref.shape[1]
    bias = jnp.where(s_ref[0] == 0, bias[:, :hf], bias[:, hf:])
    c0 = 0.7978845608028654
    c1 = c0 * 0.044715
    parts = []
    for at in range(0, hf, MLP_COLS):
        cols = slice(at, at + MLP_COLS)
        v = dot(x, w1_ref[:, cols]) + bias[:, cols]
        gh = dot_nt(g_mlp, w2_ref[cols, :])
        v2 = v * v
        th = jnp.tanh(v * (c0 + c1 * v2))
        up = 0.5 + 0.5 * th
        hid_ref[:, cols] = (v * up).astype(BF16)
        slope = up + v * (0.5 - 0.5 * (th * th)) * (c0 + 3.0 * c1 * v2)
        pre = (gh * slope).astype(BF16)
        pre_ref[:, cols] = pre
        parts.append(jnp.sum(pre.astype(F32), axis=0, keepdims=True))
    b1_part = jnp.concatenate(parts, axis=1)
    b2_part = jnp.sum(g_mlp.astype(F32), axis=0, keepdims=True)

    @pl.when(step == 0)
    def _():
        b1g_ref[...] = b1_part
        b2g_ref[...] = b2_part

    @pl.when(step > 0)
    def _():
        b1g_ref[...] += b1_part
        b2g_ref[...] += b2_part


def halves(blk, width, n):
    return [
        pl.BlockSpec((blk, width), lambda i, s: (jnp.minimum(i, n - 1), 0)),
        pl.BlockSpec((blk, width), lambda i, s: (jnp.maximum(i - n, 0), 0)),
    ]


def mlp_call(order, n2a, n2b, wa, wb, mod, w1, b1, w2):
    span, width = n2a.shape
    hf = w1.shape[1] // 2
    blk = 256
    n = span // blk
    row = lambda w: pl.BlockSpec((blk, w), lambda i, s: (i, 0))
    return order.call(
        mlp_body, [n2a, n2b, wa, wb, mod, w1, b1, w2], (2 * n,),
        halves(blk, width, n) + halves(blk, width, n)
        + [
            whole(mod.shape),
            pl.BlockSpec((width, hf), lambda i, s: (0, s[0])),
            whole(b1.shape),
            pl.BlockSpec((hf, width), lambda i, s: (s[0], 0)),
        ],
        [row(hf), row(hf), whole((1, hf)), whole((1, width))],
        [sds((2 * span, hf), BF16), sds((2 * span, hf), BF16),
         sds((1, hf), F32), sds((1, width), F32)],
        mb=24, us=9.6, name="mlp",
    )


def store_parts(s_ref, acc_ref, r, keep_ref, send_ref, base=0):
    mine = s_ref[base + 1]
    for i in range(8):
        rest = sum(((i >> (2 - j)) & 1) * s_ref[base + 6 + j] for j in range(3))
        for ref, bit in ((keep_ref, mine), (send_ref, 1 - mine)):
            at = pl.ds(pl.multiple_of((rest + bit * s_ref[base + 5]) * r, 16), r)
            ref[i // 4, i % 4] = acc_ref[at, :]


def wgrad_body(r, s_ref, la_ref, lb_ref, g_ref, keep_ref, send_ref, acc_ref):
    span = la_ref.shape[0]
    acc_ref[...] = (dot_tn(la_ref[...], g_ref[:span]) + dot_tn(lb_ref[...], g_ref[span:])).astype(BF16)
    store_parts(s_ref, acc_ref, r, keep_ref, send_ref, FF)


def wgrad_call(order, left_a, left_b, right, blk):
    rows, cols = left_a.shape[1], right.shape[1]
    length = right.shape[0]
    r = rows // 16
    out = pl.BlockSpec((2, 4, r, blk), lambda i, s: (0, 0, 0, i))
    return order.call(
        functools.partial(wgrad_body, r), [left_a, left_b, right], (cols // blk,),
        [whole(left_a.shape), whole(left_b.shape), pl.BlockSpec((length, blk), lambda i, s: (0, i))],
        [out] * 2, [sds((2, 4, r, cols), BF16)] * 2,
        scratch=[pltpu.VMEM((rows, blk), BF16)], mb=16, us=4.2, name="wgrad_fc1",
    )


def wgrad2_body(
    r, s_ref, lm_ref, lo_ref, wa_ref, wb_ref, mod_ref, w2_ref, bias_ref, keep_ref, send_ref, gate_ref, acc_ref
):
    step, n = pl.program_id(0), pl.num_programs(0)
    mine = lax.div(step, n // 2) == s_ref[0]
    span, half = wa_ref.shape
    width = 2 * half
    here = pl.ds(pl.multiple_of(s_ref[0] * half, 128), half)
    own, oth = wa_ref[...], wb_ref[...]

    @pl.when(mine)
    def _():
        acc_ref[...] = dot_tn(lm_ref[:span], own) + dot_tn(lm_ref[span:], oth)

    @pl.when(jnp.logical_not(mine))
    def _():
        acc_ref[...] = dot_tn(lo_ref[:span], oth) + dot_tn(lo_ref[span:], own)

    part = jnp.sum(acc_ref[...] * w2_ref[...].astype(F32), axis=0, keepdims=True)

    @pl.when(step == 0)
    def _():
        tokens = jnp.sum(own.astype(F32), axis=0, keepdims=True) + jnp.sum(oth.astype(F32), axis=0, keepdims=True)
        bias = bias_ref[...].astype(F32)[None, :]
        gate_ref[...] = part + tokens * jnp.where(s_ref[0] == 0, bias[:, :half], bias[:, half:])

    @pl.when(step > 0)
    def _():
        gate_ref[...] += part

    gate = mod_ref[0:1, pl.ds(pl.multiple_of(5 * width + s_ref[0] * half, 128), half)]
    za, zb = lax.div(step, 2), lax.rem(step, 2)
    two, four = jnp.where(s_ref[0] == 0, zb, za), jnp.where(s_ref[0] == 0, za, zb)
    for other in range(2):
        for ref, bit in ((keep_ref, s_ref[FF + 1]), (send_ref, 1 - s_ref[FF + 1])):
            at = pl.ds(pl.multiple_of((other * s_ref[FF + 7] + bit * s_ref[FF + 5]) * r, 16), r)
            ref[two, other * 2 + four] = (acc_ref[at, :] * gate).astype(BF16)


def wgrad2_call(order, hidden, hidden_o, wa, wb, mod, w2, bias):
    length, hf = hidden.shape
    span, width = wa.shape
    hw = width // 2
    r = hf // 8
    left = lambda first: pl.BlockSpec((length, 4 * r), lambda i, s: (0, jnp.clip(i - first(s[0]), 0, 1)))
    cols = pl.BlockSpec((span, hw), lambda i, s: (0, s[0]))
    return order.call(
        functools.partial(wgrad2_body, r), [hidden, hidden_o, wa, wb, mod, w2, bias], (4,),
        [left(lambda c: 2 * c), left(lambda c: 2 - 2 * c), cols, cols, whole(mod.shape), pl.BlockSpec((4 * r, hw), lambda i, s: (i, s[0])), whole(bias.shape)],
        [whole((2, 4, r, hw))] * 2 + [whole((1, hw))], [sds((2, 4, r, hw), BF16)] * 2 + [sds((1, hw), F32)],
        scratch=[pltpu.VMEM((4 * r, hw), F32)], mb=16, us=4.5, name="wgrad_fc2",
    )


def fold_body(s_ref, ka, ra, ks, rs, away_ref, stay_ref):
    away_ref[...] = ka[0] + ra[0]
    stay_ref[...] = ks[0] + rs[0]


def fold_call(order, step, keep, got):
    _, count, r, n = keep.shape
    blk = 768 if n % 768 == 0 else 384
    away = pl.BlockSpec((1, count, r, blk), lambda i, s: (1 - s[step], 0, 0, i))
    stay = pl.BlockSpec((1, count, r, blk), lambda i, s: (s[step], 0, 0, i))
    out = pl.BlockSpec((count, r, blk), lambda i, s: (0, 0, i))
    return order.call(
        fold_body, [keep, got, keep, got], (n // blk,), [away, away, stay, stay], [out] * 2,
        [sds((count, r, n), BF16)] * 2, mb=8, us=1.2, name="fold",
    )


def join_ff_body(s_ref, ka_ref, ga_ref, ks_ref, gs_ref, away_in, stay_in, away_ref, stay_ref):
    r = away_in.shape[1]
    width = ka_ref.shape[3]
    for out, one, k_ref, g_ref in ((away_ref, away_in, ka_ref, ga_ref), (stay_ref, stay_in, ks_ref, gs_ref)):
        out[:, :r] = one[...]
        two = k_ref[0] + g_ref[0]
        for q in range(two.shape[1] // r):
            out[:, r:, q * width : (q + 1) * width] = two[:, q * r : (q + 1) * r]


def join_ff_call(order, step, one, two):
    keep, got = two
    away_in, stay_in = one
    specs = []
    for away in (True, False):
        pick = (lambda i, s: (1 - s[step], 0, 0, 0)) if away else (lambda i, s: (s[step], 0, 0, 0))
        specs += [pl.BlockSpec((1,) + keep.shape[1:], pick)] * 2
    count, r, n = away_in.shape
    shape = (count, 2 * r, n)
    return order.call(
        join_ff_body, [keep, got, keep, got, away_in, stay_in], (1,),
        specs + [whole(away_in.shape)] * 2, [whole(shape)] * 2, [sds(shape, BF16)] * 2, mb=12, us=1.2, name="fold_ff",
    )


def relay(step, mine, keep, got):
    sources, rest = 2 ** (step - 2), 2 ** (4 - step)
    stay, away = [], []
    for read in (keep, got):
        for src in range(sources):
            both = [[read(src * 2 * rest + bit * rest + k) for k in range(rest)] for bit in range(2)]
            for k in range(rest):
                stay.append(jnp.where(mine == 0, both[0][k], both[1][k]))
                away.append(jnp.where(mine == 0, both[1][k], both[0][k]))
    return stay, away


def paired(packets):
    return [jnp.concatenate(packets[q : q + 2], axis=0).astype(BF16) for q in range(0, 8, 2)]


def single(pair):
    pairs = [pair(q).astype(F32) for q in range(4)]
    return lambda slot: pairs[slot // 2][(slot % 2) * 8 : (slot % 2) * 8 + 8]


def fold_last_body(s_ref, keep_ref, got_ref, sk_ref, sg_ref, away_ref, stay_ref, small_ref):
    mine = s_ref[2]
    r = keep_ref.shape[2]
    away_ref[:, :r] = keep_ref[1 - mine] + got_ref[1 - mine]
    stay_ref[...] = keep_ref[mine] + got_ref[mine]
    stay, away = relay(2, mine, lambda k: sk_ref[k], lambda k: sg_ref[k])
    for k in range(8):
        small_ref[k] = stay[k]
    for q, pair in enumerate(paired(away)):
        away_ref[q, r : r + 16] = pair


def fold_last_call(order, keep, got, small_keep, small_got):
    _, count, r, n = keep.shape
    args = [keep, got, small_keep, small_got]
    shapes = [((count, r + 16, n), BF16), ((count, r, n), BF16), (small_keep.shape, F32)]
    return order.call(
        fold_last_body, args, (1,), [whole(a.shape) for a in args], [whole(x) for x, _ in shapes],
        [sds(*x) for x in shapes], mb=14, us=1.2, name="fold_last",
    )


def fold_att_body(s_ref, k1_ref, g1_ref, k2_ref, g2_ref, sk_ref, away_ref, stay_ref, small_ref):
    mine = s_ref[3]
    count, r, n = k1_ref.shape[1:]
    for out, at in ((away_ref, 1 - mine), (stay_ref, mine)):
        for j in range(count):
            out[j * r : (j + 1) * r, :n] = k1_ref[at, j] + g1_ref[at, j]
            out[j * r : (j + 1) * r, n:] = k2_ref[at, j] + g2_ref[at * count + j, :r]
    got = single(lambda q: g2_ref[q, r : r + 16])
    stay, away = relay(3, mine, lambda k: sk_ref[k], got)
    for k in range(8):
        small_ref[k] = stay[k]
    w = sk_ref.shape[2]
    for q, pair in enumerate(paired(away)):
        away_ref[count * r :, q * w : (q + 1) * w] = pair


def fold_att_call(order, one, two, got, small_keep):
    _, count, r, n = one[0].shape
    full = n + two.shape[3]
    args = [*one, two, got, small_keep]
    shapes = [((count * r + 16, full), BF16), ((count * r, full), BF16), (small_keep.shape, F32)]
    return order.call(
        fold_att_body, args, (1,), [whole(a.shape) for a in args], [whole(x) for x, _ in shapes],
        [sds(*x) for x in shapes], mb=14, us=1.2, name="fold_att",
    )


def fold_end_body(s_ref, keep_ref, got_ref, sk_ref, away_ref, stay_ref, small_ref):
    mine = s_ref[4]
    r = stay_ref.shape[0]
    for out, at in ((away_ref, 1 - mine), (stay_ref, mine)):
        rows = pl.ds(pl.multiple_of(at * r, 16), r)
        out[:r] = keep_ref[rows] + got_ref[rows]
    w = sk_ref.shape[2]
    got = single(lambda q: got_ref[2 * r :, q * w : (q + 1) * w])
    stay, away = relay(4, mine, lambda k: sk_ref[k], got)
    for k in range(8):
        small_ref[k] = stay[k]
    for q, pair in enumerate(paired(away)):
        away_ref[r:, q * w : (q + 1) * w] = pair


def fold_end_call(order, keep, got, small_keep):
    r, n = keep.shape[0] // 2, keep.shape[1]
    args = [keep, got, small_keep]
    shapes = [((r + 16, n), BF16), ((r, n), BF16), (small_keep.shape, F32)]
    return order.call(
        fold_end_body, args, (1,), [whole(a.shape) for a in args], [whole(x) for x, _ in shapes],
        [sds(*x) for x in shapes], mb=14, us=1.2, name="fold_end",
    )


def add_body(s_ref, a_ref, b_ref, out_ref):
    out_ref[...] = a_ref[...] + b_ref[: out_ref.shape[0]]


def add_call(order, a, b):
    return order.call(
        add_body, [a, b], (1,), [whole(a.shape), whole(b.shape)], [whole(a.shape)], [sds(a.shape, BF16)], mb=8, us=1.0, name="add"
    )[0]


def place_ff_body(s_ref, mine_ref, other_ref, fc1_ref, fc2_ref):
    core = s_ref[0]
    r, n = fc1_ref.shape[0], mine_ref.shape[1]
    width = fc2_ref.shape[1] // 2
    for ref, at in ((mine_ref, core), (other_ref, 1 - core)):
        fc1_ref[:, pl.ds(pl.multiple_of(at * n, 128), n)] = ref[:r].astype(F32)
        cols = pl.ds(pl.multiple_of(at * width, 128), width)
        for q in range(n // width):
            fc2_ref[q * r : (q + 1) * r, cols] = ref[r:, q * width : (q + 1) * width].astype(F32)


def place_ff_call(order, mine, other, hw):
    r, n = mine.shape[0] // 2, mine.shape[1]
    shapes = [(r, 2 * n), (r * (n // hw), 2 * hw)]
    return order.call(
        place_ff_body, [mine, other], (1,), [whole(mine.shape)] * 2, [whole(x) for x in shapes],
        [sds(x, F32) for x in shapes], mb=8, us=1.0, name="place_ff",
    )


def place_att_body(s_ref, mine_ref, other_ref, out_ref, qkv_ref):
    core = s_ref[0]
    width = out_ref.shape[1]
    hw = width // 2
    for ref, at in ((mine_ref, core), (other_ref, 1 - core)):
        out_ref[:, pl.ds(pl.multiple_of(at * hw, 128), hw)] = ref[:, :hw].astype(F32)
        for p in range(hw // 128):
            for j in range(3):
                to = pl.ds(pl.multiple_of(j * width + at * hw + p * 128, 128), 128)
                src = hw + p * 384 + j * 128
                qkv_ref[:, to] = ref[:, src : src + 128].astype(F32)


def place_att_call(order, mine, other, width):
    r = mine.shape[0]
    shapes = [(r, width), (r, 3 * width)]
    return order.call(
        place_att_body, [mine, other], (1,), [whole(mine.shape)] * 2, [whole(x) for x in shapes],
        [sds(x, F32) for x in shapes], mb=8, us=1.0, name="place_att",
    )


def pack_body(
    s_ref, s1a_ref, s1b_ref, s2_ref, gate_ref, b1_ref, b2_ref, g1_ref, g2_ref, mod_ref, cond_ref, out_ref
):
    width = s2_ref.shape[1]
    h = width // 2
    core = s_ref[0]
    mine = jnp.where(core == 0, 1.0, 0.0)
    gain_one, gain_two = g1_ref[...].astype(F32)[None, :], g2_ref[...].astype(F32)[None, :]
    scale_one = 1.0 + mod_ref[0:1, width : 2 * width]
    scale_two = 1.0 + mod_ref[0:1, 4 * width : 5 * width]
    second_one, second_two = s1a_ref[1:2, :] + s1b_ref[1:2, :], s2_ref[1:2, :]
    gate = jnp.concatenate([gate_ref[...] * mine, gate_ref[...] * (1.0 - mine)], axis=1)
    flat = jnp.concatenate(
        [
            s1a_ref[0:1, :] + s1b_ref[0:1, :], second_one * gain_one, s2_ref[2:3, :],
            s2_ref[0:1, :], second_two * gain_two, gate,
        ],
        axis=1,
    )
    b1 = jnp.concatenate([b1_ref[...] * mine, b1_ref[...] * (1.0 - mine)], axis=1)
    sources = (flat, b1, second_one * scale_one, second_two * scale_two, 0.5 * b2_ref[...])
    out_ref[...] = jnp.zeros_like(out_ref)
    cond = 0.5 * cond_ref[...].astype(F32)
    ndp = out_ref.shape[0] - 2
    for d in range(ndp):
        for j, source in enumerate(sources):
            n = source.shape[1] // ndp
            out_ref[d, j : j + 1, 0:n] = source[:, d * n : (d + 1) * n]
        out_ref[d, 5:6, 0:128] = cond
    for j in range(12):
        out_ref[ndp + j // 8, j % 8 : j % 8 + 1, :] = flat[:, j * h : (j + 1) * h]


def pack_call(order, *args):
    h = args[2].shape[1] // 2
    shape = (18, 8, h)
    return order.call(
        pack_body, list(args), (1,), [whole(a.shape) for a in args], [whole(shape)], [sds(shape, F32)],
        mb=8, us=1.0, name="pack",
    )[0]


def deal_body(s_ref, a_ref, b_ref, ada_ref, cg_ref, keep_ref, send_ref, acc_ref):
    acc_ref[...] = a_ref[...] + b_ref[...]
    for i in range(8):
        rest = sum(((i >> (2 - j)) & 1) * s_ref[6 + j] for j in range(3))
        keep_ref[i] = acc_ref[rest + s_ref[1] * s_ref[5]]
        send_ref[i] = acc_ref[rest + (1 - s_ref[1]) * s_ref[5]]
    flat = jnp.concatenate([acc_ref[16 + j // 8, j % 8 : j % 8 + 1, :] for j in range(12)], axis=1)
    high = flat.astype(BF16)
    rest = flat - high.astype(F32)
    mid = rest.astype(BF16)
    low = (rest - mid.astype(F32)).astype(BF16)
    row_id = lax.broadcasted_iota(jnp.int32, (16, flat.shape[1]), 0)
    zero = jnp.zeros_like(high)
    terms = jnp.where(row_id == 0, high, jnp.where(row_id == 1, mid, jnp.where(row_id == 2, low, zero)))
    cg_ref[...] = jnp.sum(dot_nt(terms, ada_ref[...]), axis=0, keepdims=True)


def deal_call(order, mine, got, ada):
    shape = (8,) + mine.shape[1:]
    return order.call(
        deal_body, [mine, got, ada], (1,), [whole(mine.shape), whole(mine.shape), whole(ada.shape)],
        [whole((1, ada.shape[0])), whole(shape), whole(shape)],
        [sds((1, ada.shape[0]), F32), sds(shape, F32), sds(shape, F32)],
        scratch=[pltpu.VMEM(mine.shape, F32)], mb=8, us=1.0, name="deal",
    )


def last_body(s_ref, got_ref, sk_ref, ada_ref, adab_ref, b1_ref, g1_ref, g2_ref, b2_ref):
    r, w = got_ref.shape[0] - 16, sk_ref.shape[2]
    got = single(lambda q: got_ref[r:, q * w : (q + 1) * w])
    parts = [sk_ref[k] for k in range(8)] + [got(k) for k in range(8)]
    sums = parts[0]
    for part in parts[1:]:
        sums = sums + part
    cond = jnp.concatenate([part[5:6, 0:128] for part in parts], axis=0)
    grads = jnp.concatenate([part[0:1] for part in parts], axis=0)
    ada = lax.dot_general(
        cond, grads, (((0,), (0,)), ((), ())), precision=lax.Precision.HIGHEST, preferred_element_type=F32
    )
    ada_ref[...] = ada[:, : ada_ref.shape[1]]
    for j, ref in enumerate((adab_ref, b1_ref, g1_ref, g2_ref, b2_ref)):
        ref[...] = sums[j : j + 1, : ref.shape[1]]


def last_call(order, got, small_keep, ndp):
    h = small_keep.shape[2]
    na, nb, nc = 12 * h // ndp, 2 * h // ndp, 8 * h // ndp
    shapes = [(128, na), (1, na), (1, nc), (1, nb), (1, nb), (1, nb)]
    args = [got, small_keep]
    return order.call(
        last_body, args, (1,), [whole(a.shape) for a in args], [whole(x) for x in shapes],
        [sds(x, F32) for x in shapes], mb=8, us=1.0, name="small_last",
    )


def part_body(nt, s_ref, g_ref, w_ref, own_ref, oth_ref):
    step = pl.program_id(0)
    half = pl.num_programs(0) // 2
    part = dot_nt(g_ref[...], w_ref[...]) if nt else dot(g_ref[...], w_ref[...])

    @pl.when(step < half)
    def _():
        oth_ref[...] = part.astype(BF16)

    @pl.when(step >= half)
    def _():
        own_ref[...] = part


def part_call(order, nt, g, w):
    length, hf = g.shape
    width = w.shape[0] if nt else w.shape[1]
    blk = 512
    n = length // 2 // blk
    wspec = (
        pl.BlockSpec((width, hf), lambda i, s: (0, s[0]))
        if nt
        else pl.BlockSpec((hf, width), lambda i, s: (s[0], 0))
    )
    return order.call(
        functools.partial(part_body, nt), [g, w], (2 * n,),
        [pl.BlockSpec((blk, hf), lambda i, s: ((i + n) % (2 * n), 0)), wspec],
        [
            pl.BlockSpec((blk, width), lambda i, s: (jnp.maximum(i - n, 0), 0)),
            pl.BlockSpec((blk, width), lambda i, s: (jnp.minimum(i, n - 1), 0)),
        ],
        [sds((length // 2, width), F32), sds((length // 2, width), BF16)],
        mb=12, us=4.2, name="part",
    )


def norm2_body(s_ref, own_ref, got_ref, mid_ref, br_ref, wtd_ref, mod_ref, gain_ref, gmid_ref, gatt_ref, sum_ref):
    width = mid_ref.shape[1]
    g = own_ref[...] + got_ref[...].astype(F32)
    a_two, inv = layer_stats(mid_ref[...])
    ga = g * (gain_ref[...].astype(F32)[None, :] * (1.0 + mod_ref[0:1, 4 * width : 5 * width]))
    gaa = ga * a_two
    g_mid = wtd_ref[...].astype(F32) + inv * (
        ga - jnp.mean(ga, -1, keepdims=True) - a_two * jnp.mean(gaa, -1, keepdims=True)
    )
    gmid_ref[...] = g_mid
    gatt_ref[...] = (g_mid * mod_ref[0:1, 2 * width : 3 * width]).astype(BF16)
    sums = jnp.concatenate(
        [
            jnp.sum(g, axis=0, keepdims=True),
            jnp.sum(g * a_two, axis=0, keepdims=True),
            jnp.sum(g_mid * br_ref[...], axis=0, keepdims=True),
        ],
        axis=0,
    )

    @pl.when(pl.program_id(0) == 0)
    def _():
        sum_ref[...] = jnp.zeros_like(sum_ref)

    sum_ref[0:3, :] += sums


def norm2_call(order, own, got, mid, br, wtd, mod, gain):
    span, width = mid.shape
    blk = 512
    row = pl.BlockSpec((blk, width), lambda i, s: (i, 0))
    return order.call(
        norm2_body, [own, got, mid, br, wtd, mod, gain], (span // blk,),
        [row] * 5 + [whole(mod.shape), whole(gain.shape)],
        [row, row, whole((8, width))],
        [sds((span, width), F32), sds((span, width), BF16), sds((8, width), F32)],
        mb=12, us=3, name="norm2",
    )


def oproj_body(r, s_ref, w_ref, ga_ref, gb_ref, am_ref, ao_ref, gt_ref, keep_ref, send_ref, acc_ref):
    span = ga_ref.shape[0]
    half = am_ref.shape[0]
    core = s_ref[0]
    w = w_ref[...]
    gt_ref[:, :span] = dot_nt(w, ga_ref[...]).astype(BF16)
    gt_ref[:, span:] = dot_nt(w, gb_ref[...]).astype(BF16)
    cols = pl.ds(pl.multiple_of(core * half, 128), half)
    gac, gbc = ga_ref[:, cols], gb_ref[:, cols]
    mine = dot(am_ref[:, :span], gac) + dot(am_ref[:, span:], gbc)
    other = dot(ao_ref[:, span:], gac) + dot(ao_ref[:, :span], gbc)
    acc_ref[pl.ds(pl.multiple_of(core * half, 16), half), :] = mine.astype(BF16)
    acc_ref[pl.ds(pl.multiple_of((1 - core) * half, 16), half), :] = other.astype(BF16)
    store_parts(s_ref, acc_ref, r, keep_ref, send_ref)


def oproj_call(order, blocks, out_weight, ga, gb, att_t, att_o):
    span, width = ga.shape
    hw = width // 2
    r = width // 16
    out = pl.BlockSpec((2, 4, r, hw), lambda i, s: (0, 0, 0, 0))
    return order.call(
        functools.partial(oproj_body, r), [out_weight, ga, gb, att_t, att_o], (1,),
        [pl.BlockSpec((hw, width), lambda i, s: (s[0], 0)), whole(ga.shape), whole(ga.shape),
         whole(att_t.shape), whole(att_t.shape)],
        [whole((hw, 2 * span))] + [out] * 2,
        [sds((hw, 2 * span), BF16)] + [sds((2, 4, r, blocks * hw), BF16)] * 2,
        scratch=[pltpu.VMEM((width, hw), BF16)], mb=8, us=3, name="oproj",
    )


def norm1_body(s_ref, own_ref, got_ref, tok_ref, gmid_ref, mod_ref, gain_ref, out_ref):
    width = tok_ref.shape[1]
    g = own_ref[...] + got_ref[...].astype(F32)
    a_one, inv = layer_stats(tok_ref[...].astype(F32))
    ga = g * (gain_ref[...].astype(F32)[None, :] * (1.0 + mod_ref[0:1, width : 2 * width]))
    gaa = ga * a_one
    out_ref[...] = (
        gmid_ref[...]
        + inv * (ga - jnp.mean(ga, -1, keepdims=True) - a_one * jnp.mean(gaa, -1, keepdims=True))
    ).astype(BF16)


def norm1_call(order, own, got, tok, gmid, mod, gain):
    span, width = tok.shape
    blk = 256
    row = pl.BlockSpec((blk, width), lambda i, s: (i, 0))
    return order.call(
        norm1_body, [own, got, tok, gmid, mod, gain], (span // blk,),
        [row] * 4 + [whole(mod.shape), whole(gain.shape)], [row], [sds((span, width), BF16)],
        mb=12, us=3, name="norm1",
    )[0]


def dgrad_body(np_, s_ref, *refs):
    gs, (wq_ref, wk_ref, wv_ref), out_ref = refs[:np_], refs[np_ : np_ + 3], refs[np_ + 3]
    total = None
    for j, w_ref in enumerate((wq_ref, wk_ref, wv_ref)):
        left = jnp.concatenate(
            [g[:, at + j * 128 : at + (j + 1) * 128] for g in gs for at in range(0, g.shape[1], 384)], axis=1
        )
        part = dot_nt(left, w_ref[...])
        total = part if total is None else total + part
    out_ref[...] = total.astype(out_ref.dtype)


def dgrad_call(order, gs, qkv_weight, half):
    span = gs[0].shape[0] // 2
    width = qkv_weight.shape[0]
    hw = width // 2
    wspec = lambda j: pl.BlockSpec((width, hw), lambda i, s: (0, 2 * j + s[0]))
    return order.call(
        functools.partial(dgrad_body, len(gs)), [*gs, qkv_weight, qkv_weight, qkv_weight], (1,),
        [pl.BlockSpec((span, g.shape[1]), lambda i, s: (half, 0)) for g in gs] + [wspec(0), wspec(1), wspec(2)],
        [whole((span, width))], [sds((span, width), BF16 if half else F32)], mb=12, us=2.0, name="dgrad",
    )[0]


class Grid:
    ATT_ORDERS = ((1, 2, 4, 8), (2, 1, 8, 4))
    FF_ORDERS = ((1, 4, 2, 8), (2, 8, 1, 4))

    def __init__(self, ndp):
        self.index = lax.axis_index("dp")
        core = lax.axis_index("ctx")
        place = [core]
        self.pairs = []
        for orders in (self.ATT_ORDERS, self.FF_ORDERS):
            masks = [jnp.where(core == 0, a, b) for a, b in zip(*orders)]
            bits = [jnp.where((self.index & m) > 0, 1, 0) for m in masks]
            place += [*bits, *masks, self.index // 4, self.index]
            self.pairs.append(
                [[(2 * i + c, 2 * (i ^ orders[c][step]) + c) for i in range(ndp) for c in range(2)] for step in range(4)]
            )
        self.place = jnp.stack(place).astype(jnp.int32)


class Job:
    def __init__(self, pairs, base):
        self.pairs, self.base, self.step = pairs, base, 0

    def start(self, keep, send):
        self.keep = keep
        self.got = lax.ppermute(send, ("dp", "ctx"), self.pairs[self.step])
        self.step += 1

    def parts(self):
        shape = self.keep.shape
        if self.step > 1:
            shape = (2, shape[0] // 2) + shape[1:]
        return self.keep.reshape(shape), self.got.reshape(shape)

    def fold(self, order):
        away, stay = self.split(order)
        self.start(stay, away)

    def split(self, order):
        return fold_call(order, self.base + self.step + 1, *self.parts())

    def last(self):
        return self.keep[0], self.got[0]


def join(order, fold, one, two):
    job = Job(two.pairs, two.base)
    job.step = two.step
    away, stay = fold(order, job.base + job.step + 1, one if isinstance(one, tuple) else one.parts(), two.parts())
    job.start(stay, away)
    return job


def local_pair(
    tokens_in, cond_vec, positions, absorbed, cotangent, norm1_gain, qkv_weight, out_weight,
    norm2_gain, fc1_weight, fc1_bias, fc2_weight, fc2_bias, ada_weight, ada_bias, *, ndp,
):
    _, span, width = tokens_in.shape
    hw = width // 2
    grid = Grid(ndp)
    order = Order(grid.place)
    swap = lambda v: lax.ppermute(v, "ctx", [(0, 1), (1, 0)])

    tok = tokens_in[0]
    tok_o = swap(tok)
    pos_o = swap(positions)

    a_one, queries, keys, values, cos_t, sin_t, att_t, prob, inverse, mod, wtd = attend_call(
        order, tok, tok_o, cond_vec, ada_weight, ada_bias, norm1_gain, qkv_weight, positions, pos_o,
        cotangent[0], absorbed,
    )
    wtd_o = swap(wtd)
    att_o = swap(att_t)
    middle, branch, n2 = post_call(order, att_t, att_o, out_weight, hbm(tok), mod, norm2_gain)
    n2_o = swap(n2)
    hidden, g_pre, b1_sum, b2_sum = mlp_call(
        order, n2, n2_o, wtd, wtd_o, mod, fc1_weight, fc1_bias, fc2_weight
    )
    hidden_o = swap(hidden)
    fc1, fc2 = (Job(grid.pairs[1], FF) for _ in range(2))
    rest, last = (Job(grid.pairs[0], 0) for _ in range(2))
    fc1.start(*wgrad_call(order, n2, n2_o, g_pre, 768))
    pn_own, pn_oth = part_call(order, True, g_pre, fc1_weight)
    pn_got = swap(pn_oth)
    *bufs, gate_sum = wgrad2_call(order, hidden, hidden_o, wtd, wtd_o, mod, fc2_weight, fc2_bias)
    fc2.start(*bufs)
    pm_own, pm_oth = part_call(order, False, hidden, fc2_weight)
    pm_got = swap(pm_oth)
    fc1.fold(order)
    g_mid, g_att, sums2 = norm2_call(order, pn_own, pn_got, middle, branch, wtd, mod, norm2_gain)
    g_att_o = swap(g_att)
    g_attn_t, *bufs = oproj_call(order, 3, out_weight, g_att, g_att_o, att_t, att_o)

    def back(start, count, old, block, blocks):
        return attn_bwd(
            order, start, count, hbm(prob), inverse, g_attn_t, att_t, queries, keys, values, cos_t, sin_t,
            a_one, mod, norm1_gain, qkv_weight, old, block, blocks,
        )

    pairs = hw // 128
    g_a, sums_a, *bufs = back(0, pairs - 1, bufs, 1, pairs)
    rest.start(*bufs)
    fc2.fold(order)
    fc1.fold(order)
    g_b, sums_b, *bufs = back(pairs - 1, 1, None, 0, 1)
    last.start(*bufs)
    mixed = mix_call(order, pm_own, pm_got, middle, mod, fc2_bias)
    fc1_split = fc1.split(order)
    packet = pack_call(
        order, sums_a, sums_b, sums2, gate_sum, b1_sum, b2_sum, norm1_gain, norm2_gain, mod, cond_vec
    )
    packet_o = swap(packet)
    d_got = swap(dgrad_call(order, [g_a, g_b], qkv_weight, 1))
    fc2.fold(order)
    rest.fold(order)
    cond_grad, small_keep, send = deal_call(order, packet, packet_o, ada_weight)
    along = lambda step, v: lax.ppermute(v, ("dp", "ctx"), grid.pairs[0][step - 1])
    small_got = along(1, send)
    d_own = dgrad_call(order, [g_a, g_b], qkv_weight, 0)
    ff = join(order, join_ff_call, tuple(fc1_split), fc2)
    away, last_keep, small_keep = fold_last_call(order, *last.parts(), small_keep, small_got)
    last_got = along(2, away)
    input_grad = norm1_call(order, d_own, d_got, tok, g_mid, mod, norm1_gain)
    away, keep, small_keep = fold_att_call(
        order, rest.parts(), last_keep.reshape((2, 2) + last_keep.shape[1:]), last_got, small_keep
    )
    got = along(3, away)
    ff_sum = add_call(order, *ff.last())
    ff_other = swap(ff_sum)
    fc1_grad, fc2_grad = place_ff_call(order, ff_sum, ff_other, hw)
    away, keep, small_keep = fold_end_call(order, keep, got, small_keep)
    got = along(4, away)
    att_sum = add_call(order, keep, got)
    att_other = swap(att_sum)
    ada_grad, ada_bias_grad, fc1_bias_grad, norm1_grad, norm2_grad, fc2_bias_grad = last_call(
        order, got, small_keep, ndp
    )
    out_grad, qkv_grad = place_att_call(order, att_sum, att_other, width)
    return (
        mixed[None], input_grad[None], cond_grad, norm1_grad[0], qkv_grad, out_grad, norm2_grad[0],
        fc1_grad, fc1_bias_grad[0], fc2_grad, fc2_bias_grad[0], ada_grad, ada_bias_grad[0],
    )


def layer_norm(stream):
    row_mean = jnp.mean(stream, axis=-1, keepdims=True)
    centred = stream - row_mean
    variance = jnp.mean(centred * centred, axis=-1, keepdims=True)
    return centred * lax.rsqrt(variance + EPS)


def pre_norm(stream, norm_gain, shift_vec, scale_vec):
    return layer_norm(stream) * norm_gain * (1.0 + scale_vec[:, None, :]) + shift_vec[:, None, :]


def gelu_tanh(stream):
    return jax.nn.gelu(stream, approximate=True)


def block_rows(row_count):
    size_now = row_count
    while size_now > 512 and size_now % 2 == 0:
        size_now = size_now // 2
    return size_now


def rotary_tables(positions):
    inv_freq = 10000.0 ** (-jnp.arange(0, HEAD_DIM, 2).astype(jnp.float32) / HEAD_DIM)
    angles = positions.astype(jnp.float32)[..., None] * inv_freq
    cos_table = jnp.concatenate([jnp.cos(angles), jnp.cos(angles)], axis=-1)[..., None, :]
    sin_table = jnp.concatenate([jnp.sin(angles), jnp.sin(angles)], axis=-1)[..., None, :]
    return (cos_table, sin_table)


def rotate_pos(stream, cos_table, sin_table):
    half_dim = stream.shape[-1] // 2
    turned = jnp.concatenate([-stream[..., half_dim:], stream[..., :half_dim]], axis=-1)
    return stream * cos_table + turned * sin_table


def over_blocks(step_fn, fold_state, pieces):
    row_count = pieces[0].shape[1]
    size_now = block_rows(row_count)

    def one_turn(turn_idx, inner_state):
        part_list = tuple(
            (
                lax.dynamic_slice_in_dim(member, turn_idx * size_now, size_now, 1)
                for member in pieces
            )
        )
        return step_fn(inner_state, part_list, turn_idx * size_now)

    return lax.fori_loop(0, row_count // size_now, one_turn, fold_state)


def score_grads(query_blk, key_blk, value_blk, grad_blk, top_blk, total_blk, delta_blk):
    scores = (
        jnp.einsum("sqhd,skhd->sqhk", query_blk, key_blk, preferred_element_type=jnp.float32)
        * SCORE_SCALE
    )
    probability = jnp.exp(scores - top_blk[..., None]) / total_blk[..., None]
    grad_prob = jnp.einsum(
        "sqhd,skhd->sqhk", grad_blk, value_blk, preferred_element_type=jnp.float32
    )
    grad_scores = (probability * (grad_prob - delta_blk[..., None])).astype(jnp.bfloat16)
    return (probability, grad_scores)


def local_any(
    tokens_in,
    cond_vec,
    positions,
    absorbed,
    cotangent,
    norm1_gain,
    qkv_weight,
    out_weight,
    norm2_gain,
    fc1_weight,
    fc1_bias,
    fc2_weight,
    fc2_bias,
    ada_weight,
    ada_bias,
):
    seqs_here, span_len, model_width = tokens_in.shape
    head_shape = (seqs_here, span_len, HEADS, HEAD_DIM)
    stream = tokens_in.astype(jnp.float32)
    modulation = jnp.dot(
        cond_vec, ada_weight, preferred_element_type=jnp.float32
    ) + ada_bias.astype(jnp.float32)
    shift_one, scale_one, gate_one, shift_two, scale_two, gate_two = jnp.split(
        modulation, 6, axis=-1
    )
    gain_one = norm1_gain.astype(jnp.float32)
    gain_two = norm2_gain.astype(jnp.float32)
    normed_f, pull_one = jax.vjp(pre_norm, stream, gain_one, shift_one, scale_one)
    normed_one = normed_f.astype(jnp.bfloat16)
    projected = jnp.dot(normed_one, qkv_weight, preferred_element_type=jnp.float32)
    cos_table, sin_table = rotary_tables(positions)
    turned_pair, pull_rot = jax.vjp(
        lambda query_pre, key_pre: (
            rotate_pos(query_pre, cos_table, sin_table),
            rotate_pos(key_pre, cos_table, sin_table),
        ),
        projected[..., :model_width].reshape(head_shape),
        projected[..., model_width : 2 * model_width].reshape(head_shape),
    )
    queries = turned_pair[0].astype(jnp.bfloat16)
    key_loc = turned_pair[1].astype(jnp.bfloat16).reshape(seqs_here, span_len, model_width)
    value_loc = projected[..., 2 * model_width :].astype(jnp.bfloat16)

    def forward_step(fold_state, part_list, offset):
        run_max, run_sum, run_acc = fold_state
        key_blk = part_list[0].reshape(seqs_here, -1, HEADS, HEAD_DIM)
        value_blk = part_list[1].reshape(seqs_here, -1, HEADS, HEAD_DIM)
        scores = (
            jnp.einsum("sqhd,skhd->sqhk", queries, key_blk, preferred_element_type=jnp.float32)
            * SCORE_SCALE
        )
        new_max = jnp.maximum(run_max, jnp.max(scores, axis=-1))
        raised = jnp.exp(scores - new_max[..., None])
        shrink = jnp.exp(run_max - new_max)
        run_sum = run_sum * shrink + jnp.sum(raised, axis=-1)
        run_acc = run_acc * shrink[..., None] + jnp.einsum(
            "sqhk,skhd->sqhd",
            raised.astype(jnp.bfloat16),
            value_blk,
            preferred_element_type=jnp.float32,
        )
        return (new_max, run_sum, run_acc)

    empty_state = (
        jnp.full((seqs_here, span_len, HEADS), NEG_START, jnp.float32),
        jnp.zeros((seqs_here, span_len, HEADS), jnp.float32),
        jnp.zeros(head_shape, jnp.float32),
    )
    final_max, final_sum, final_acc = over_blocks(
        forward_step,
        empty_state,
        (
            lax.all_gather(key_loc, "ctx", axis=1, tiled=True),
            lax.all_gather(value_loc, "ctx", axis=1, tiled=True),
        ),
    )
    attn_out = final_acc / final_sum[..., None]
    attended = attn_out.reshape(seqs_here, span_len, model_width).astype(jnp.bfloat16)
    branch_att = jnp.dot(attended, out_weight, preferred_element_type=jnp.float32)
    middle = stream + gate_one[:, None, :] * branch_att
    normed_f2, pull_two = jax.vjp(pre_norm, middle, gain_two, shift_two, scale_two)
    normed_two = normed_f2.astype(jnp.bfloat16)
    hidden_pre = jnp.dot(
        normed_two, fc1_weight, preferred_element_type=jnp.float32
    ) + fc1_bias.astype(jnp.float32)
    hidden_f, pull_gelu = jax.vjp(gelu_tanh, hidden_pre)
    hidden = hidden_f.astype(jnp.bfloat16)
    branch_mlp = jnp.dot(hidden, fc2_weight, preferred_element_type=jnp.float32) + fc2_bias.astype(
        jnp.float32
    )
    mixed = (middle + gate_two[:, None, :] * branch_mlp).astype(jnp.bfloat16)
    weighted = cotangent.astype(jnp.float32) * absorbed.astype(jnp.float32)[..., None]
    grad_gate_two = jnp.sum(weighted * branch_mlp, axis=1)
    grad_mlp = (weighted * gate_two[:, None, :]).astype(jnp.bfloat16)
    grad_fc2b = jnp.sum(grad_mlp.astype(jnp.float32), axis=(0, 1))
    grad_fc2 = jnp.einsum("scf,scd->fd", hidden, grad_mlp, preferred_element_type=jnp.float32)
    grad_hidden = jnp.einsum(
        "scd,fd->scf", grad_mlp, fc2_weight, preferred_element_type=jnp.float32
    )
    grad_pre = pull_gelu(grad_hidden)[0].astype(jnp.bfloat16)
    grad_fc1b = jnp.sum(grad_pre.astype(jnp.float32), axis=(0, 1))
    grad_fc1 = jnp.einsum("scd,scf->df", normed_two, grad_pre, preferred_element_type=jnp.float32)
    grad_normed_two = jnp.einsum(
        "scf,df->scd", grad_pre, fc1_weight, preferred_element_type=jnp.float32
    )
    grad_mid_part, grad_gain_two, grad_shift_two, grad_scale_two = pull_two(grad_normed_two)
    grad_middle = weighted + grad_mid_part
    grad_gate_one = jnp.sum(grad_middle * branch_att, axis=1)
    grad_att = (grad_middle * gate_one[:, None, :]).astype(jnp.bfloat16)
    grad_out = jnp.einsum("scd,sce->de", attended, grad_att, preferred_element_type=jnp.float32)
    grad_attended = (
        jnp.einsum("sce,de->scd", grad_att, out_weight, preferred_element_type=jnp.float32)
        .astype(jnp.bfloat16)
        .reshape(head_shape)
    )
    row_delta = jnp.sum(grad_attended.astype(jnp.float32) * attn_out, axis=-1)

    def query_only_step(fold_state, part_list, offset):
        piece_len = part_list[0].shape[1]
        key_blk = part_list[0].reshape(seqs_here, piece_len, HEADS, HEAD_DIM)
        value_blk = part_list[1].reshape(seqs_here, piece_len, HEADS, HEAD_DIM)
        probability, grad_scores = score_grads(
            queries, key_blk, value_blk, grad_attended, final_max, final_sum, row_delta
        )
        return (
            fold_state
            + jnp.einsum(
                "sqhk,skhd->sqhd", grad_scores, key_blk, preferred_element_type=jnp.float32
            )
            * SCORE_SCALE
        )

    start_state = jnp.zeros(head_shape, jnp.float32)
    back_state = over_blocks(
        query_only_step,
        start_state,
        (
            lax.all_gather(key_loc, "ctx", axis=1, tiled=True),
            lax.all_gather(value_loc, "ctx", axis=1, tiled=True),
        ),
    )
    key_heads = key_loc.reshape(head_shape)
    value_heads = value_loc.reshape(head_shape)

    def local_key_step(fold_state, part_list, offset):
        grad_key_loc, grad_value_loc = fold_state
        query_blk = part_list[0].astype(jnp.bfloat16)
        grad_blk = part_list[1].astype(jnp.bfloat16)
        probability, grad_scores = score_grads(
            query_blk, key_heads, value_heads, grad_blk, part_list[2], part_list[3], part_list[4]
        )
        grad_value_loc = grad_value_loc + jnp.einsum(
            "sqhk,sqhd->skhd",
            probability.astype(jnp.bfloat16),
            grad_blk,
            preferred_element_type=jnp.float32,
        )
        grad_key_loc = (
            grad_key_loc
            + jnp.einsum(
                "sqhk,sqhd->skhd", grad_scores, query_blk, preferred_element_type=jnp.float32
            )
            * SCORE_SCALE
        )
        return (grad_key_loc, grad_value_loc)

    key_start = (jnp.zeros(head_shape, jnp.float32), jnp.zeros(head_shape, jnp.float32))
    grad_key_h, grad_value_h = over_blocks(
        local_key_step,
        key_start,
        (
            lax.all_gather(queries.astype(jnp.float32), "ctx", axis=1, tiled=True),
            lax.all_gather(grad_attended.astype(jnp.float32), "ctx", axis=1, tiled=True),
            lax.all_gather(final_max, "ctx", axis=1, tiled=True),
            lax.all_gather(final_sum, "ctx", axis=1, tiled=True),
            lax.all_gather(row_delta, "ctx", axis=1, tiled=True),
        ),
    )
    grad_key_loc = grad_key_h.reshape(seqs_here, span_len, model_width)
    grad_value_loc = grad_value_h.reshape(seqs_here, span_len, model_width)
    grad_query_pre, grad_key_pre = pull_rot((back_state, grad_key_loc.reshape(head_shape)))
    grad_proj = jnp.concatenate(
        [
            grad_query_pre.reshape(seqs_here, span_len, model_width),
            grad_key_pre.reshape(seqs_here, span_len, model_width),
            grad_value_loc,
        ],
        axis=-1,
    ).astype(jnp.bfloat16)
    grad_qkv = jnp.einsum("scd,sce->de", normed_one, grad_proj, preferred_element_type=jnp.float32)
    grad_normed_one = jnp.einsum(
        "sce,de->scd", grad_proj, qkv_weight, preferred_element_type=jnp.float32
    )
    grad_in_part, grad_gain_one, grad_shift_one, grad_scale_one = pull_one(grad_normed_one)
    input_grad = (grad_middle + grad_in_part).astype(jnp.bfloat16)
    partial_mod = jnp.concatenate(
        [
            grad_shift_one,
            grad_scale_one,
            grad_gate_one,
            grad_shift_two,
            grad_scale_two,
            grad_gate_two,
        ],
        axis=-1,
    )
    grad_mod = lax.psum(partial_mod, "ctx")
    cond_grad = jnp.einsum(
        "se,ce->sc",
        grad_mod,
        ada_weight.astype(jnp.float32),
        precision=lax.Precision.HIGHEST,
        preferred_element_type=jnp.float32,
    )
    first_cycle = (lax.axis_index("ctx") == 0).astype(jnp.float32)
    grad_ada = (
        jnp.einsum(
            "sc,se->ce",
            cond_vec.astype(jnp.float32),
            grad_mod,
            precision=lax.Precision.HIGHEST,
            preferred_element_type=jnp.float32,
        )
        * first_cycle
    )
    grad_adab = jnp.sum(grad_mod, axis=0) * first_cycle
    (
        part_g1,
        part_qkv,
        part_out,
        part_g2,
        part_fc1,
        part_fc1b,
        part_fc2,
        part_fc2b,
        part_ada,
        part_adab,
    ) = (
        lax.psum_scatter(grad_gain_one, "dp", scatter_dimension=0, tiled=True),
        lax.psum_scatter(grad_qkv, "dp", scatter_dimension=0, tiled=True),
        lax.psum_scatter(grad_out, "dp", scatter_dimension=0, tiled=True),
        lax.psum_scatter(grad_gain_two, "dp", scatter_dimension=0, tiled=True),
        lax.psum_scatter(grad_fc1, "dp", scatter_dimension=0, tiled=True),
        lax.psum_scatter(grad_fc1b, "dp", scatter_dimension=0, tiled=True),
        lax.psum_scatter(grad_fc2, "dp", scatter_dimension=0, tiled=True),
        lax.psum_scatter(grad_fc2b, "dp", scatter_dimension=0, tiled=True),
        lax.psum_scatter(grad_ada, "dp", scatter_dimension=1, tiled=True),
        lax.psum_scatter(grad_adab, "dp", scatter_dimension=0, tiled=True),
    )
    summed = lax.psum(
        (
            part_g1,
            part_qkv,
            part_out,
            part_g2,
            part_fc1,
            part_fc1b,
            part_fc2,
            part_fc2b,
            part_ada,
            part_adab,
        ),
        "ctx",
    )
    return (mixed, input_grad, cond_grad) + tuple(summed)


def local(*args, ndp, nctx):
    seqs, span, _ = args[0].shape
    if nctx == 2 and seqs == 1 and ndp == 16 and span == 512:
        return local_pair(*args, ndp=ndp)
    return local_any(*args)


def solution(mesh):
    in_specs = (
        P("dp", "ctx", None),
        P("dp", None),
        P("dp", "ctx"),
        P("dp", "ctx"),
        P("dp", "ctx", None),
        P(),
        P(),
        P(),
        P(),
        P(),
        P(),
        P(),
        P(),
        P(),
        P(),
    )
    out_specs = (
        P("dp", "ctx", None),
        P("dp", "ctx", None),
        P("dp", None),
        P("dp"),
        P("dp", None),
        P("dp", None),
        P("dp"),
        P("dp", None),
        P("dp"),
        P("dp", None),
        P("dp"),
        P(None, "dp"),
        P("dp"),
    )
    step = functools.partial(local, ndp=mesh.shape["dp"], nctx=mesh.shape["ctx"])
    return jax.shard_map(step, mesh=mesh, in_specs=in_specs, out_specs=out_specs, check_vma=False)
```

```python
import functools

import jax
import jax.numpy as jnp
import numpy as np
from jax import lax
from jax.experimental import pallas as pl
from jax.experimental.pallas import tpu as pltpu
from jax.sharding import PartitionSpec as P

HEADS = 12
HEAD_DIM = 64
EPS = 1e-05
SCORE_SCALE = 0.125
NEG_START = -1e30
F32, BF16 = jnp.float32, jnp.bfloat16
COST = 2e8
FF = 10
MLP_COLS = 1536
BWD_BLK = 1024


def dot(a, b):
    return jnp.dot(a, b, preferred_element_type=F32)


def dot_tn(a, b):
    return lax.dot_general(a, b, (((0,), (0,)), ((), ())), preferred_element_type=F32)


def dot_nt(a, b):
    return lax.dot_general(a, b, (((1,), (1,)), ((), ())), preferred_element_type=F32)


def sds(shape, dtype):
    return jax.ShapeDtypeStruct(shape, dtype)


def hbm(x):
    return pltpu.with_memory_space_constraint(x, pltpu.HBM)


class Order:
    def __init__(self, place):
        self.place, self.token = place, None

    def call(
        self, body, args, grid, in_specs, out_specs, out_shape, scratch=(), mb=32, us=1.0, aliases=None, after=(),
        name=None,
    ):
        after = list(after) + ([] if self.token is None else [self.token])
        extra, n_in, n_out = len(after), 1 + len(args), len(out_shape)

        def inner(*refs):
            outs = refs[n_in + extra :]
            body(*refs[:n_in], *outs[:n_out], *outs[n_out + 1 :])

        *outs, self.token = pl.pallas_call(
            inner,
            grid_spec=pltpu.PrefetchScalarGridSpec(
                num_scalar_prefetch=1,
                grid=grid,
                in_specs=list(in_specs) + [ANY] * extra,
                out_specs=list(out_specs) + [ANY],
                scratch_shapes=list(scratch),
            ),
            out_shape=list(out_shape) + [sds((8, 128), F32)],
            input_output_aliases=aliases or {},
            compiler_params=pltpu.CompilerParams(vmem_limit_bytes=mb << 20),
            cost_estimate=pl.CostEstimate(flops=int(us * COST), bytes_accessed=1 << 16, transcendentals=0),
            name=name,
        )(self.place, *args, *after)
        return outs


ANY = pl.BlockSpec(memory_space=pl.ANY)


def whole(shape):
    return pl.BlockSpec(shape, lambda *a: (0,) * len(shape))


def layer_stats(stream):
    row_mean = jnp.mean(stream, axis=-1, keepdims=True)
    centred = stream - row_mean
    variance = jnp.mean(centred * centred, axis=-1, keepdims=True)
    inv = lax.rsqrt(variance + EPS)
    return centred * inv, inv


def swap_lanes(x):
    lane = lax.broadcasted_iota(jnp.int32, x.shape, 1) % HEAD_DIM
    half = HEAD_DIM // 2
    return jnp.where(lane < half, pltpu.roll(x, 128 - half, 1), pltpu.roll(x, half, 1))


def mask_half(value, head):
    lane = lax.broadcasted_iota(jnp.int32, value.shape, 1)
    keep = (lane < HEAD_DIM) if head == 0 else (lane >= HEAD_DIM)
    return jnp.where(keep, value, jnp.zeros_like(value))


def attend_body(
    s_ref, ta_ref, tb_ref, cond_ref, ada_ref, adab_ref, gain_ref, wq_ref, wk_ref, wv_ref, pa_ref, pb_ref, freq_ref,
    cot_ref, abs_ref,
    n1_out, q_out, k_out, v_out, cost_ref, sint_ref,
    out_ref, prob_ref, inv_ref, mod_ref, wtd_ref, scores_ref, top_ref, vt_ref, n1_ref, q_ref, k_ref, v_ref,
):
    pair, step = pl.program_id(0), pl.program_id(1)
    span, width = ta_ref.shape
    blk = out_ref.shape[1]

    @pl.when((pair == 0) & (step == 0))
    def _():
        kept = jnp.broadcast_to(abs_ref[...].astype(F32), (128, span)).T[:, 0:1]
        wtd_ref[...] = (cot_ref[...].astype(F32) * kept).astype(BF16)
        cond = jnp.broadcast_to(cond_ref[...].astype(F32), (16, cond_ref.shape[1])).astype(BF16)
        mod_ref[...] = dot(cond, ada_ref[...])[:8] + adab_ref[...].astype(F32)[None, :]
        shift, scale = mod_ref[0:1, 0:width], mod_ref[0:1, width : 2 * width]
        gain = gain_ref[...].astype(F32)[None, :] * (1.0 + scale)
        for half, (t_ref, p_ref) in enumerate(((ta_ref, pa_ref), (tb_ref, pb_ref))):
            rows = slice(half * span, (half + 1) * span)
            angles = freq_ref[...] * p_ref[...].astype(F32)
            cos_h, sin_h = jnp.cos(angles), jnp.sin(angles)
            cos_t, sin_t = rotation(cos_h, sin_h)
            cost_ref[:, rows] = cos_h
            sint_ref[:, rows] = sin_h
            cos_n, sin_n = cos_t.T, sin_t.T
            a_one, _ = layer_stats(t_ref[...].astype(F32))
            normed = (a_one * gain + shift).astype(BF16)
            n1_ref[rows, :] = a_one.astype(BF16)
            q_pre = dot(normed, wq_ref[...])
            k_pre = dot(normed, wk_ref[...])
            v_ref[rows, :] = dot(normed, wv_ref[...]).astype(BF16)
            for p in range(q_pre.shape[1] // 128):
                at = slice(p * 128, (p + 1) * 128)
                part = q_pre[:, at]
                q_ref[rows, at] = (SCORE_SCALE * (part * cos_n + swap_lanes(part) * sin_n)).astype(BF16)
                part = k_pre[:, at]
                k_ref[rows, at] = (part * cos_n + swap_lanes(part) * sin_n).astype(BF16)

    pairs, blocks = pl.num_programs(0), pl.num_programs(1)
    lanes = lambda p: pl.ds(pl.multiple_of(p * 128, 128), 128)
    piece = jnp.minimum(pair * blocks + step, n1_ref.shape[0] // n1_out.shape[0] - 1)
    n1_out[...] = n1_ref[pl.ds(pl.multiple_of(piece * n1_out.shape[0], 128), n1_out.shape[0]), :]
    length = k_ref.shape[0]
    cut = 512

    def queries(p, i, head):
        return mask_half(q_ref[pl.ds(pl.multiple_of(i * blk, blk), blk), lanes(p)], head)

    def top_rows(scores):
        return jnp.max(scores.reshape(scores.shape[0] // 8, 8, blk), axis=0)

    @pl.when((pair == 0) & (step == 0))
    def _():
        vt_ref[...] = v_ref[...].T
        q_0 = queries(0, 0, 0)
        top = None
        for at in range(0, length, cut):
            scores = dot_nt(k_ref[at : at + cut, 0:128], q_0)
            scores_ref[0, at : at + cut] = scores
            top = top_rows(scores) if top is None else jnp.maximum(top, top_rows(scores))
        top_ref[0] = top

    @pl.when(step == 0)
    def _():
        q_out[...] = q_ref[:, lanes(pair)]
        k_out[...] = k_ref[:, lanes(pair)]
        v_out[...] = v_ref[:, lanes(pair)]

    for head in (0, 1):
        if head == 0:
            next_pair, next_step = pair, step
        else:
            wrap = step == blocks - 1
            next_step = jnp.where(wrap, 0, step + 1)
            next_pair = jnp.minimum(jnp.where(wrap, pair + 1, pair), pairs - 1)
        q_next = queries(next_pair, next_step, 1 - head)
        top = jnp.max(top_ref[head], axis=0, keepdims=True)
        rows = pl.ds(pl.multiple_of(pair * 128 + head * HEAD_DIM, HEAD_DIM), HEAD_DIM)
        next_top = sums = part = None
        for at in range(0, length, cut):
            here = slice(at, at + cut)
            scores = dot_nt(k_ref[here, lanes(next_pair)], q_next)
            scores_ref[1 - head, here] = scores
            new_top = top_rows(scores)
            raised = jnp.exp(scores_ref[head, here] - top)
            new_sums = jnp.sum(raised.reshape(cut // 8, 8, blk), axis=0)
            prob = raised.astype(BF16)
            prob_ref[head, here] = prob
            new_part = dot(vt_ref[rows, here], prob)
            next_top = new_top if next_top is None else jnp.maximum(next_top, new_top)
            sums = new_sums if sums is None else sums + new_sums
            part = new_part if part is None else part + new_part
        top_ref[1 - head] = next_top
        inverse = 1.0 / jnp.sum(sums, axis=0, keepdims=True)
        inv_ref[0, head : head + 1, :] = inverse
        out_ref[head * HEAD_DIM : (head + 1) * HEAD_DIM, :] = (part * inverse).astype(BF16)


def attend_call(order, tok, tok_o, cond, ada, adab, gain, qkv_weight, pos, pos_o, cot, absorbed):
    span, width = tok.shape
    length, hw = 2 * span, width // 2
    pairs, blk = hw // 128, 512
    freq = np.power(10000.0, -np.arange(0, HEAD_DIM, 2) / HEAD_DIM).astype(np.float32)[:, None]
    wspec = lambda j: pl.BlockSpec((width, hw), lambda p, i, s: (0, 2 * j + s[0]))
    col = pl.BlockSpec((length, 128), lambda p, i, s: (0, p))
    return order.call(
        attend_body,
        [hbm(tok), tok_o, hbm(cond), hbm(ada), hbm(adab), hbm(gain), *[hbm(qkv_weight)] * 3, hbm(pos), pos_o, hbm(jnp.asarray(freq)), hbm(cot), hbm(absorbed)],
        (pairs, length // blk),
        [whole(tok.shape), whole(tok.shape), whole(cond.shape), whole(ada.shape), whole(adab.shape), whole(gain.shape), wspec(0), wspec(1), wspec(2),
         whole(pos.shape), whole(pos.shape), whole(freq.shape), whole(cot.shape), whole(absorbed.shape)],
        [pl.BlockSpec((length // 4, width), lambda p, i, s: (jnp.minimum(p * (length // blk) + i, 3), 0)),
         col, col, col, whole((HEAD_DIM // 2, length)), whole((HEAD_DIM // 2, length)),
         pl.BlockSpec((128, blk), lambda p, i, s: (p, i)),
         pl.BlockSpec((2, length, blk), lambda p, i, s: (p, 0, i)),
         pl.BlockSpec((1, 8, blk), lambda p, i, s: (p, 0, i)), whole((8, ada.shape[1])), whole(tok.shape)],
        [sds((length, width), BF16)] + [sds((length, hw), BF16)] * 3
        + [sds((HEAD_DIM // 2, length), F32)] * 2
        + [sds((hw, length), BF16), pltpu.HBM((2 * pairs, length, length), BF16), sds((pairs, 8, length), F32),
           sds((8, ada.shape[1]), F32), sds(tok.shape, BF16)],
        scratch=[pltpu.VMEM((2, length, blk), F32), pltpu.VMEM((2, 8, blk), F32), pltpu.VMEM((hw, length), BF16),
                 pltpu.VMEM((length, width), BF16)] + [pltpu.VMEM((length, hw), BF16)] * 3,
        mb=40, us=20, name="attend",
    )


def swap_rows(x):
    half = HEAD_DIM // 2
    return jnp.concatenate([x[half * j : half * (j + 1)] for j in (1, 0, 3, 2)], axis=0)


def rotation(cos_h, sin_h):
    return jnp.concatenate([cos_h] * 4, axis=0), jnp.concatenate([-sin_h, sin_h, -sin_h, sin_h], axis=0)


def attn_bwd_body(
    r, s_ref, prob_ref, inv_ref, gt_ref, out_ref, q_ref, k_ref, v_ref, cost_ref, sint_ref, a_ref,
    mod_ref, gain_ref, wq_ref, wk_ref, wv_ref,
    g_ref, sum_ref, keep_ref, send_ref, vm_ref, kt_ref, dk_acc, dv_acc, acc_ref,
):
    step = pl.program_id(1)
    blk = q_ref.shape[0]

    @pl.when(step == 0)
    def _():
        values = v_ref[...]
        for head in (0, 1):
            vm_ref[head] = mask_half(values, head)
        kt_ref[...] = k_ref[...].T

    queries = q_ref[...]
    grad_t = gt_ref[...].astype(jnp.float32)
    row_id = lax.broadcasted_iota(jnp.int32, (128, blk), 0)
    inverse = jnp.where(row_id < HEAD_DIM, inv_ref[0, 0:1, :], inv_ref[0, 1:2, :])
    grad_t = grad_t * inverse
    product = grad_t * out_ref[...].astype(jnp.float32)
    grad_b = grad_t.astype(jnp.bfloat16)
    dk_new = None
    dq_parts = []
    for head in (0, 1):
        rows = slice(head * HEAD_DIM, (head + 1) * HEAD_DIM)
        delta = jnp.sum(product[rows], axis=0, keepdims=True)
        keep = (row_id < HEAD_DIM) if head == 0 else (row_id >= HEAD_DIM)
        grad_m = jnp.where(keep, grad_b, jnp.zeros_like(grad_b))
        grad_p = jnp.dot(vm_ref[head], grad_b, preferred_element_type=jnp.float32)
        prob = prob_ref[head]
        grad_s = (prob.astype(jnp.float32) * (grad_p - delta)).astype(jnp.bfloat16)
        dv_h = dot_nt(prob, grad_m)
        dk_h = dot(grad_s, mask_half(queries, head))
        if dk_new is None:
            dk_new, dv_new = dk_h, dv_h
        else:
            dk_new, dv_new = dk_new + dk_h, dv_new + dv_h
        dq_parts.append(dot(kt_ref[rows, :], grad_s) * SCORE_SCALE)
    dq_t = jnp.concatenate(dq_parts, axis=0)
    here = pl.ds(pl.multiple_of(step * blk, blk), blk)
    cos_t, sin_t = rotation(cost_ref[:, here], sint_ref[:, here])
    dq_t = dq_t * cos_t - swap_rows(dq_t) * sin_t
    g_ref[here, 0:128] = dq_t.T.astype(jnp.bfloat16)

    @pl.when(step == 0)
    def _():
        dk_acc[...] = dk_new
        dv_acc[...] = dv_new

    @pl.when(step > 0)
    def _():
        dk_acc[...] += dk_new
        dv_acc[...] += dv_new

    @pl.when(step == pl.num_programs(1) - 1)
    def _():
        dk = dk_acc[...]
        cos_t, sin_t = rotation(cost_ref[...], sint_ref[...])
        g_ref[:, 128:256] = (dk * cos_t.T - swap_lanes(dk) * sin_t.T).astype(jnp.bfloat16)
        g_ref[:, 256:384] = dv_acc[...].astype(jnp.bfloat16)
        grads = g_ref[...]
        product = dot_tn(a_ref[...], grads)
        width = a_ref.shape[1]
        column = lambda row: jnp.broadcast_to(row, (128, width)).T
        gain = column(gain_ref[...].astype(F32)[None, :] * (1.0 + mod_ref[0:1, width : 2 * width]))
        shift = column(mod_ref[0:1, 0:width])
        tokens = jnp.sum(grads.astype(F32), axis=0, keepdims=True)
        high = tokens.astype(BF16)
        low = (tokens - high.astype(F32)).astype(BF16)
        row_id = lax.broadcasted_iota(jnp.int32, (16, 384), 0)
        terms = jnp.where(row_id == 0, high, jnp.where(row_id == 1, low, jnp.zeros_like(high)))
        against = None
        for j, w_ref in enumerate((wq_ref, wk_ref, wv_ref)):
            at = slice(j * 128, (j + 1) * 128)
            part = product[:, at]
            acc_ref[:, at] = (part * gain + shift * tokens[:, at]).astype(BF16)
            weights = w_ref[...]
            scaled = part * weights.astype(F32)
            shifted = dot_nt(terms[:, at], weights)
            against = scaled if against is None else against + scaled
            shifts = shifted if j == 0 else shifts + shifted
        new = jnp.concatenate(
            [jnp.sum(shifts, axis=0, keepdims=True), jnp.sum(against.T, axis=0, keepdims=True)], axis=0
        )

        @pl.when(pl.program_id(0) == 0)
        def _():
            sum_ref[0:2, :] = new

        @pl.when(pl.program_id(0) > 0)
        def _():
            sum_ref[0:2, :] += new

        store_parts(s_ref, acc_ref, r, keep_ref, send_ref)


def attn_bwd(
    order, start, count, prob, inverse, grad_t, out_t, queries, keys, values, cos_t, sin_t, a_one,
    mod, gain, qkv_weight, old, block, blocks,
):
    length = keys.shape[0]
    width = a_one.shape[1]
    hw = width // 2
    wspec = lambda j: pl.BlockSpec((width, 128), lambda p, i, s: (0, (2 * j + s[0]) * (hw // 128) + p + start))
    blk = BWD_BLK
    r = width // 16
    col = pl.BlockSpec((length, 128), lambda p, i, s: (0, p + start))
    rowt = pl.BlockSpec((128, blk), lambda p, i, s: (p + start, i))
    out = pl.BlockSpec((2, 4, r, 384), lambda p, i, s: (0, 0, 0, p + block))
    args = [prob, inverse, grad_t, out_t, queries, keys, values, cos_t, sin_t, a_one, mod, gain, qkv_weight, qkv_weight, qkv_weight]
    aliases = {}
    after = []
    if old is not None:
        aliases = {1 + len(args) + j: 2 + j for j in range(2)}
        after = list(old)
    return order.call(
        functools.partial(attn_bwd_body, r), args, (count, length // blk),
        [
            pl.BlockSpec((2, length, blk), lambda p, i, s: (p + start, 0, i)),
            pl.BlockSpec((1, 8, blk), lambda p, i, s: (p + start, 0, i)),
            rowt, rowt,
            pl.BlockSpec((blk, 128), lambda p, i, s: (i, p + start)),
            col, col, whole(cos_t.shape), whole(cos_t.shape), whole(a_one.shape),
            whole(mod.shape), whole(gain.shape), wspec(0), wspec(1), wspec(2),
        ],
        [pl.BlockSpec((length, 384), lambda p, i, s: (0, p)), whole((8, width))] + [out] * 2,
        [sds((length, 384 * count), BF16), sds((8, width), F32)] + [sds((2, 4, r, 384 * blocks), BF16)] * 2,
        scratch=[
            pltpu.VMEM((2, length, 128), BF16),
            pltpu.VMEM((128, length), BF16),
            pltpu.VMEM((length, 128), F32),
            pltpu.VMEM((length, 128), F32),
            pltpu.VMEM((width, 384), BF16),
        ],
        mb=40, us=8.0 * count, aliases=aliases, after=after, name="attn_bwd",
    )


def mix_body(s_ref, own_ref, got_ref, mid_ref, mod_ref, bias_ref, out_ref):
    width = mid_ref.shape[1]
    branch = own_ref[...] + got_ref[...].astype(F32) + bias_ref[...].astype(F32)[None, :]
    out_ref[...] = (mid_ref[...] + mod_ref[0:1, 5 * width : 6 * width] * branch).astype(BF16)


def mix_call(order, own, got, mid, mod, bias):
    span, width = mid.shape
    blk = 256
    row = pl.BlockSpec((blk, width), lambda i, s: (i, 0))
    return order.call(
        mix_body, [own, got, mid, mod, bias], (span // blk,),
        [row] * 3 + [whole(mod.shape), whole(bias.shape)],
        [row], [sds((span, width), BF16)], mb=12, us=2.5, name="mix",
    )[0]


def post_body(s_ref, att_ref, oth_ref, wm_ref, wo_ref, tok_ref, mod_ref, gain_ref, mid_ref, br_ref, n2_ref):
    width = tok_ref.shape[1]
    branch = dot_tn(att_ref[...], wm_ref[...]) + dot_tn(oth_ref[...], wo_ref[...])
    br_ref[...] = branch
    middle = tok_ref[...].astype(F32) + mod_ref[0:1, 2 * width : 3 * width] * branch
    mid_ref[...] = middle
    a_two, _ = layer_stats(middle)
    scale = mod_ref[0:1, 4 * width : 5 * width]
    n2_ref[...] = (
        a_two * (gain_ref[...].astype(F32)[None, :] * (1.0 + scale)) + mod_ref[0:1, 3 * width : 4 * width]
    ).astype(BF16)


def post_call(order, att_t, att_o, out_weight, tok, mod, gain):
    span, width = tok.shape
    hw = width // 2
    blk = 512
    n = span // blk
    row = pl.BlockSpec((blk, width), lambda i, s: (i, 0))
    return order.call(
        post_body, [att_t, att_o, out_weight, out_weight, tok, mod, gain], (n,),
        [
            pl.BlockSpec((hw, blk), lambda i, s: (0, i)),
            pl.BlockSpec((hw, blk), lambda i, s: (0, i + n)),
            pl.BlockSpec((hw, width), lambda i, s: (s[0], 0)),
            pl.BlockSpec((hw, width), lambda i, s: (1 - s[0], 0)),
            row, whole(mod.shape), whole(gain.shape),
        ],
        [row, row, row],
        [sds((span, width), F32), sds((span, width), F32), sds((span, width), BF16)],
        mb=12, us=3, name="post",
    )


def mlp_body(
    s_ref, n2a_ref, n2b_ref, wa_ref, wb_ref, mod_ref, w1_ref, b1_ref, w2_ref,
    hid_ref, pre_ref, b1g_ref, b2g_ref,
):
    step = pl.program_id(0)
    first = step < pl.num_programs(0) // 2
    width = n2a_ref.shape[1]
    x = jnp.where(first, n2a_ref[...], n2b_ref[...])
    wtd = jnp.where(first, wa_ref[...], wb_ref[...]).astype(F32)
    g_mlp = (wtd * mod_ref[0:1, 5 * width : 6 * width]).astype(BF16)
    bias = b1_ref[...].astype(F32)[None, :]
    hf = w1_ref.shape[1]
    bias = jnp.where(s_ref[0] == 0, bias[:, :hf], bias[:, hf:])
    c0 = 0.7978845608028654
    c1 = c0 * 0.044715
    parts = []
    for at in range(0, hf, MLP_COLS):
        cols = slice(at, at + MLP_COLS)
        v = dot(x, w1_ref[:, cols]) + bias[:, cols]
        gh = dot_nt(g_mlp, w2_ref[cols, :])
        v2 = v * v
        th = jnp.tanh(v * (c0 + c1 * v2))
        up = 0.5 + 0.5 * th
        hid_ref[:, cols] = (v * up).astype(BF16)
        slope = up + v * (0.5 - 0.5 * (th * th)) * (c0 + 3.0 * c1 * v2)
        pre = (gh * slope).astype(BF16)
        pre_ref[:, cols] = pre
        parts.append(jnp.sum(pre.astype(F32), axis=0, keepdims=True))
    b1_part = jnp.concatenate(parts, axis=1)
    b2_part = jnp.sum(g_mlp.astype(F32), axis=0, keepdims=True)

    @pl.when(step == 0)
    def _():
        b1g_ref[...] = b1_part
        b2g_ref[...] = b2_part

    @pl.when(step > 0)
    def _():
        b1g_ref[...] += b1_part
        b2g_ref[...] += b2_part


def halves(blk, width, n):
    return [
        pl.BlockSpec((blk, width), lambda i, s: (jnp.minimum(i, n - 1), 0)),
        pl.BlockSpec((blk, width), lambda i, s: (jnp.maximum(i - n, 0), 0)),
    ]


def mlp_call(order, n2a, n2b, wa, wb, mod, w1, b1, w2):
    span, width = n2a.shape
    hf = w1.shape[1] // 2
    blk = 256
    n = span // blk
    row = lambda w: pl.BlockSpec((blk, w), lambda i, s: (i, 0))
    return order.call(
        mlp_body, [n2a, n2b, wa, wb, mod, w1, b1, w2], (2 * n,),
        halves(blk, width, n) + halves(blk, width, n)
        + [
            whole(mod.shape),
            pl.BlockSpec((width, hf), lambda i, s: (0, s[0])),
            whole(b1.shape),
            pl.BlockSpec((hf, width), lambda i, s: (s[0], 0)),
        ],
        [row(hf), row(hf), whole((1, hf)), whole((1, width))],
        [sds((2 * span, hf), BF16), sds((2 * span, hf), BF16),
         sds((1, hf), F32), sds((1, width), F32)],
        mb=24, us=9.6, name="mlp",
    )


def store_parts(s_ref, acc_ref, r, keep_ref, send_ref, base=0):
    mine = s_ref[base + 1]
    for i in range(8):
        rest = sum(((i >> (2 - j)) & 1) * s_ref[base + 6 + j] for j in range(3))
        for ref, bit in ((keep_ref, mine), (send_ref, 1 - mine)):
            at = pl.ds(pl.multiple_of((rest + bit * s_ref[base + 5]) * r, 16), r)
            ref[i // 4, i % 4] = acc_ref[at, :]


def wgrad_body(r, s_ref, la_ref, lb_ref, g_ref, keep_ref, send_ref, acc_ref):
    span = la_ref.shape[0]
    acc_ref[...] = (dot_tn(la_ref[...], g_ref[:span]) + dot_tn(lb_ref[...], g_ref[span:])).astype(BF16)
    store_parts(s_ref, acc_ref, r, keep_ref, send_ref, FF)


def wgrad_call(order, left_a, left_b, right, blk):
    rows, cols = left_a.shape[1], right.shape[1]
    length = right.shape[0]
    r = rows // 16
    out = pl.BlockSpec((2, 4, r, blk), lambda i, s: (0, 0, 0, i))
    return order.call(
        functools.partial(wgrad_body, r), [left_a, left_b, right], (cols // blk,),
        [whole(left_a.shape), whole(left_b.shape), pl.BlockSpec((length, blk), lambda i, s: (0, i))],
        [out] * 2, [sds((2, 4, r, cols), BF16)] * 2,
        scratch=[pltpu.VMEM((rows, blk), BF16)], mb=16, us=4.2, name="wgrad_fc1",
    )


def wgrad2_body(
    r, s_ref, lm_ref, lo_ref, wa_ref, wb_ref, mod_ref, w2_ref, bias_ref, keep_ref, send_ref, gate_ref, acc_ref
):
    step, n = pl.program_id(0), pl.num_programs(0)
    mine = lax.div(step, n // 2) == s_ref[0]
    span, half = wa_ref.shape
    width = 2 * half
    here = pl.ds(pl.multiple_of(s_ref[0] * half, 128), half)
    own, oth = wa_ref[...], wb_ref[...]

    @pl.when(mine)
    def _():
        acc_ref[...] = dot_tn(lm_ref[:span], own) + dot_tn(lm_ref[span:], oth)

    @pl.when(jnp.logical_not(mine))
    def _():
        acc_ref[...] = dot_tn(lo_ref[:span], oth) + dot_tn(lo_ref[span:], own)

    part = jnp.sum(acc_ref[...] * w2_ref[...].astype(F32), axis=0, keepdims=True)

    @pl.when(step == 0)
    def _():
        tokens = jnp.sum(own.astype(F32), axis=0, keepdims=True) + jnp.sum(oth.astype(F32), axis=0, keepdims=True)
        bias = bias_ref[...].astype(F32)[None, :]
        gate_ref[...] = part + tokens * jnp.where(s_ref[0] == 0, bias[:, :half], bias[:, half:])

    @pl.when(step > 0)
    def _():
        gate_ref[...] += part

    gate = mod_ref[0:1, pl.ds(pl.multiple_of(5 * width + s_ref[0] * half, 128), half)]
    za, zb = lax.div(step, 2), lax.rem(step, 2)
    two, four = jnp.where(s_ref[0] == 0, zb, za), jnp.where(s_ref[0] == 0, za, zb)
    for other in range(2):
        for ref, bit in ((keep_ref, s_ref[FF + 1]), (send_ref, 1 - s_ref[FF + 1])):
            at = pl.ds(pl.multiple_of((other * s_ref[FF + 7] + bit * s_ref[FF + 5]) * r, 16), r)
            ref[two, other * 2 + four] = (acc_ref[at, :] * gate).astype(BF16)


def wgrad2_call(order, hidden, hidden_o, wa, wb, mod, w2, bias):
    length, hf = hidden.shape
    span, width = wa.shape
    hw = width // 2
    r = hf // 8
    left = lambda first: pl.BlockSpec((length, 4 * r), lambda i, s: (0, jnp.clip(i - first(s[0]), 0, 1)))
    cols = pl.BlockSpec((span, hw), lambda i, s: (0, s[0]))
    return order.call(
        functools.partial(wgrad2_body, r), [hidden, hidden_o, wa, wb, mod, w2, bias], (4,),
        [left(lambda c: 2 * c), left(lambda c: 2 - 2 * c), cols, cols, whole(mod.shape), pl.BlockSpec((4 * r, hw), lambda i, s: (i, s[0])), whole(bias.shape)],
        [whole((2, 4, r, hw))] * 2 + [whole((1, hw))], [sds((2, 4, r, hw), BF16)] * 2 + [sds((1, hw), F32)],
        scratch=[pltpu.VMEM((4 * r, hw), F32)], mb=16, us=4.5, name="wgrad_fc2",
    )


def fold_body(s_ref, ka, ra, ks, rs, away_ref, stay_ref):
    away_ref[...] = ka[0] + ra[0]
    stay_ref[...] = ks[0] + rs[0]


def fold_call(order, step, keep, got):
    _, count, r, n = keep.shape
    blk = 768 if n % 768 == 0 else 384
    away = pl.BlockSpec((1, count, r, blk), lambda i, s: (1 - s[step], 0, 0, i))
    stay = pl.BlockSpec((1, count, r, blk), lambda i, s: (s[step], 0, 0, i))
    out = pl.BlockSpec((count, r, blk), lambda i, s: (0, 0, i))
    return order.call(
        fold_body, [keep, got, keep, got], (n // blk,), [away, away, stay, stay], [out] * 2,
        [sds((count, r, n), BF16)] * 2, mb=8, us=1.2, name="fold",
    )


def join_ff_body(s_ref, ka_ref, ga_ref, ks_ref, gs_ref, away_in, stay_in, away_ref, stay_ref):
    r = away_in.shape[1]
    width = ka_ref.shape[3]
    for out, one, k_ref, g_ref in ((away_ref, away_in, ka_ref, ga_ref), (stay_ref, stay_in, ks_ref, gs_ref)):
        out[:, :r] = one[...]
        two = k_ref[0] + g_ref[0]
        for q in range(two.shape[1] // r):
            out[:, r:, q * width : (q + 1) * width] = two[:, q * r : (q + 1) * r]


def join_ff_call(order, step, one, two):
    keep, got = two
    away_in, stay_in = one
    specs = []
    for away in (True, False):
        pick = (lambda i, s: (1 - s[step], 0, 0, 0)) if away else (lambda i, s: (s[step], 0, 0, 0))
        specs += [pl.BlockSpec((1,) + keep.shape[1:], pick)] * 2
    count, r, n = away_in.shape
    shape = (count, 2 * r, n)
    return order.call(
        join_ff_body, [keep, got, keep, got, away_in, stay_in], (1,),
        specs + [whole(away_in.shape)] * 2, [whole(shape)] * 2, [sds(shape, BF16)] * 2, mb=12, us=1.2, name="fold_ff",
    )


def relay(step, mine, keep, got):
    sources, rest = 2 ** (step - 2), 2 ** (4 - step)
    stay, away = [], []
    for read in (keep, got):
        for src in range(sources):
            both = [[read(src * 2 * rest + bit * rest + k) for k in range(rest)] for bit in range(2)]
            for k in range(rest):
                stay.append(jnp.where(mine == 0, both[0][k], both[1][k]))
                away.append(jnp.where(mine == 0, both[1][k], both[0][k]))
    return stay, away


def paired(packets):
    return [jnp.concatenate(packets[q : q + 2], axis=0).astype(BF16) for q in range(0, 8, 2)]


def single(pair):
    pairs = [pair(q).astype(F32) for q in range(4)]
    return lambda slot: pairs[slot // 2][(slot % 2) * 8 : (slot % 2) * 8 + 8]


def fold_last_body(s_ref, keep_ref, got_ref, sk_ref, sg_ref, away_ref, stay_ref, small_ref):
    mine = s_ref[2]
    r = keep_ref.shape[2]
    away_ref[:, :r] = keep_ref[1 - mine] + got_ref[1 - mine]
    stay_ref[...] = keep_ref[mine] + got_ref[mine]
    stay, away = relay(2, mine, lambda k: sk_ref[k], lambda k: sg_ref[k])
    for k in range(8):
        small_ref[k] = stay[k]
    for q, pair in enumerate(paired(away)):
        away_ref[q, r : r + 16] = pair


def fold_last_call(order, keep, got, small_keep, small_got):
    _, count, r, n = keep.shape
    args = [keep, got, small_keep, small_got]
    shapes = [((count, r + 16, n), BF16), ((count, r, n), BF16), (small_keep.shape, F32)]
    return order.call(
        fold_last_body, args, (1,), [whole(a.shape) for a in args], [whole(x) for x, _ in shapes],
        [sds(*x) for x in shapes], mb=14, us=1.2, name="fold_last",
    )


def fold_att_body(s_ref, k1_ref, g1_ref, k2_ref, g2_ref, sk_ref, away_ref, stay_ref, small_ref):
    mine = s_ref[3]
    count, r, n = k1_ref.shape[1:]
    for out, at in ((away_ref, 1 - mine), (stay_ref, mine)):
        for j in range(count):
            out[j * r : (j + 1) * r, :n] = k1_ref[at, j] + g1_ref[at, j]
            out[j * r : (j + 1) * r, n:] = k2_ref[at, j] + g2_ref[at * count + j, :r]
    got = single(lambda q: g2_ref[q, r : r + 16])
    stay, away = relay(3, mine, lambda k: sk_ref[k], got)
    for k in range(8):
        small_ref[k] = stay[k]
    w = sk_ref.shape[2]
    for q, pair in enumerate(paired(away)):
        away_ref[count * r :, q * w : (q + 1) * w] = pair


def fold_att_call(order, one, two, got, small_keep):
    _, count, r, n = one[0].shape
    full = n + two.shape[3]
    args = [*one, two, got, small_keep]
    shapes = [((count * r + 16, full), BF16), ((count * r, full), BF16), (small_keep.shape, F32)]
    return order.call(
        fold_att_body, args, (1,), [whole(a.shape) for a in args], [whole(x) for x, _ in shapes],
        [sds(*x) for x in shapes], mb=14, us=1.2, name="fold_att",
    )


def fold_end_body(s_ref, keep_ref, got_ref, sk_ref, away_ref, stay_ref, small_ref):
    mine = s_ref[4]
    r = stay_ref.shape[0]
    for out, at in ((away_ref, 1 - mine), (stay_ref, mine)):
        rows = pl.ds(pl.multiple_of(at * r, 16), r)
        out[:r] = keep_ref[rows] + got_ref[rows]
    w = sk_ref.shape[2]
    got = single(lambda q: got_ref[2 * r :, q * w : (q + 1) * w])
    stay, away = relay(4, mine, lambda k: sk_ref[k], got)
    for k in range(8):
        small_ref[k] = stay[k]
    for q, pair in enumerate(paired(away)):
        away_ref[r:, q * w : (q + 1) * w] = pair


def fold_end_call(order, keep, got, small_keep):
    r, n = keep.shape[0] // 2, keep.shape[1]
    args = [keep, got, small_keep]
    shapes = [((r + 16, n), BF16), ((r, n), BF16), (small_keep.shape, F32)]
    return order.call(
        fold_end_body, args, (1,), [whole(a.shape) for a in args], [whole(x) for x, _ in shapes],
        [sds(*x) for x in shapes], mb=14, us=1.2, name="fold_end",
    )


def add_body(s_ref, a_ref, b_ref, out_ref):
    out_ref[...] = a_ref[...] + b_ref[: out_ref.shape[0]]


def add_call(order, a, b):
    return order.call(
        add_body, [a, b], (1,), [whole(a.shape), whole(b.shape)], [whole(a.shape)], [sds(a.shape, BF16)], mb=8, us=1.0, name="add"
    )[0]


def place_ff_body(s_ref, mine_ref, other_ref, fc1_ref, fc2_ref):
    core = s_ref[0]
    r, n = fc1_ref.shape[0], mine_ref.shape[1]
    width = fc2_ref.shape[1] // 2
    for ref, at in ((mine_ref, core), (other_ref, 1 - core)):
        fc1_ref[:, pl.ds(pl.multiple_of(at * n, 128), n)] = ref[:r].astype(F32)
        cols = pl.ds(pl.multiple_of(at * width, 128), width)
        for q in range(n // width):
            fc2_ref[q * r : (q + 1) * r, cols] = ref[r:, q * width : (q + 1) * width].astype(F32)


def place_ff_call(order, mine, other, hw):
    r, n = mine.shape[0] // 2, mine.shape[1]
    shapes = [(r, 2 * n), (r * (n // hw), 2 * hw)]
    return order.call(
        place_ff_body, [mine, other], (1,), [whole(mine.shape)] * 2, [whole(x) for x in shapes],
        [sds(x, F32) for x in shapes], mb=8, us=1.0, name="place_ff",
    )


def place_att_body(s_ref, mine_ref, other_ref, out_ref, qkv_ref):
    core = s_ref[0]
    width = out_ref.shape[1]
    hw = width // 2
    for ref, at in ((mine_ref, core), (other_ref, 1 - core)):
        out_ref[:, pl.ds(pl.multiple_of(at * hw, 128), hw)] = ref[:, :hw].astype(F32)
        for p in range(hw // 128):
            for j in range(3):
                to = pl.ds(pl.multiple_of(j * width + at * hw + p * 128, 128), 128)
                src = hw + p * 384 + j * 128
                qkv_ref[:, to] = ref[:, src : src + 128].astype(F32)


def place_att_call(order, mine, other, width):
    r = mine.shape[0]
    shapes = [(r, width), (r, 3 * width)]
    return order.call(
        place_att_body, [mine, other], (1,), [whole(mine.shape)] * 2, [whole(x) for x in shapes],
        [sds(x, F32) for x in shapes], mb=8, us=1.0, name="place_att",
    )


def pack_body(
    s_ref, s1a_ref, s1b_ref, s2_ref, gate_ref, b1_ref, b2_ref, g1_ref, g2_ref, mod_ref, cond_ref, out_ref
):
    width = s2_ref.shape[1]
    h = width // 2
    core = s_ref[0]
    mine = jnp.where(core == 0, 1.0, 0.0)
    gain_one, gain_two = g1_ref[...].astype(F32)[None, :], g2_ref[...].astype(F32)[None, :]
    scale_one = 1.0 + mod_ref[0:1, width : 2 * width]
    scale_two = 1.0 + mod_ref[0:1, 4 * width : 5 * width]
    second_one, second_two = s1a_ref[1:2, :] + s1b_ref[1:2, :], s2_ref[1:2, :]
    gate = jnp.concatenate([gate_ref[...] * mine, gate_ref[...] * (1.0 - mine)], axis=1)
    flat = jnp.concatenate(
        [
            s1a_ref[0:1, :] + s1b_ref[0:1, :], second_one * gain_one, s2_ref[2:3, :],
            s2_ref[0:1, :], second_two * gain_two, gate,
        ],
        axis=1,
    )
    b1 = jnp.concatenate([b1_ref[...] * mine, b1_ref[...] * (1.0 - mine)], axis=1)
    sources = (flat, b1, second_one * scale_one, second_two * scale_two, 0.5 * b2_ref[...])
    out_ref[...] = jnp.zeros_like(out_ref)
    cond = 0.5 * cond_ref[...].astype(F32)
    ndp = out_ref.shape[0] - 2
    for d in range(ndp):
        for j, source in enumerate(sources):
            n = source.shape[1] // ndp
            out_ref[d, j : j + 1, 0:n] = source[:, d * n : (d + 1) * n]
        out_ref[d, 5:6, 0:128] = cond
    for j in range(12):
        out_ref[ndp + j // 8, j % 8 : j % 8 + 1, :] = flat[:, j * h : (j + 1) * h]


def pack_call(order, *args):
    h = args[2].shape[1] // 2
    shape = (18, 8, h)
    return order.call(
        pack_body, list(args), (1,), [whole(a.shape) for a in args], [whole(shape)], [sds(shape, F32)],
        mb=8, us=1.0, name="pack",
    )[0]


def deal_body(s_ref, a_ref, b_ref, ada_ref, cg_ref, keep_ref, send_ref, acc_ref):
    acc_ref[...] = a_ref[...] + b_ref[...]
    for i in range(8):
        rest = sum(((i >> (2 - j)) & 1) * s_ref[6 + j] for j in range(3))
        keep_ref[i] = acc_ref[rest + s_ref[1] * s_ref[5]]
        send_ref[i] = acc_ref[rest + (1 - s_ref[1]) * s_ref[5]]
    flat = jnp.concatenate([acc_ref[16 + j // 8, j % 8 : j % 8 + 1, :] for j in range(12)], axis=1)
    high = flat.astype(BF16)
    rest = flat - high.astype(F32)
    mid = rest.astype(BF16)
    low = (rest - mid.astype(F32)).astype(BF16)
    row_id = lax.broadcasted_iota(jnp.int32, (16, flat.shape[1]), 0)
    zero = jnp.zeros_like(high)
    terms = jnp.where(row_id == 0, high, jnp.where(row_id == 1, mid, jnp.where(row_id == 2, low, zero)))
    cg_ref[...] = jnp.sum(dot_nt(terms, ada_ref[...]), axis=0, keepdims=True)


def deal_call(order, mine, got, ada):
    shape = (8,) + mine.shape[1:]
    return order.call(
        deal_body, [mine, got, ada], (1,), [whole(mine.shape), whole(mine.shape), whole(ada.shape)],
        [whole((1, ada.shape[0])), whole(shape), whole(shape)],
        [sds((1, ada.shape[0]), F32), sds(shape, F32), sds(shape, F32)],
        scratch=[pltpu.VMEM(mine.shape, F32)], mb=8, us=1.0, name="deal",
    )


def last_body(s_ref, got_ref, sk_ref, ada_ref, adab_ref, b1_ref, g1_ref, g2_ref, b2_ref):
    r, w = got_ref.shape[0] - 16, sk_ref.shape[2]
    got = single(lambda q: got_ref[r:, q * w : (q + 1) * w])
    parts = [sk_ref[k] for k in range(8)] + [got(k) for k in range(8)]
    sums = parts[0]
    for part in parts[1:]:
        sums = sums + part
    cond = jnp.concatenate([part[5:6, 0:128] for part in parts], axis=0)
    grads = jnp.concatenate([part[0:1] for part in parts], axis=0)
    ada = lax.dot_general(
        cond, grads, (((0,), (0,)), ((), ())), precision=lax.Precision.HIGHEST, preferred_element_type=F32
    )
    ada_ref[...] = ada[:, : ada_ref.shape[1]]
    for j, ref in enumerate((adab_ref, b1_ref, g1_ref, g2_ref, b2_ref)):
        ref[...] = sums[j : j + 1, : ref.shape[1]]


def last_call(order, got, small_keep, ndp):
    h = small_keep.shape[2]
    na, nb, nc = 12 * h // ndp, 2 * h // ndp, 8 * h // ndp
    shapes = [(128, na), (1, na), (1, nc), (1, nb), (1, nb), (1, nb)]
    args = [got, small_keep]
    return order.call(
        last_body, args, (1,), [whole(a.shape) for a in args], [whole(x) for x in shapes],
        [sds(x, F32) for x in shapes], mb=8, us=1.0, name="small_last",
    )


def part_body(nt, s_ref, g_ref, w_ref, own_ref, oth_ref):
    step = pl.program_id(0)
    half = pl.num_programs(0) // 2
    part = dot_nt(g_ref[...], w_ref[...]) if nt else dot(g_ref[...], w_ref[...])

    @pl.when(step < half)
    def _():
        oth_ref[...] = part.astype(BF16)

    @pl.when(step >= half)
    def _():
        own_ref[...] = part


def part_call(order, nt, g, w):
    length, hf = g.shape
    width = w.shape[0] if nt else w.shape[1]
    blk = 512
    n = length // 2 // blk
    wspec = (
        pl.BlockSpec((width, hf), lambda i, s: (0, s[0]))
        if nt
        else pl.BlockSpec((hf, width), lambda i, s: (s[0], 0))
    )
    return order.call(
        functools.partial(part_body, nt), [g, w], (2 * n,),
        [pl.BlockSpec((blk, hf), lambda i, s: ((i + n) % (2 * n), 0)), wspec],
        [
            pl.BlockSpec((blk, width), lambda i, s: (jnp.maximum(i - n, 0), 0)),
            pl.BlockSpec((blk, width), lambda i, s: (jnp.minimum(i, n - 1), 0)),
        ],
        [sds((length // 2, width), F32), sds((length // 2, width), BF16)],
        mb=12, us=4.2, name="part",
    )


def norm2_body(s_ref, own_ref, got_ref, mid_ref, br_ref, wtd_ref, mod_ref, gain_ref, gmid_ref, gatt_ref, sum_ref):
    width = mid_ref.shape[1]
    g = own_ref[...] + got_ref[...].astype(F32)
    a_two, inv = layer_stats(mid_ref[...])
    ga = g * (gain_ref[...].astype(F32)[None, :] * (1.0 + mod_ref[0:1, 4 * width : 5 * width]))
    gaa = ga * a_two
    g_mid = wtd_ref[...].astype(F32) + inv * (
        ga - jnp.mean(ga, -1, keepdims=True) - a_two * jnp.mean(gaa, -1, keepdims=True)
    )
    gmid_ref[...] = g_mid
    gatt_ref[...] = (g_mid * mod_ref[0:1, 2 * width : 3 * width]).astype(BF16)
    sums = jnp.concatenate(
        [
            jnp.sum(g, axis=0, keepdims=True),
            jnp.sum(g * a_two, axis=0, keepdims=True),
            jnp.sum(g_mid * br_ref[...], axis=0, keepdims=True),
        ],
        axis=0,
    )

    @pl.when(pl.program_id(0) == 0)
    def _():
        sum_ref[...] = jnp.zeros_like(sum_ref)

    sum_ref[0:3, :] += sums


def norm2_call(order, own, got, mid, br, wtd, mod, gain):
    span, width = mid.shape
    blk = 512
    row = pl.BlockSpec((blk, width), lambda i, s: (i, 0))
    return order.call(
        norm2_body, [own, got, mid, br, wtd, mod, gain], (span // blk,),
        [row] * 5 + [whole(mod.shape), whole(gain.shape)],
        [row, row, whole((8, width))],
        [sds((span, width), F32), sds((span, width), BF16), sds((8, width), F32)],
        mb=12, us=3, name="norm2",
    )


def oproj_body(r, s_ref, w_ref, ga_ref, gb_ref, am_ref, ao_ref, gt_ref, keep_ref, send_ref, acc_ref):
    span = ga_ref.shape[0]
    half = am_ref.shape[0]
    core = s_ref[0]
    w = w_ref[...]
    gt_ref[:, :span] = dot_nt(w, ga_ref[...]).astype(BF16)
    gt_ref[:, span:] = dot_nt(w, gb_ref[...]).astype(BF16)
    cols = pl.ds(pl.multiple_of(core * half, 128), half)
    gac, gbc = ga_ref[:, cols], gb_ref[:, cols]
    mine = dot(am_ref[:, :span], gac) + dot(am_ref[:, span:], gbc)
    other = dot(ao_ref[:, span:], gac) + dot(ao_ref[:, :span], gbc)
    acc_ref[pl.ds(pl.multiple_of(core * half, 16), half), :] = mine.astype(BF16)
    acc_ref[pl.ds(pl.multiple_of((1 - core) * half, 16), half), :] = other.astype(BF16)
    store_parts(s_ref, acc_ref, r, keep_ref, send_ref)


def oproj_call(order, blocks, out_weight, ga, gb, att_t, att_o):
    span, width = ga.shape
    hw = width // 2
    r = width // 16
    out = pl.BlockSpec((2, 4, r, hw), lambda i, s: (0, 0, 0, 0))
    return order.call(
        functools.partial(oproj_body, r), [out_weight, ga, gb, att_t, att_o], (1,),
        [pl.BlockSpec((hw, width), lambda i, s: (s[0], 0)), whole(ga.shape), whole(ga.shape),
         whole(att_t.shape), whole(att_t.shape)],
        [whole((hw, 2 * span))] + [out] * 2,
        [sds((hw, 2 * span), BF16)] + [sds((2, 4, r, blocks * hw), BF16)] * 2,
        scratch=[pltpu.VMEM((width, hw), BF16)], mb=8, us=3, name="oproj",
    )


def norm1_body(s_ref, own_ref, got_ref, tok_ref, gmid_ref, mod_ref, gain_ref, out_ref):
    width = tok_ref.shape[1]
    g = own_ref[...] + got_ref[...].astype(F32)
    a_one, inv = layer_stats(tok_ref[...].astype(F32))
    ga = g * (gain_ref[...].astype(F32)[None, :] * (1.0 + mod_ref[0:1, width : 2 * width]))
    gaa = ga * a_one
    out_ref[...] = (
        gmid_ref[...]
        + inv * (ga - jnp.mean(ga, -1, keepdims=True) - a_one * jnp.mean(gaa, -1, keepdims=True))
    ).astype(BF16)


def norm1_call(order, own, got, tok, gmid, mod, gain):
    span, width = tok.shape
    blk = 256
    row = pl.BlockSpec((blk, width), lambda i, s: (i, 0))
    return order.call(
        norm1_body, [own, got, tok, gmid, mod, gain], (span // blk,),
        [row] * 4 + [whole(mod.shape), whole(gain.shape)], [row], [sds((span, width), BF16)],
        mb=12, us=3, name="norm1",
    )[0]


def dgrad_body(np_, s_ref, *refs):
    gs, (wq_ref, wk_ref, wv_ref), out_ref = refs[:np_], refs[np_ : np_ + 3], refs[np_ + 3]
    total = None
    for j, w_ref in enumerate((wq_ref, wk_ref, wv_ref)):
        left = jnp.concatenate(
            [g[:, at + j * 128 : at + (j + 1) * 128] for g in gs for at in range(0, g.shape[1], 384)], axis=1
        )
        part = dot_nt(left, w_ref[...])
        total = part if total is None else total + part
    out_ref[...] = total.astype(out_ref.dtype)


def dgrad_call(order, gs, qkv_weight, half):
    span = gs[0].shape[0] // 2
    width = qkv_weight.shape[0]
    hw = width // 2
    wspec = lambda j: pl.BlockSpec((width, hw), lambda i, s: (0, 2 * j + s[0]))
    return order.call(
        functools.partial(dgrad_body, len(gs)), [*gs, qkv_weight, qkv_weight, qkv_weight], (1,),
        [pl.BlockSpec((span, g.shape[1]), lambda i, s: (half, 0)) for g in gs] + [wspec(0), wspec(1), wspec(2)],
        [whole((span, width))], [sds((span, width), BF16 if half else F32)], mb=12, us=2.0, name="dgrad",
    )[0]


class Grid:
    ATT_ORDERS = ((1, 2, 4, 8), (2, 1, 8, 4))
    FF_ORDERS = ((1, 4, 2, 8), (2, 8, 1, 4))

    def __init__(self, ndp):
        self.index = lax.axis_index("dp")
        core = lax.axis_index("ctx")
        place = [core]
        self.pairs = []
        for orders in (self.ATT_ORDERS, self.FF_ORDERS):
            masks = [jnp.where(core == 0, a, b) for a, b in zip(*orders)]
            bits = [jnp.where((self.index & m) > 0, 1, 0) for m in masks]
            place += [*bits, *masks, self.index // 4, self.index]
            self.pairs.append(
                [[(2 * i + c, 2 * (i ^ orders[c][step]) + c) for i in range(ndp) for c in range(2)] for step in range(4)]
            )
        self.place = jnp.stack(place).astype(jnp.int32)


class Job:
    def __init__(self, pairs, base):
        self.pairs, self.base, self.step = pairs, base, 0

    def start(self, keep, send):
        self.keep = keep
        self.got = lax.ppermute(send, ("dp", "ctx"), self.pairs[self.step])
        self.step += 1

    def parts(self):
        shape = self.keep.shape
        if self.step > 1:
            shape = (2, shape[0] // 2) + shape[1:]
        return self.keep.reshape(shape), self.got.reshape(shape)

    def fold(self, order):
        away, stay = self.split(order)
        self.start(stay, away)

    def split(self, order):
        return fold_call(order, self.base + self.step + 1, *self.parts())

    def last(self):
        return self.keep[0], self.got[0]


def join(order, fold, one, two):
    job = Job(two.pairs, two.base)
    job.step = two.step
    away, stay = fold(order, job.base + job.step + 1, one if isinstance(one, tuple) else one.parts(), two.parts())
    job.start(stay, away)
    return job


def local_pair(
    tokens_in, cond_vec, positions, absorbed, cotangent, norm1_gain, qkv_weight, out_weight,
    norm2_gain, fc1_weight, fc1_bias, fc2_weight, fc2_bias, ada_weight, ada_bias, *, ndp,
):
    _, span, width = tokens_in.shape
    hw = width // 2
    grid = Grid(ndp)
    order = Order(grid.place)
    swap = lambda v: lax.ppermute(v, "ctx", [(0, 1), (1, 0)])

    tok = tokens_in[0]
    tok_o = swap(tok)
    pos_o = swap(positions)

    a_one, queries, keys, values, cos_t, sin_t, att_t, prob, inverse, mod, wtd = attend_call(
        order, tok, tok_o, cond_vec, ada_weight, ada_bias, norm1_gain, qkv_weight, positions, pos_o,
        cotangent[0], absorbed,
    )
    wtd_o = swap(wtd)
    att_o = swap(att_t)
    middle, branch, n2 = post_call(order, att_t, att_o, out_weight, hbm(tok), mod, norm2_gain)
    n2_o = swap(n2)
    hidden, g_pre, b1_sum, b2_sum = mlp_call(
        order, n2, n2_o, wtd, wtd_o, mod, fc1_weight, fc1_bias, fc2_weight
    )
    hidden_o = swap(hidden)
    fc1, fc2 = (Job(grid.pairs[1], FF) for _ in range(2))
    rest, last = (Job(grid.pairs[0], 0) for _ in range(2))
    fc1.start(*wgrad_call(order, n2, n2_o, g_pre, 768))
    pn_own, pn_oth = part_call(order, True, g_pre, fc1_weight)
    pn_got = swap(pn_oth)
    *bufs, gate_sum = wgrad2_call(order, hidden, hidden_o, wtd, wtd_o, mod, fc2_weight, fc2_bias)
    fc2.start(*bufs)
    pm_own, pm_oth = part_call(order, False, hidden, fc2_weight)
    pm_got = swap(pm_oth)
    fc1.fold(order)
    g_mid, g_att, sums2 = norm2_call(order, pn_own, pn_got, middle, branch, wtd, mod, norm2_gain)
    g_att_o = swap(g_att)
    g_attn_t, *bufs = oproj_call(order, 3, out_weight, g_att, g_att_o, att_t, att_o)

    def back(start, count, old, block, blocks):
        return attn_bwd(
            order, start, count, hbm(prob), inverse, g_attn_t, att_t, queries, keys, values, cos_t, sin_t,
            a_one, mod, norm1_gain, qkv_weight, old, block, blocks,
        )

    pairs = hw // 128
    g_a, sums_a, *bufs = back(0, pairs - 1, bufs, 1, pairs)
    rest.start(*bufs)
    fc2.fold(order)
    fc1.fold(order)
    g_b, sums_b, *bufs = back(pairs - 1, 1, None, 0, 1)
    last.start(*bufs)
    fc1_split = fc1.split(order)
    packet = pack_call(
        order, sums_a, sums_b, sums2, gate_sum, b1_sum, b2_sum, norm1_gain, norm2_gain, mod, cond_vec
    )
    packet_o = swap(packet)
    d_got = swap(dgrad_call(order, [g_a, g_b], qkv_weight, 1))
    fc2.fold(order)
    rest.fold(order)
    cond_grad, small_keep, send = deal_call(order, packet, packet_o, ada_weight)
    along = lambda step, v: lax.ppermute(v, ("dp", "ctx"), grid.pairs[0][step - 1])
    small_got = along(1, send)
    d_own = dgrad_call(order, [g_a, g_b], qkv_weight, 0)
    ff = join(order, join_ff_call, tuple(fc1_split), fc2)
    away, last_keep, small_keep = fold_last_call(order, *last.parts(), small_keep, small_got)
    last_got = along(2, away)
    input_grad = norm1_call(order, d_own, d_got, tok, g_mid, mod, norm1_gain)
    away, keep, small_keep = fold_att_call(
        order, rest.parts(), last_keep.reshape((2, 2) + last_keep.shape[1:]), last_got, small_keep
    )
    got = along(3, away)
    ff_sum = add_call(order, *ff.last())
    ff_other = swap(ff_sum)
    fc1_grad, fc2_grad = place_ff_call(order, ff_sum, ff_other, hw)
    away, keep, small_keep = fold_end_call(order, keep, got, small_keep)
    got = along(4, away)
    mixed = mix_call(order, pm_own, pm_got, middle, mod, fc2_bias)
    att_sum = add_call(order, keep, got)
    att_other = swap(att_sum)
    ada_grad, ada_bias_grad, fc1_bias_grad, norm1_grad, norm2_grad, fc2_bias_grad = last_call(
        order, got, small_keep, ndp
    )
    out_grad, qkv_grad = place_att_call(order, att_sum, att_other, width)
    return (
        mixed[None], input_grad[None], cond_grad, norm1_grad[0], qkv_grad, out_grad, norm2_grad[0],
        fc1_grad, fc1_bias_grad[0], fc2_grad, fc2_bias_grad[0], ada_grad, ada_bias_grad[0],
    )


def layer_norm(stream):
    row_mean = jnp.mean(stream, axis=-1, keepdims=True)
    centred = stream - row_mean
    variance = jnp.mean(centred * centred, axis=-1, keepdims=True)
    return centred * lax.rsqrt(variance + EPS)


def pre_norm(stream, norm_gain, shift_vec, scale_vec):
    return layer_norm(stream) * norm_gain * (1.0 + scale_vec[:, None, :]) + shift_vec[:, None, :]


def gelu_tanh(stream):
    return jax.nn.gelu(stream, approximate=True)


def block_rows(row_count):
    size_now = row_count
    while size_now > 512 and size_now % 2 == 0:
        size_now = size_now // 2
    return size_now


def rotary_tables(positions):
    inv_freq = 10000.0 ** (-jnp.arange(0, HEAD_DIM, 2).astype(jnp.float32) / HEAD_DIM)
    angles = positions.astype(jnp.float32)[..., None] * inv_freq
    cos_table = jnp.concatenate([jnp.cos(angles), jnp.cos(angles)], axis=-1)[..., None, :]
    sin_table = jnp.concatenate([jnp.sin(angles), jnp.sin(angles)], axis=-1)[..., None, :]
    return (cos_table, sin_table)


def rotate_pos(stream, cos_table, sin_table):
    half_dim = stream.shape[-1] // 2
    turned = jnp.concatenate([-stream[..., half_dim:], stream[..., :half_dim]], axis=-1)
    return stream * cos_table + turned * sin_table


def over_blocks(step_fn, fold_state, pieces):
    row_count = pieces[0].shape[1]
    size_now = block_rows(row_count)

    def one_turn(turn_idx, inner_state):
        part_list = tuple(
            (
                lax.dynamic_slice_in_dim(member, turn_idx * size_now, size_now, 1)
                for member in pieces
            )
        )
        return step_fn(inner_state, part_list, turn_idx * size_now)

    return lax.fori_loop(0, row_count // size_now, one_turn, fold_state)


def score_grads(query_blk, key_blk, value_blk, grad_blk, top_blk, total_blk, delta_blk):
    scores = (
        jnp.einsum("sqhd,skhd->sqhk", query_blk, key_blk, preferred_element_type=jnp.float32)
        * SCORE_SCALE
    )
    probability = jnp.exp(scores - top_blk[..., None]) / total_blk[..., None]
    grad_prob = jnp.einsum(
        "sqhd,skhd->sqhk", grad_blk, value_blk, preferred_element_type=jnp.float32
    )
    grad_scores = (probability * (grad_prob - delta_blk[..., None])).astype(jnp.bfloat16)
    return (probability, grad_scores)


def local_any(
    tokens_in,
    cond_vec,
    positions,
    absorbed,
    cotangent,
    norm1_gain,
    qkv_weight,
    out_weight,
    norm2_gain,
    fc1_weight,
    fc1_bias,
    fc2_weight,
    fc2_bias,
    ada_weight,
    ada_bias,
):
    seqs_here, span_len, model_width = tokens_in.shape
    head_shape = (seqs_here, span_len, HEADS, HEAD_DIM)
    stream = tokens_in.astype(jnp.float32)
    modulation = jnp.dot(
        cond_vec, ada_weight, preferred_element_type=jnp.float32
    ) + ada_bias.astype(jnp.float32)
    shift_one, scale_one, gate_one, shift_two, scale_two, gate_two = jnp.split(
        modulation, 6, axis=-1
    )
    gain_one = norm1_gain.astype(jnp.float32)
    gain_two = norm2_gain.astype(jnp.float32)
    normed_f, pull_one = jax.vjp(pre_norm, stream, gain_one, shift_one, scale_one)
    normed_one = normed_f.astype(jnp.bfloat16)
    projected = jnp.dot(normed_one, qkv_weight, preferred_element_type=jnp.float32)
    cos_table, sin_table = rotary_tables(positions)
    turned_pair, pull_rot = jax.vjp(
        lambda query_pre, key_pre: (
            rotate_pos(query_pre, cos_table, sin_table),
            rotate_pos(key_pre, cos_table, sin_table),
        ),
        projected[..., :model_width].reshape(head_shape),
        projected[..., model_width : 2 * model_width].reshape(head_shape),
    )
    queries = turned_pair[0].astype(jnp.bfloat16)
    key_loc = turned_pair[1].astype(jnp.bfloat16).reshape(seqs_here, span_len, model_width)
    value_loc = projected[..., 2 * model_width :].astype(jnp.bfloat16)

    def forward_step(fold_state, part_list, offset):
        run_max, run_sum, run_acc = fold_state
        key_blk = part_list[0].reshape(seqs_here, -1, HEADS, HEAD_DIM)
        value_blk = part_list[1].reshape(seqs_here, -1, HEADS, HEAD_DIM)
        scores = (
            jnp.einsum("sqhd,skhd->sqhk", queries, key_blk, preferred_element_type=jnp.float32)
            * SCORE_SCALE
        )
        new_max = jnp.maximum(run_max, jnp.max(scores, axis=-1))
        raised = jnp.exp(scores - new_max[..., None])
        shrink = jnp.exp(run_max - new_max)
        run_sum = run_sum * shrink + jnp.sum(raised, axis=-1)
        run_acc = run_acc * shrink[..., None] + jnp.einsum(
            "sqhk,skhd->sqhd",
            raised.astype(jnp.bfloat16),
            value_blk,
            preferred_element_type=jnp.float32,
        )
        return (new_max, run_sum, run_acc)

    empty_state = (
        jnp.full((seqs_here, span_len, HEADS), NEG_START, jnp.float32),
        jnp.zeros((seqs_here, span_len, HEADS), jnp.float32),
        jnp.zeros(head_shape, jnp.float32),
    )
    final_max, final_sum, final_acc = over_blocks(
        forward_step,
        empty_state,
        (
            lax.all_gather(key_loc, "ctx", axis=1, tiled=True),
            lax.all_gather(value_loc, "ctx", axis=1, tiled=True),
        ),
    )
    attn_out = final_acc / final_sum[..., None]
    attended = attn_out.reshape(seqs_here, span_len, model_width).astype(jnp.bfloat16)
    branch_att = jnp.dot(attended, out_weight, preferred_element_type=jnp.float32)
    middle = stream + gate_one[:, None, :] * branch_att
    normed_f2, pull_two = jax.vjp(pre_norm, middle, gain_two, shift_two, scale_two)
    normed_two = normed_f2.astype(jnp.bfloat16)
    hidden_pre = jnp.dot(
        normed_two, fc1_weight, preferred_element_type=jnp.float32
    ) + fc1_bias.astype(jnp.float32)
    hidden_f, pull_gelu = jax.vjp(gelu_tanh, hidden_pre)
    hidden = hidden_f.astype(jnp.bfloat16)
    branch_mlp = jnp.dot(hidden, fc2_weight, preferred_element_type=jnp.float32) + fc2_bias.astype(
        jnp.float32
    )
    mixed = (middle + gate_two[:, None, :] * branch_mlp).astype(jnp.bfloat16)
    weighted = cotangent.astype(jnp.float32) * absorbed.astype(jnp.float32)[..., None]
    grad_gate_two = jnp.sum(weighted * branch_mlp, axis=1)
    grad_mlp = (weighted * gate_two[:, None, :]).astype(jnp.bfloat16)
    grad_fc2b = jnp.sum(grad_mlp.astype(jnp.float32), axis=(0, 1))
    grad_fc2 = jnp.einsum("scf,scd->fd", hidden, grad_mlp, preferred_element_type=jnp.float32)
    grad_hidden = jnp.einsum(
        "scd,fd->scf", grad_mlp, fc2_weight, preferred_element_type=jnp.float32
    )
    grad_pre = pull_gelu(grad_hidden)[0].astype(jnp.bfloat16)
    grad_fc1b = jnp.sum(grad_pre.astype(jnp.float32), axis=(0, 1))
    grad_fc1 = jnp.einsum("scd,scf->df", normed_two, grad_pre, preferred_element_type=jnp.float32)
    grad_normed_two = jnp.einsum(
        "scf,df->scd", grad_pre, fc1_weight, preferred_element_type=jnp.float32
    )
    grad_mid_part, grad_gain_two, grad_shift_two, grad_scale_two = pull_two(grad_normed_two)
    grad_middle = weighted + grad_mid_part
    grad_gate_one = jnp.sum(grad_middle * branch_att, axis=1)
    grad_att = (grad_middle * gate_one[:, None, :]).astype(jnp.bfloat16)
    grad_out = jnp.einsum("scd,sce->de", attended, grad_att, preferred_element_type=jnp.float32)
    grad_attended = (
        jnp.einsum("sce,de->scd", grad_att, out_weight, preferred_element_type=jnp.float32)
        .astype(jnp.bfloat16)
        .reshape(head_shape)
    )
    row_delta = jnp.sum(grad_attended.astype(jnp.float32) * attn_out, axis=-1)

    def query_only_step(fold_state, part_list, offset):
        piece_len = part_list[0].shape[1]
        key_blk = part_list[0].reshape(seqs_here, piece_len, HEADS, HEAD_DIM)
        value_blk = part_list[1].reshape(seqs_here, piece_len, HEADS, HEAD_DIM)
        probability, grad_scores = score_grads(
            queries, key_blk, value_blk, grad_attended, final_max, final_sum, row_delta
        )
        return (
            fold_state
            + jnp.einsum(
                "sqhk,skhd->sqhd", grad_scores, key_blk, preferred_element_type=jnp.float32
            )
            * SCORE_SCALE
        )

    start_state = jnp.zeros(head_shape, jnp.float32)
    back_state = over_blocks(
        query_only_step,
        start_state,
        (
            lax.all_gather(key_loc, "ctx", axis=1, tiled=True),
            lax.all_gather(value_loc, "ctx", axis=1, tiled=True),
        ),
    )
    key_heads = key_loc.reshape(head_shape)
    value_heads = value_loc.reshape(head_shape)

    def local_key_step(fold_state, part_list, offset):
        grad_key_loc, grad_value_loc = fold_state
        query_blk = part_list[0].astype(jnp.bfloat16)
        grad_blk = part_list[1].astype(jnp.bfloat16)
        probability, grad_scores = score_grads(
            query_blk, key_heads, value_heads, grad_blk, part_list[2], part_list[3], part_list[4]
        )
        grad_value_loc = grad_value_loc + jnp.einsum(
            "sqhk,sqhd->skhd",
            probability.astype(jnp.bfloat16),
            grad_blk,
            preferred_element_type=jnp.float32,
        )
        grad_key_loc = (
            grad_key_loc
            + jnp.einsum(
                "sqhk,sqhd->skhd", grad_scores, query_blk, preferred_element_type=jnp.float32
            )
            * SCORE_SCALE
        )
        return (grad_key_loc, grad_value_loc)

    key_start = (jnp.zeros(head_shape, jnp.float32), jnp.zeros(head_shape, jnp.float32))
    grad_key_h, grad_value_h = over_blocks(
        local_key_step,
        key_start,
        (
            lax.all_gather(queries.astype(jnp.float32), "ctx", axis=1, tiled=True),
            lax.all_gather(grad_attended.astype(jnp.float32), "ctx", axis=1, tiled=True),
            lax.all_gather(final_max, "ctx", axis=1, tiled=True),
            lax.all_gather(final_sum, "ctx", axis=1, tiled=True),
            lax.all_gather(row_delta, "ctx", axis=1, tiled=True),
        ),
    )
    grad_key_loc = grad_key_h.reshape(seqs_here, span_len, model_width)
    grad_value_loc = grad_value_h.reshape(seqs_here, span_len, model_width)
    grad_query_pre, grad_key_pre = pull_rot((back_state, grad_key_loc.reshape(head_shape)))
    grad_proj = jnp.concatenate(
        [
            grad_query_pre.reshape(seqs_here, span_len, model_width),
            grad_key_pre.reshape(seqs_here, span_len, model_width),
            grad_value_loc,
        ],
        axis=-1,
    ).astype(jnp.bfloat16)
    grad_qkv = jnp.einsum("scd,sce->de", normed_one, grad_proj, preferred_element_type=jnp.float32)
    grad_normed_one = jnp.einsum(
        "sce,de->scd", grad_proj, qkv_weight, preferred_element_type=jnp.float32
    )
    grad_in_part, grad_gain_one, grad_shift_one, grad_scale_one = pull_one(grad_normed_one)
    input_grad = (grad_middle + grad_in_part).astype(jnp.bfloat16)
    partial_mod = jnp.concatenate(
        [
            grad_shift_one,
            grad_scale_one,
            grad_gate_one,
            grad_shift_two,
            grad_scale_two,
            grad_gate_two,
        ],
        axis=-1,
    )
    grad_mod = lax.psum(partial_mod, "ctx")
    cond_grad = jnp.einsum(
        "se,ce->sc",
        grad_mod,
        ada_weight.astype(jnp.float32),
        precision=lax.Precision.HIGHEST,
        preferred_element_type=jnp.float32,
    )
    first_cycle = (lax.axis_index("ctx") == 0).astype(jnp.float32)
    grad_ada = (
        jnp.einsum(
            "sc,se->ce",
            cond_vec.astype(jnp.float32),
            grad_mod,
            precision=lax.Precision.HIGHEST,
            preferred_element_type=jnp.float32,
        )
        * first_cycle
    )
    grad_adab = jnp.sum(grad_mod, axis=0) * first_cycle
    (
        part_g1,
        part_qkv,
        part_out,
        part_g2,
        part_fc1,
        part_fc1b,
        part_fc2,
        part_fc2b,
        part_ada,
        part_adab,
    ) = (
        lax.psum_scatter(grad_gain_one, "dp", scatter_dimension=0, tiled=True),
        lax.psum_scatter(grad_qkv, "dp", scatter_dimension=0, tiled=True),
        lax.psum_scatter(grad_out, "dp", scatter_dimension=0, tiled=True),
        lax.psum_scatter(grad_gain_two, "dp", scatter_dimension=0, tiled=True),
        lax.psum_scatter(grad_fc1, "dp", scatter_dimension=0, tiled=True),
        lax.psum_scatter(grad_fc1b, "dp", scatter_dimension=0, tiled=True),
        lax.psum_scatter(grad_fc2, "dp", scatter_dimension=0, tiled=True),
        lax.psum_scatter(grad_fc2b, "dp", scatter_dimension=0, tiled=True),
        lax.psum_scatter(grad_ada, "dp", scatter_dimension=1, tiled=True),
        lax.psum_scatter(grad_adab, "dp", scatter_dimension=0, tiled=True),
    )
    summed = lax.psum(
        (
            part_g1,
            part_qkv,
            part_out,
            part_g2,
            part_fc1,
            part_fc1b,
            part_fc2,
            part_fc2b,
            part_ada,
            part_adab,
        ),
        "ctx",
    )
    return (mixed, input_grad, cond_grad) + tuple(summed)


def local(*args, ndp, nctx):
    seqs, span, _ = args[0].shape
    if nctx == 2 and seqs == 1 and ndp == 16 and span == 512:
        return local_pair(*args, ndp=ndp)
    return local_any(*args)


def solution(mesh):
    in_specs = (
        P("dp", "ctx", None),
        P("dp", None),
        P("dp", "ctx"),
        P("dp", "ctx"),
        P("dp", "ctx", None),
        P(),
        P(),
        P(),
        P(),
        P(),
        P(),
        P(),
        P(),
        P(),
        P(),
    )
    out_specs = (
        P("dp", "ctx", None),
        P("dp", "ctx", None),
        P("dp", None),
        P("dp"),
        P("dp", None),
        P("dp", None),
        P("dp"),
        P("dp", None),
        P("dp"),
        P("dp", None),
        P("dp"),
        P(None, "dp"),
        P("dp"),
    )
    step = functools.partial(local, ndp=mesh.shape["dp"], nctx=mesh.shape["ctx"])
    return jax.shard_map(step, mesh=mesh, in_specs=in_specs, out_specs=out_specs, check_vma=False)
```
